256 devices in a mesh: feat: 4 (over y_lo, core), row: 4 (over x), col: 16 (over z, y_hi).
Axes of the slice: x: 4, y: 4 (y_hi: 2, y_lo: 2; y = y_hi * 2 + y_lo), z: 8, core: 2. Of those that a mesh axis runs over, the one named last changes fastest.
Arguments:
- features: bfloat16 [24576, 768], P('col', 'feat'), may hold values from -6 to 6
- weight: bfloat16 [768, 256], P('feat'), may hold values from -0.21875 to 0.21875
- tile_values: bfloat16 [4, 16, 64, 128, 128], P('row', 'col'), as said below
- tile_rows: int32 [4, 16, 64], P('row', 'col'), may hold values from 0 to 47, as said below
- tile_cols: int32 [4, 16, 64], P('row', 'col'), may hold values from 0 to 11
- tile_count: int32 [4, 16], P('row', 'col'), may hold values from 1 to 64, as said below
- cotangent: bfloat16 [24576, 256], P(('row', 'col')), may hold values from -6 to 6
Outputs:
- activated: bfloat16 [24576, 256], P(('row', 'col'))
- feature_grad: bfloat16 [16, 1536, 768], P('col', 'row', 'feat')
- weight_grad: float32 [768, 256], P('feat')
The draws below stay inside these ranges and needn't reach their ends.
Inputs may be any that keep to these rules, and one draw needn't show every extreme that they name: Within one block (r, c) the pairs (tile_rows, tile_cols) of all slots are distinct. `tile_count`: some block has all 64 slots live. `tile_values`: entries are nonnegative.
All inputs are finite; a program needn't handle non-finite values.
Results may differ from the reference program's by a relative error of at most 0.025.
Values may be sent and summed in bfloat16 or wider, within the bound.
A program may use at most 128 MiB of HBM per device.

```python
import math
import jax
import jax.numpy as jnp
from jax import lax

F_IN = 768
OUT = 256
TILE = 128
NODE_DEV = 384
NODES = 24576
ROW_TILES = 48
COL_TILES = 12
TILES_DEV = 64
FAN_ADJ = 1365
N_ROW = 4
N_COL = 16


def tile_slots(key):
    keys = jax.random.split(key, N_ROW * N_COL)
    slots = jax.vmap(lambda one: jax.random.permutation(one, ROW_TILES * COL_TILES)[:TILES_DEV])(keys)
    return slots.reshape(N_ROW, N_COL, TILES_DEV).astype(jnp.int32)


def draw_tile_rows(key, part):
    slots = tile_slots(key)
    return (slots // COL_TILES).astype(jnp.int32)


def draw_tile_cols(key, part):
    slots = tile_slots(key)
    return (slots % COL_TILES).astype(jnp.int32)


def draw_tile_count(key, part):
    key = jax.random.fold_in(key, 7)
    first, second = jax.random.split(key)
    lowest = max(1, TILES_DEV // 8)
    counts = jax.random.randint(first, (N_ROW * N_COL,), lowest, TILES_DEV + 1).astype(jnp.int32)
    busiest = jax.random.randint(second, (), 0, N_ROW * N_COL).astype(jnp.int32)
    counts = counts.at[busiest].set(TILES_DEV)
    return counts.reshape(N_ROW, N_COL).astype(jnp.int32)


def draw_tile_values(key, part):
    key = jax.random.fold_in(key, 11)
    first = jax.random.fold_in(key, 0)
    shape = (N_ROW, N_COL, TILES_DEV, TILE, TILE)
    factor = FAN_ADJ ** (-0.5)
    base = jnp.minimum(jnp.abs(jax.random.normal(first, shape, jnp.float32)), 3.0) * 1.25
    return (base * factor).astype(jnp.bfloat16)


def block_levels(rng, shape, pieces, smallest, largest):
    def one(dim, shards_of):
        steps = jax.random.uniform(jax.random.fold_in(jax.random.fold_in(rng, 6), dim), (shards_of,), jnp.float32, smallest / len(pieces), largest / len(pieces))
        return jnp.repeat(jnp.exp(steps), shape[dim] // shards_of).reshape((-1,) + (1,) * (len(shape) - dim - 1))

    factor_of = one(*pieces[0])
    for cut in pieces[1:]:
        factor_of = factor_of * one(*cut)
    return factor_of


def scatter_about(stream_key, extent, spread, bound, pieces=(), kind=jnp.bfloat16):
    drawn = spread * jax.random.normal(stream_key, extent, jnp.float32)
    if pieces:
        drawn = drawn * block_levels(stream_key, extent, pieces, -0.22, 0.18)
    return jnp.clip(drawn, -bound, bound).astype(kind)


def setup_inputs(seed: int = 0) -> dict:
    key_list = jax.random.split(jax.random.key(seed), 8)
    return {
        "features": scatter_about(key_list[0], (NODES, F_IN), 1.0, 6.0, ((0, 16), (1, 4))),
        "weight": scatter_about(key_list[1], (F_IN, OUT), F_IN ** -0.5, 0.21875, ((0, 4),)),
        "tile_values": draw_tile_values(jax.random.fold_in(key_list[7], 71), 0),
        "tile_rows": draw_tile_rows(jax.random.fold_in(key_list[7], 71), 0),
        "tile_cols": draw_tile_cols(jax.random.fold_in(key_list[7], 71), 0),
        "tile_count": draw_tile_count(jax.random.fold_in(key_list[7], 71), 0),
        "cotangent": scatter_about(key_list[6], (NODES, OUT), 1.0, 6.0, ((0, 64),)),
    }


def silu_slope(values):
    sigma = jax.nn.sigmoid(values)
    return sigma * (1.0 + values * (1.0 - sigma))

def live_mask(count):
    return (jnp.arange(TILES_DEV)[:, None, None] < count).astype(jnp.float32)

def reference(features, weight, tile_values, tile_rows, tile_cols, tile_count, cotangent):
    sources = features.reshape(N_COL, COL_TILES, TILE, F_IN)

    def forward_row(pack):
        vals, rows, cols, counts = pack

        def add_col(total, inner):
            tiles, rows_one, cols_one, count_one, blocks = inner
            tiles = tiles.astype(jnp.float32) * live_mask(count_one)
            picked = blocks[cols_one].astype(jnp.float32)
            product = jnp.einsum('tij,tjf->tif', tiles, picked)
            part = jax.ops.segment_sum(product, rows_one, num_segments=ROW_TILES)
            part = lax.optimization_barrier(part.astype(jnp.bfloat16)).astype(jnp.float32)
            return (total + part, None)
        start = jnp.zeros((ROW_TILES, TILE, F_IN), jnp.float32)
        total, _ = lax.scan(add_col, start, (vals, rows, cols, counts, sources))
        return total.astype(jnp.bfloat16)
    aggregated = lax.map(forward_row, (tile_values, tile_rows, tile_cols, tile_count)).reshape(NODES, F_IN)
    hidden = jnp.dot(aggregated, weight, preferred_element_type=jnp.float32)
    activated = jax.nn.silu(hidden).astype(jnp.bfloat16)
    hidden_grad = (cotangent.astype(jnp.float32) * silu_slope(hidden)).astype(jnp.bfloat16)
    projected = jnp.dot(hidden_grad, weight.T, preferred_element_type=jnp.float32).astype(jnp.bfloat16)
    targets = projected.reshape(N_ROW, ROW_TILES, TILE, F_IN)

    def backward_col(col_index):
        vals = jnp.take(tile_values, col_index, axis=1)
        rows = jnp.take(tile_rows, col_index, axis=1)
        cols = jnp.take(tile_cols, col_index, axis=1)
        counts = jnp.take(tile_count, col_index, axis=1)

        def add_row(total, inner):
            tiles, rows_one, cols_one, count_one, blocks = inner
            tiles = tiles.astype(jnp.float32) * live_mask(count_one)
            picked = blocks[rows_one].astype(jnp.float32)
            product = jnp.einsum('tji,tjf->tif', tiles, picked)
            part = jax.ops.segment_sum(product, cols_one, num_segments=COL_TILES)
            part = lax.optimization_barrier(part.astype(jnp.bfloat16)).astype(jnp.float32)
            return (total + part, None)
        start = jnp.zeros((COL_TILES, TILE, F_IN), jnp.float32)
        total, _ = lax.scan(add_row, start, (vals, rows, cols, counts, targets))
        return total.astype(jnp.bfloat16)
    feature_grad = lax.map(backward_col, jnp.arange(N_COL).astype(jnp.int32)).reshape(N_COL, NODE_DEV * N_ROW, F_IN)
    weight_grad = jnp.dot(aggregated.T, hidden_grad, preferred_element_type=jnp.float32) * (1.0 / math.sqrt(NODES))
    return (activated, feature_grad, weight_grad)
```

```python
import functools
import math

import jax
import jax.numpy as jnp
from jax import lax
from jax.experimental import pallas as pl
from jax.experimental.pallas import tpu as pltpu
from jax.sharding import PartitionSpec as P

MESH = pl.DeviceIdType.MESH
F32 = jnp.float32
BF16 = jnp.bfloat16


def far_first(n):
    return sorted(range(1, n), key=lambda k: (-min(k, n - k), k))


def kernel(
    n_row, n_z, slots, total_nodes,
    rows_s, cols_s, prev_r, last_r, prev_c, last_c,
    feat_hbm, w_ref, tiles_hbm, cot_hbm,
    act_out, fg_out, wg_out,
    x_v, tiles_v, cot_v,
    y_send, y_recv, y_buf, prod_f,
    s_buf, yh_recv, t_buf, z_recv, hg_buf, act_v,
    prod_b, b_send, b_recv, b_full,
    u_f32, u_send, u_recv, v_buf, wg_piece,
    in_sem, p1_s, p1_r, p2_s, p2_r, p3a_s, p3a_r, p3b_s, p3b_r,
    act_s, act_r, p4z_s, p4z_r, p4y_s, p4y_r, p5_s, p5_r, p6_s, p6_r,
    k1_s, k1_r, k2_s, k2_r, k3_s, k3_r,
):
    f = lax.axis_index("feat")
    r = lax.axis_index("row")
    c = lax.axis_index("col")
    y_low, b = f // 2, f % 2
    z, h = c // 2, c % 2
    a = (y_low + h) % 2
    n_g = 2 * n_row

    def feat_of(role, core):
        return ((role + h) % 2) * 2 + core

    def remote(src, dst, send, recv, device):
        return pltpu.make_async_remote_copy(
            src_ref=src, dst_ref=dst, send_sem=send, recv_sem=recv, device_id=device, device_id_type=MESH
        )

    feat_peers = [{"feat": (f + k) % 4} for k in range(1, 4)]

    def g_peer(k):
        g2 = (2 * r + a + k) % n_g
        return g2, {"feat": feat_of(g2 % 2, b), "row": g2 // 2}

    def u_peer(k):
        u2 = (2 * r + h + k) % n_g
        return u2, {"row": u2 // 2, "col": 2 * z + u2 % 2}

    def z_peer(k):
        return {"col": 2 * ((z + k) % n_z) + h}

    y_partner = {"feat": (f + 2) % 4, "col": c + 1 - 2 * h}

    node_dev = x_v.shape[0]
    in_x = pltpu.make_async_copy(
        feat_hbm.at[pl.ds(pl.multiple_of(r * node_dev, node_dev), node_dev)], x_v, in_sem.at[0])
    in_t = pltpu.make_async_copy(tiles_hbm.at[:, a], tiles_v, in_sem.at[1])
    in_c = pltpu.make_async_copy(
        cot_hbm.at[:, a, :, pl.ds(pl.multiple_of(b * 128, 128), 128)], cot_v, in_sem.at[2])
    in_x.start()
    in_t.start()
    in_c.start()

    barrier = pltpu.get_barrier_semaphore()
    peers = list(feat_peers)
    for k in range(1, n_row):
        peers.append({"row": (r + k) % n_row})
        peers.append({"feat": (f + 2) % 4, "row": (r + k) % n_row})
    peers += [z_peer(k) for k in range(1, n_z)]
    peers.append(y_partner)
    peers += [{"row": (r + k) % n_row, "col": c + 1 - 2 * h} for k in range(n_row)]
    for peer in peers:
        pl.semaphore_signal(barrier, inc=1, device_id=peer, device_id_type=MESH)

    in_x.wait()
    y_part = jnp.dot(x_v[...], w_ref[...], preferred_element_type=F32).astype(BF16)
    for q in range(2):
        for core in range(2):
            y_send[2 * q + core] = y_part[192 * q:192 * (q + 1), 128 * core:128 * (core + 1)].reshape(3, 64, 128)
    pl.semaphore_wait(barrier, len(peers))

    copies = []
    for k in range(1, 4):
        f2 = (f + k) % 4
        piece = ((f2 // 2 + h) % 2) * 2 + f2 % 2
        cp = remote(y_send.at[piece], y_recv.at[k - 1], p1_s.at[k - 1], p1_r.at[k - 1], feat_peers[k - 1])
        cp.start()
        copies.append(cp)
    total = y_send[2 * a + b].astype(F32)
    for k in range(3):
        copies[k].wait_recv()
        total = total + y_recv[k].astype(F32)
    g = 2 * r + a
    y_buf[pl.ds(3 * g, 3)] = total.astype(BF16)

    p2 = []
    for k in range(1, n_g):
        _, dev = g_peer(k)
        cp = remote(y_buf.at[pl.ds(3 * g, 3)], y_buf.at[pl.ds(3 * g, 3)], p2_s.at[k - 1], p2_r.at[k - 1], dev)
        cp.start()
        p2.append(cp)
    prod_f[slots] = jnp.zeros((64, 128), F32)
    prod_b[slots] = jnp.zeros((128, 128), F32)
    in_t.wait()
    for k in range(1, n_g):
        src = (g + n_g - k) % n_g
        remote(y_buf.at[pl.ds(3 * src, 3)], y_buf.at[pl.ds(3 * src, 3)], p2_s.at[k - 1], p2_r.at[k - 1],
               y_partner).wait_recv()

    def forward(s, _):
        block = y_buf[pl.ds(2 * cols_s[s], 2)].reshape(128, 128)
        prod_f[s] = jnp.dot(tiles_v[s], block, preferred_element_type=F32)
        return 0

    lax.fori_loop(0, slots, forward, 0, unroll=8)

    def chain_forward(s, _):
        prod_f[s] = prod_f[s] + prod_f[prev_r[s]]
        return 0

    lax.fori_loop(0, slots, chain_forward, 0, unroll=4)

    def fill(c2):
        for w in range(3):
            s_buf[c2, w] = prod_f[last_r[3 * c2 + w]].astype(BF16)

    offs = far_first(n_z) + [0]
    p3a = []
    for j, off in enumerate(offs):
        c2 = 2 * ((z + off) % n_z) + 1 - h
        fill(c2)
        cp = remote(s_buf.at[c2], yh_recv.at[j], p3a_s.at[j], p3a_r.at[j], y_partner)
        cp.start()
        p3a.append(cp)
    for j, off in enumerate(offs):
        fill(2 * ((z + off) % n_z) + h)
    p3b = []
    for j, off in enumerate(offs):
        c2 = 2 * ((z + off) % n_z) + h
        p3a[j].wait_recv()
        both = s_buf[c2].astype(F32) + yh_recv[j].astype(F32)
        if off:
            t_buf[j] = both.astype(BF16)
            cp = remote(t_buf.at[j], z_recv.at[j], p3b_s.at[j], p3b_r.at[j], z_peer(off))
            cp.start()
            p3b.append(cp)
        else:
            hidden = both
    for j in range(n_z - 1):
        p3b[j].wait_recv()
        hidden = hidden + z_recv[j].astype(F32)

    in_c.wait()
    sigma = jax.nn.sigmoid(hidden)
    grad = cot_v[...].astype(F32) * (sigma * (1.0 + hidden * (1.0 - sigma)))
    hg_buf[pl.ds(3 * c, 3)] = grad.astype(BF16)
    act_v[...] = (hidden * sigma).astype(BF16)

    own = hg_buf.at[pl.ds(3 * c, 3)]
    p4y = [remote(own, own, p4y_s.at[n_z - 1], p4y_r.at[n_z - 1], y_partner)]
    p4y[0].start()
    p4z = []
    for j, off in enumerate(offs[:-1]):
        cp = remote(own, own, p4z_s.at[j], p4z_r.at[j], z_peer(off))
        cp.start()
        p4z.append(cp)
    act_cols = pl.ds(pl.multiple_of(b * 128, 128), 128)
    act_dst = act_out.at[:, a, :, act_cols]
    local = pltpu.make_async_copy(act_v, act_dst, in_sem.at[3])
    local.start()
    acts = []
    for k in range(1, 4):
        cp = remote(act_v, act_dst, act_s.at[k - 1], act_r.at[k - 1], feat_peers[k - 1])
        cp.start()
        acts.append(cp)
    for j in reversed(range(n_z - 1)):
        c2 = 2 * ((z + n_z - offs[j]) % n_z) + h
        got = hg_buf.at[pl.ds(3 * c2, 3)]
        remote(got, got, p4z_s.at[j], p4z_r.at[j], y_partner).wait_recv()
        cp = remote(got, got, p4y_s.at[j], p4y_r.at[j], y_partner)
        cp.start()
        p4y.append(cp)
    for j in range(n_z):
        off = offs[j]
        c2 = 2 * ((z + n_z - off) % n_z) + 1 - h
        got = hg_buf.at[pl.ds(3 * c2, 3)]
        remote(got, got, p4y_s.at[j], p4y_r.at[j], y_partner).wait_recv()

    def backward(s, _):
        prod_b[s] = lax.dot_general(
            tiles_v[s], hg_buf[rows_s[s]], (((0,), (0,)), ((), ())), preferred_element_type=F32)
        return 0

    lax.fori_loop(0, slots, backward, 0, unroll=8)

    def chain_backward(s, _):
        prod_b[s] = prod_b[s] + prod_b[prev_c[s]]
        return 0

    lax.fori_loop(0, slots, chain_backward, 0, unroll=4)

    for j in range(3 * n_row):
        b_send[pl.ds(2 * j, 2)] = prod_b[last_c[j]].astype(BF16).reshape(2, 64, 128)

    p5 = []
    for k in range(1, n_g):
        g2, dev = g_peer(k)
        cp = remote(b_send.at[pl.ds(3 * g2, 3)], b_recv.at[k - 1], p5_s.at[k - 1], p5_r.at[k - 1], dev)
        cp.start()
        p5.append(cp)
    total = b_send[pl.ds(3 * g, 3)].astype(F32)
    for k in range(n_g - 1):
        p5[k].wait_recv()
        total = total + b_recv[k].astype(F32)
    b_full[2 * a + b] = total.astype(BF16)

    mine = b_full.at[2 * a + b]
    p6 = []
    for k in range(1, 4):
        cp = remote(mine, mine, p6_s.at[k - 1], p6_r.at[k - 1], feat_peers[k - 1])
        cp.start()
        p6.append(cp)
    for k in range(1, 4):
        f2 = (f + 4 - k) % 4
        got = b_full.at[((f2 // 2 + h) % 2) * 2 + f2 % 2]
        remote(got, got, p6_s.at[k - 1], p6_r.at[k - 1], y_partner).wait_recv()

    piece_rows = u_f32.shape[1]
    for core in range(2):
        part = jnp.zeros((192, 128), F32)
        for q in range(2):
            part = part + lax.dot_general(
                x_v[192 * q:192 * (q + 1)], b_full[2 * q + core].reshape(192, 128),
                (((0,), (0,)), ((), ())), preferred_element_type=F32)
        part = part.reshape(n_row, piece_rows, 128)
        u_f32[n_row * core:n_row * (core + 1)] = part
        u_send[n_row * core:n_row * (core + 1)] = part.astype(BF16)
    u = 2 * r + h
    k1 = []
    for k in range(1, n_g):
        u2, dev = u_peer(k)
        cp = remote(u_send.at[u2], u_recv.at[k - 1], k1_s.at[k - 1], k1_r.at[k - 1], dev)
        cp.start()
        k1.append(cp)
    for q in range(2):
        grad_rows = jnp.zeros((192, w_ref.shape[0]), F32)
        for core in range(2):
            grad_rows = grad_rows + lax.dot_general(
                b_full[2 * q + core].reshape(192, 128), w_ref[:, 128 * core:128 * (core + 1)],
                (((1,), (1,)), ((), ())), preferred_element_type=F32)
        fg_out[192 * q:192 * (q + 1)] = grad_rows.astype(BF16)
    total = u_f32[u]
    for k in range(n_g - 1):
        k1[k].wait_recv()
        total = total + u_recv[k].astype(F32)
    v_buf[z] = total.astype(BF16)
    k2 = []
    for j, off in enumerate(offs[:-1]):
        cp = remote(v_buf.at[z], v_buf.at[z], k2_s.at[j], k2_r.at[j], z_peer(off))
        cp.start()
        k2.append(cp)
    for j, off in enumerate(offs[:-1]):
        got = v_buf.at[(z + n_z - off) % n_z]
        remote(got, got, k2_s.at[j], k2_r.at[j], y_partner).wait_recv()
    total = v_buf[0].astype(F32)
    for j in range(1, n_z):
        total = total + v_buf[j].astype(F32)
    wg_piece[...] = total * (1.0 / math.sqrt(total_nodes))

    def wg_place(piece):
        return wg_out.at[
            pl.ds(pl.multiple_of((piece % n_row) * piece_rows, piece_rows), piece_rows),
            pl.ds(pl.multiple_of((piece // n_row) * 128, 128), 128),
        ]

    local_wg = pltpu.make_async_copy(wg_piece, wg_place(u), in_sem.at[4])
    local_wg.start()
    k3 = []
    for k in range(1, n_g):
        _, dev = u_peer(k)
        cp = remote(wg_piece, wg_place(u), k3_s.at[k - 1], k3_r.at[k - 1], dev)
        cp.start()
        k3.append(cp)
    for k in range(1, n_g):
        got = wg_place((u + n_g - k) % n_g)
        remote(wg_piece, got, k3_s.at[k - 1], k3_r.at[k - 1], y_partner).wait_recv()
    for k in range(1, 4):
        f2 = (f + 4 - k) % 4
        got = act_out.at[:, (f2 // 2 + h) % 2, :, pl.ds(pl.multiple_of((f2 % 2) * 128, 128), 128)]
        remote(act_v, got, act_s.at[k - 1], act_r.at[k - 1], y_partner).wait_recv()
    local.wait()
    local_wg.wait()
    for cp in copies + p2 + p3a + p3b + p4y + p4z + acts + p5 + p6 + k1 + k2 + k3:
        cp.wait_send()


def slot_links(keys, count, places):
    slots = keys.shape[0]
    ids = jnp.arange(slots, dtype=jnp.int32)
    live = ids < count
    same = (keys[:, None] == keys[None, :]) & live[None, :] & (ids[None, :] < ids[:, None])
    prev = jnp.max(jnp.where(same, ids[None, :], -1), axis=1)
    there = (jnp.arange(places, dtype=jnp.int32)[:, None] == keys[None, :]) & live[None, :]
    last = jnp.max(jnp.where(there, ids[None, :], -1), axis=1)
    return jnp.where(prev < 0, slots, prev), jnp.where(last < 0, slots, last)


def shards(n_row, n_z, features, weight, tile_values, tile_rows, tile_cols, tile_count, cotangent):
    slots = tile_values.shape[2]
    node_dev, out = cotangent.shape
    width = features.shape[1]
    n_g = 2 * n_row
    n_col = 2 * n_z
    rows = tile_rows[0, 0]
    cols = tile_cols[0, 0]
    count = tile_count[0, 0]
    prev_r, last_r = slot_links(rows, count, 3 * n_col)
    prev_c, last_c = slot_links(cols, count, 3 * n_row)
    piece_rows = 2 * width // n_g
    dma = pltpu.SemaphoreType.DMA
    smem = pl.BlockSpec(memory_space=pltpu.SMEM)
    vmem = pl.BlockSpec(memory_space=pltpu.VMEM)
    hbm = pl.BlockSpec(memory_space=pl.ANY)
    sem_counts = [5, 3, 3, n_g - 1, n_g - 1, n_z, n_z, n_z - 1, n_z - 1, 3, 3, n_z - 1, n_z - 1, n_z, n_z,
                  n_g - 1, n_g - 1, 3, 3, n_g - 1, n_g - 1, n_z - 1, n_z - 1, n_g - 1, n_g - 1]
    act, fg, wg = pl.pallas_call(
        functools.partial(kernel, n_row, n_z, slots, node_dev * n_row * n_col),
        out_shape=[
            jax.ShapeDtypeStruct((3, 2, 64, out), BF16),
            jax.ShapeDtypeStruct((node_dev, width), BF16),
            jax.ShapeDtypeStruct((width, out), F32),
        ],
        in_specs=[smem] * 6 + [hbm, vmem, hbm, hbm],
        out_specs=[vmem] * 3,
        scratch_shapes=[
            pltpu.VMEM((node_dev, width), BF16),
            pltpu.VMEM((slots, 64, 128), BF16),
            pltpu.VMEM((3, 64, 128), BF16),
            pltpu.VMEM((4, 3, 64, 128), BF16),
            pltpu.VMEM((3, 3, 64, 128), BF16),
            pltpu.VMEM((3 * n_g, 64, 128), BF16),
            pltpu.VMEM((slots + 1, 64, 128), F32),
            pltpu.VMEM((n_col, 3, 64, 128), BF16),
            pltpu.VMEM((n_z, 3, 64, 128), BF16),
            pltpu.VMEM((n_z - 1, 3, 64, 128), BF16),
            pltpu.VMEM((n_z - 1, 3, 64, 128), BF16),
            pltpu.VMEM((3 * n_col, 64, 128), BF16),
            pltpu.VMEM((3, 64, 128), BF16),
            pltpu.VMEM((slots + 1, 128, 128), F32),
            pltpu.VMEM((3 * n_g, 64, 128), BF16),
            pltpu.VMEM((n_g - 1, 3, 64, 128), BF16),
            pltpu.VMEM((4, 3, 64, 128), BF16),
            pltpu.VMEM((n_g, piece_rows, 128), F32),
            pltpu.VMEM((n_g, piece_rows, 128), BF16),
            pltpu.VMEM((n_g - 1, piece_rows, 128), BF16),
            pltpu.VMEM((n_z, piece_rows, 128), BF16),
            pltpu.VMEM((piece_rows, 128), F32),
        ] + [dma((n,)) for n in sem_counts],
        compiler_params=pltpu.CompilerParams(
            collective_id=0, has_side_effects=True, vmem_limit_bytes=40 * 1024 * 1024),
    )(
        rows, cols, prev_r, last_r, prev_c, last_c,
        features, weight, tile_values.reshape(slots, 2, 64, 128), cotangent.reshape(3, 2, 64, out),
    )
    return act.reshape(node_dev, out), fg.reshape(1, node_dev, width), wg


def solution(mesh):
    return jax.shard_map(
        functools.partial(shards, mesh.shape["row"], mesh.shape["col"] // 2),
        mesh=mesh,
        in_specs=(
            P("col", "feat"),
            P("feat", None),
            P("row", "col", None, None, None),
            P("row", "col", None),
            P("row", "col", None),
            P("row", "col"),
            P(("row", "col"), None),
        ),
        out_specs=(P(("row", "col"), None), P("col", "row", "feat"), P("feat", None)),
        check_vma=False,
    )
```

```python
import functools
import math

import jax
import jax.numpy as jnp
from jax import lax
from jax.experimental import pallas as pl
from jax.experimental.pallas import tpu as pltpu
from jax.sharding import PartitionSpec as P

MESH = pl.DeviceIdType.MESH
F32 = jnp.float32
BF16 = jnp.bfloat16


def far_first(n):
    return sorted(range(1, n), key=lambda k: (-min(k, n - k), k))


def kernel(
    n_row, n_z, slots, total_nodes,
    rows_hbm, cols_hbm, count_s, feat_hbm, w_hbm, tiles_hbm, cot_hbm,
    act_out, fg_out, wg_out,
    rows_s, cols_s, keys_v, links_v, links_s,
    x_v, w_ref, tiles_v, cot_v,
    y_send, y_recv, y_buf, prod_f,
    s_buf, yh_recv, t_buf, z_recv, hg_buf, act_v,
    prod_b, b_send, b_recv, b_full,
    u_f32, u_send, u_recv, v_buf, wg_piece,
    in_sem, p1_s, p1_r, p2_s, p2_r, p3a_s, p3a_r, p3b_s, p3b_r,
    act_s, act_r, p4z_s, p4z_r, p4y_s, p4y_r, p5_s, p5_r, p6_s, p6_r,
    k1_s, k1_r, k2_s, k2_r, k3_s, k3_r,
):
    f = lax.axis_index("feat")
    r = lax.axis_index("row")
    c = lax.axis_index("col")
    y_low, b = f // 2, f % 2
    z, h = c // 2, c % 2
    a = (y_low + h) % 2
    n_g = 2 * n_row

    def feat_of(role, core):
        return ((role + h) % 2) * 2 + core

    def remote(src, dst, send, recv, device):
        return pltpu.make_async_remote_copy(
            src_ref=src, dst_ref=dst, send_sem=send, recv_sem=recv, device_id=device, device_id_type=MESH
        )

    feat_peers = [{"feat": (f + k) % 4} for k in range(1, 4)]

    def g_peer(k):
        g2 = (2 * r + a + k) % n_g
        return g2, {"feat": feat_of(g2 % 2, b), "row": g2 // 2}

    def u_peer(k):
        u2 = (2 * r + h + k) % n_g
        return u2, {"row": u2 // 2, "col": 2 * z + u2 % 2}

    def z_peer(k):
        return {"col": 2 * ((z + k) % n_z) + h}

    y_partner = {"feat": (f + 2) % 4, "col": c + 1 - 2 * h}

    node_dev = x_v.shape[1]
    in_x = pltpu.make_async_copy(
        feat_hbm.at[:, pl.ds(pl.multiple_of(r * node_dev, node_dev), node_dev)], x_v, in_sem.at[0])
    in_w = pltpu.make_async_copy(w_hbm, w_ref, in_sem.at[5])
    in_keys = [
        pltpu.make_async_copy(rows_hbm, keys_v.at[0], in_sem.at[6]),
        pltpu.make_async_copy(cols_hbm, keys_v.at[1], in_sem.at[7]),
        pltpu.make_async_copy(rows_hbm, rows_s, in_sem.at[8]),
        pltpu.make_async_copy(cols_hbm, cols_s, in_sem.at[9]),
    ]
    in_t = pltpu.make_async_copy(tiles_hbm.at[:, a], tiles_v, in_sem.at[1])
    in_c = pltpu.make_async_copy(
        cot_hbm.at[:, a, :, pl.ds(pl.multiple_of(b * 128, 128), 128)], cot_v, in_sem.at[2])
    in_x.start()
    in_w.start()
    for cp in in_keys:
        cp.start()
    in_t.start()
    in_c.start()

    barrier = pltpu.get_barrier_semaphore()
    peers = list(feat_peers)
    for k in range(1, n_row):
        peers.append({"row": (r + k) % n_row})
        peers.append({"feat": (f + 2) % 4, "row": (r + k) % n_row})
    peers += [z_peer(k) for k in range(1, n_z)]
    peers.append(y_partner)
    peers += [{"row": (r + k) % n_row, "col": c + 1 - 2 * h} for k in range(n_row)]
    for peer in peers:
        pl.semaphore_signal(barrier, inc=1, device_id=peer, device_id_type=MESH)

    in_x.wait()
    in_w.wait()
    y_part = lax.dot_general(
        x_v[...], w_ref[...], (((0,), (0,)), ((), ())), preferred_element_type=F32).astype(BF16)
    for q in range(2):
        for core in range(2):
            y_send[2 * q + core] = y_part[192 * q:192 * (q + 1), 128 * core:128 * (core + 1)].reshape(3, 64, 128)
    pl.semaphore_wait(barrier, len(peers))

    copies = []
    for k in range(1, 4):
        f2 = (f + k) % 4
        piece = ((f2 // 2 + h) % 2) * 2 + f2 % 2
        cp = remote(y_send.at[piece], y_recv.at[k - 1], p1_s.at[k - 1], p1_r.at[k - 1], feat_peers[k - 1])
        cp.start()
        copies.append(cp)
    for cp in in_keys:
        cp.wait()
    ids = lax.broadcasted_iota(jnp.int32, (slots, 128), 0)
    lanes = lax.broadcasted_iota(jnp.int32, (slots, 128), 1)
    live = ids < count_s[0, 0]
    for i in range(2):
        across = jnp.broadcast_to(keys_v[i], (slots, slots))
        across = jnp.concatenate([across, jnp.zeros((slots, 128 - slots), jnp.int32)], axis=1)
        down = jnp.sum(jnp.where(ids == lanes, across, 0), axis=1, keepdims=True)
        down = jnp.broadcast_to(down, (slots, 128))
        before = jnp.where(live & (ids < lanes) & (down == across), ids, -1)
        there = jnp.where(live & (down == lanes), ids, -1)
        for w, found in ((0, before), (1, there)):
            top = jnp.max(found, axis=0, keepdims=True)
            links_v[pl.ds(2 * i + w, 1), :] = jnp.where(top < 0, slots, top)
    links = pltpu.make_async_copy(links_v, links_s, in_sem.at[10])
    links.start()
    total = y_send[2 * a + b].astype(F32)
    for k in range(3):
        copies[k].wait_recv()
        total = total + y_recv[k].astype(F32)
    g = 2 * r + a
    y_buf[pl.ds(3 * g, 3)] = total.astype(BF16)

    p2 = []
    for k in range(1, n_g):
        _, dev = g_peer(k)
        cp = remote(y_buf.at[pl.ds(3 * g, 3)], y_buf.at[pl.ds(3 * g, 3)], p2_s.at[k - 1], p2_r.at[k - 1], dev)
        cp.start()
        p2.append(cp)
    prod_f[slots] = jnp.zeros((64, 128), F32)
    prod_b[slots] = jnp.zeros((128, 128), F32)
    in_t.wait()
    links.wait()
    for k in range(1, n_g):
        src = (g + n_g - k) % n_g
        remote(y_buf.at[pl.ds(3 * src, 3)], y_buf.at[pl.ds(3 * src, 3)], p2_s.at[k - 1], p2_r.at[k - 1],
               y_partner).wait_recv()

    def forward(s, _):
        block = y_buf[pl.ds(2 * cols_s[0, s], 2)].reshape(128, 128)
        prod_f[s] = jnp.dot(tiles_v[s], block, preferred_element_type=F32)
        return 0

    lax.fori_loop(0, slots, forward, 0, unroll=8)

    def chain_forward(s, _):
        prod_f[s] = prod_f[s] + prod_f[links_s[0, s]]
        return 0

    lax.fori_loop(0, slots, chain_forward, 0, unroll=4)

    def fill(c2):
        for w in range(3):
            s_buf[c2, w] = prod_f[links_s[1, 3 * c2 + w]].astype(BF16)

    offs = far_first(n_z) + [0]
    p3a = []
    for j, off in enumerate(offs):
        c2 = 2 * ((z + off) % n_z) + 1 - h
        fill(c2)
        cp = remote(s_buf.at[c2], yh_recv.at[j], p3a_s.at[j], p3a_r.at[j], y_partner)
        cp.start()
        p3a.append(cp)
    for j, off in enumerate(offs):
        fill(2 * ((z + off) % n_z) + h)
    p3b = []
    for j, off in enumerate(offs):
        c2 = 2 * ((z + off) % n_z) + h
        p3a[j].wait_recv()
        both = s_buf[c2].astype(F32) + yh_recv[j].astype(F32)
        if off:
            t_buf[j] = both.astype(BF16)
            cp = remote(t_buf.at[j], z_recv.at[j], p3b_s.at[j], p3b_r.at[j], z_peer(off))
            cp.start()
            p3b.append(cp)
        else:
            hidden = both
    for j in range(n_z - 1):
        p3b[j].wait_recv()
        hidden = hidden + z_recv[j].astype(F32)

    in_c.wait()
    sigma = jax.nn.sigmoid(hidden)
    grad = cot_v[...].astype(F32) * (sigma * (1.0 + hidden * (1.0 - sigma)))
    hg_buf[pl.ds(3 * c, 3)] = grad.astype(BF16)
    act_v[...] = (hidden * sigma).astype(BF16)

    own = hg_buf.at[pl.ds(3 * c, 3)]
    p4y = [remote(own, own, p4y_s.at[n_z - 1], p4y_r.at[n_z - 1], y_partner)]
    p4y[0].start()
    p4z = []
    for j, off in enumerate(offs[:-1]):
        cp = remote(own, own, p4z_s.at[j], p4z_r.at[j], z_peer(off))
        cp.start()
        p4z.append(cp)
    act_cols = pl.ds(pl.multiple_of(b * 128, 128), 128)
    act_dst = act_out.at[:, a, :, act_cols]
    local = pltpu.make_async_copy(act_v, act_dst, in_sem.at[3])
    local.start()
    acts = []
    for k in range(1, 4):
        cp = remote(act_v, act_dst, act_s.at[k - 1], act_r.at[k - 1], feat_peers[k - 1])
        cp.start()
        acts.append(cp)
    for j in reversed(range(n_z - 1)):
        c2 = 2 * ((z + n_z - offs[j]) % n_z) + h
        got = hg_buf.at[pl.ds(3 * c2, 3)]
        remote(got, got, p4z_s.at[j], p4z_r.at[j], y_partner).wait_recv()
        cp = remote(got, got, p4y_s.at[j], p4y_r.at[j], y_partner)
        cp.start()
        p4y.append(cp)
    for j in range(n_z):
        off = offs[j]
        c2 = 2 * ((z + n_z - off) % n_z) + 1 - h
        got = hg_buf.at[pl.ds(3 * c2, 3)]
        remote(got, got, p4y_s.at[j], p4y_r.at[j], y_partner).wait_recv()

    def backward(s, _):
        prod_b[s] = lax.dot_general(
            tiles_v[s], hg_buf[rows_s[0, s]], (((0,), (0,)), ((), ())), preferred_element_type=F32)
        return 0

    lax.fori_loop(0, slots, backward, 0, unroll=8)

    def chain_backward(s, _):
        prod_b[s] = prod_b[s] + prod_b[links_s[2, s]]
        return 0

    lax.fori_loop(0, slots, chain_backward, 0, unroll=4)

    for j in range(3 * n_row):
        b_send[pl.ds(2 * j, 2)] = prod_b[links_s[3, j]].astype(BF16).reshape(2, 64, 128)

    p5 = []
    for k in range(1, n_g):
        g2, dev = g_peer(k)
        cp = remote(b_send.at[pl.ds(3 * g2, 3)], b_recv.at[k - 1], p5_s.at[k - 1], p5_r.at[k - 1], dev)
        cp.start()
        p5.append(cp)
    total = b_send[pl.ds(3 * g, 3)].astype(F32)
    for k in range(n_g - 1):
        p5[k].wait_recv()
        total = total + b_recv[k].astype(F32)
    b_full[2 * b + a] = total.astype(BF16)

    mine = b_full.at[2 * b + a]
    p6 = []
    for k in range(1, 4):
        cp = remote(mine, mine, p6_s.at[k - 1], p6_r.at[k - 1], feat_peers[k - 1])
        cp.start()
        p6.append(cp)
    for k in range(1, 4):
        f2 = (f + 4 - k) % 4
        got = b_full.at[2 * (f2 % 2) + (f2 // 2 + h) % 2]
        remote(got, got, p6_s.at[k - 1], p6_r.at[k - 1], y_partner).wait_recv()

    piece_rows = u_f32.shape[1]
    for core in range(2):
        half = b_full[2 * core:2 * core + 2].reshape(node_dev, 128)
        part = jnp.dot(x_v[...], half, preferred_element_type=F32)
        part = part.reshape(n_row, piece_rows, 128)
        u_f32[n_row * core:n_row * (core + 1)] = part
        u_send[n_row * core:n_row * (core + 1)] = part.astype(BF16)
    u = 2 * r + h
    k1 = []
    for k in range(1, n_g):
        u2, dev = u_peer(k)
        cp = remote(u_send.at[u2], u_recv.at[k - 1], k1_s.at[k - 1], k1_r.at[k - 1], dev)
        cp.start()
        k1.append(cp)
    grad_t = jnp.zeros((w_ref.shape[0], node_dev), F32)
    for core in range(2):
        grad_t = grad_t + lax.dot_general(
            w_ref[:, 128 * core:128 * (core + 1)], b_full[2 * core:2 * core + 2].reshape(node_dev, 128),
            (((1,), (1,)), ((), ())), preferred_element_type=F32)
    fg_out[...] = grad_t.astype(BF16)
    total = u_f32[u]
    for k in range(n_g - 1):
        k1[k].wait_recv()
        total = total + u_recv[k].astype(F32)
    v_buf[z] = total.astype(BF16)
    k2 = []
    for j, off in enumerate(offs[:-1]):
        cp = remote(v_buf.at[z], v_buf.at[z], k2_s.at[j], k2_r.at[j], z_peer(off))
        cp.start()
        k2.append(cp)
    for j, off in enumerate(offs[:-1]):
        got = v_buf.at[(z + n_z - off) % n_z]
        remote(got, got, k2_s.at[j], k2_r.at[j], y_partner).wait_recv()
    total = v_buf[0].astype(F32)
    for j in range(1, n_z):
        total = total + v_buf[j].astype(F32)
    wg_piece[...] = total * (1.0 / math.sqrt(total_nodes))

    def wg_place(piece):
        return wg_out.at[
            pl.ds(pl.multiple_of((piece % n_row) * piece_rows, piece_rows), piece_rows),
            pl.ds(pl.multiple_of((piece // n_row) * 128, 128), 128),
        ]

    local_wg = pltpu.make_async_copy(wg_piece, wg_place(u), in_sem.at[4])
    local_wg.start()
    k3 = []
    for k in range(1, n_g):
        _, dev = u_peer(k)
        cp = remote(wg_piece, wg_place(u), k3_s.at[k - 1], k3_r.at[k - 1], dev)
        cp.start()
        k3.append(cp)
    for k in range(1, n_g):
        got = wg_place((u + n_g - k) % n_g)
        remote(wg_piece, got, k3_s.at[k - 1], k3_r.at[k - 1], y_partner).wait_recv()
    for k in range(1, 4):
        f2 = (f + 4 - k) % 4
        got = act_out.at[:, (f2 // 2 + h) % 2, :, pl.ds(pl.multiple_of((f2 % 2) * 128, 128), 128)]
        remote(act_v, got, act_s.at[k - 1], act_r.at[k - 1], y_partner).wait_recv()
    local.wait()
    local_wg.wait()
    for cp in copies + p2 + p3a + p3b + p4y + p4z + acts + p5 + p6 + k1 + k2 + k3:
        cp.wait_send()


def shards(n_row, n_z, features, weight, tile_values, tile_rows, tile_cols, tile_count, cotangent):
    slots = tile_values.shape[2]
    node_dev, out = cotangent.shape
    width = features.shape[1]
    n_g = 2 * n_row
    n_col = 2 * n_z
    piece_rows = 2 * width // n_g
    dma = pltpu.SemaphoreType.DMA
    smem = pl.BlockSpec(memory_space=pltpu.SMEM)
    vmem = pl.BlockSpec(memory_space=pltpu.VMEM)
    hbm = pl.BlockSpec(memory_space=pltpu.HBM)
    sem_counts = [11, 3, 3, n_g - 1, n_g - 1, n_z, n_z, n_z - 1, n_z - 1, 3, 3, n_z - 1, n_z - 1, n_z, n_z,
                  n_g - 1, n_g - 1, 3, 3, n_g - 1, n_g - 1, n_z - 1, n_z - 1, n_g - 1, n_g - 1]
    act, fg, wg = pl.pallas_call(
        functools.partial(kernel, n_row, n_z, slots, node_dev * n_row * n_col),
        out_shape=[
            jax.ShapeDtypeStruct((3, 2, 64, out), BF16),
            jax.ShapeDtypeStruct((width, node_dev), BF16),
            jax.ShapeDtypeStruct((width, out), F32),
        ],
        in_specs=[hbm, hbm, smem, hbm, hbm, hbm, hbm],
        out_specs=[vmem] * 3,
        scratch_shapes=[
            pltpu.SMEM((1, slots), jnp.int32),
            pltpu.SMEM((1, slots), jnp.int32),
            pltpu.VMEM((2, 1, slots), jnp.int32),
            pltpu.VMEM((8, 128), jnp.int32),
            pltpu.SMEM((8, 128), jnp.int32),
            pltpu.VMEM((width, node_dev), BF16),
            pltpu.VMEM((width, out), BF16),
            pltpu.VMEM((slots, 64, 128), BF16),
            pltpu.VMEM((3, 64, 128), BF16),
            pltpu.VMEM((4, 3, 64, 128), BF16),
            pltpu.VMEM((3, 3, 64, 128), BF16),
            pltpu.VMEM((3 * n_g, 64, 128), BF16),
            pltpu.VMEM((slots + 1, 64, 128), F32),
            pltpu.VMEM((n_col, 3, 64, 128), BF16),
            pltpu.VMEM((n_z, 3, 64, 128), BF16),
            pltpu.VMEM((n_z - 1, 3, 64, 128), BF16),
            pltpu.VMEM((n_z - 1, 3, 64, 128), BF16),
            pltpu.VMEM((3 * n_col, 64, 128), BF16),
            pltpu.VMEM((3, 64, 128), BF16),
            pltpu.VMEM((slots + 1, 128, 128), F32),
            pltpu.VMEM((3 * n_g, 64, 128), BF16),
            pltpu.VMEM((n_g - 1, 3, 64, 128), BF16),
            pltpu.VMEM((4, 3, 64, 128), BF16),
            pltpu.VMEM((n_g, piece_rows, 128), F32),
            pltpu.VMEM((n_g, piece_rows, 128), BF16),
            pltpu.VMEM((n_g - 1, piece_rows, 128), BF16),
            pltpu.VMEM((n_z, piece_rows, 128), BF16),
            pltpu.VMEM((piece_rows, 128), F32),
        ] + [dma((n,)) for n in sem_counts],
        compiler_params=pltpu.CompilerParams(
            collective_id=0, has_side_effects=True, vmem_limit_bytes=60 * 1024 * 1024),
    )(
        tile_rows.reshape(1, slots), tile_cols.reshape(1, slots), tile_count,
        features.T, weight, tile_values.reshape(slots, 2, 64, 128), cotangent.reshape(3, 2, 64, out),
    )
    return act.reshape(node_dev, out), fg.T.reshape(1, node_dev, width), wg


def solution(mesh):
    return jax.shard_map(
        functools.partial(shards, mesh.shape["row"], mesh.shape["col"] // 2),
        mesh=mesh,
        in_specs=(
            P("col", "feat"),
            P("feat", None),
            P("row", "col", None, None, None),
            P("row", "col", None),
            P("row", "col", None),
            P("row", "col"),
            P(("row", "col"), None),
        ),
        out_specs=(P(("row", "col"), None), P("col", "row", "feat"), P("feat", None)),
        check_vma=False,
    )
```

```python
import functools
import math

import jax
import jax.numpy as jnp
from jax import lax
from jax.experimental import pallas as pl
from jax.experimental.pallas import tpu as pltpu
from jax.sharding import PartitionSpec as P

MESH = pl.DeviceIdType.MESH
F32 = jnp.float32
BF16 = jnp.bfloat16


def far_first(n):
    return sorted(range(1, n), key=lambda k: (-min(k, n - k), k))


def kernel(
    n_row, n_z, slots, total_nodes,
    rows_hbm, cols_hbm, count_s, feat_hbm, w_hbm, tiles_hbm, cot_hbm,
    act_out, fg_out, wg_out,
    rows_s, cols_s, keys_v, links_v, links_s,
    x_v, w_ref, tiles_v, cot_v,
    y_send, y_recv, y_buf, prod_f,
    s_buf, yh_recv, t_buf, z_recv, hg_buf, act_v,
    prod_b, b_both, b_recv, b_full,
    xt_both, u_send, u_recv, v_buf, wg_piece,
    in_sem, p1_s, p1_r, p2_s, p2_r, p3a_s, p3a_r, p3b_s, p3b_r,
    act_s, act_r, p4z_s, p4z_r, p4y_s, p4y_r, xg_s, xg_r, bc_s, bc_r, p5_s, p5_r, p6_s, p6_r,
    k1_s, k1_r, k2_s, k2_r, k3_s, k3_r,
):
    f = lax.axis_index("feat")
    r = lax.axis_index("row")
    c = lax.axis_index("col")
    y_low, b = f // 2, f % 2
    z, h = c // 2, c % 2
    a = (y_low + h) % 2
    n_g = 2 * n_row

    def feat_of(role, core):
        return ((role + h) % 2) * 2 + core

    def remote(src, dst, send, recv, device):
        return pltpu.make_async_remote_copy(
            src_ref=src, dst_ref=dst, send_sem=send, recv_sem=recv, device_id=device, device_id_type=MESH
        )

    feat_peers = [{"feat": (f + k) % 4} for k in range(1, 4)]

    def g_peer(k):
        g2 = (2 * r + a + k) % n_g
        return g2, {"feat": feat_of(g2 % 2, b), "row": g2 // 2}

    def u_peer(k):
        u2 = (2 * r + h + k) % n_g
        return u2, {"row": u2 // 2, "col": 2 * z + u2 % 2}

    def z_peer(k):
        return {"col": 2 * ((z + k) % n_z) + h}

    y_partner = {"feat": (f + 2) % 4, "col": c + 1 - 2 * h}

    node_dev = x_v.shape[1]
    in_x = pltpu.make_async_copy(
        feat_hbm.at[:, pl.ds(pl.multiple_of(r * node_dev, node_dev), node_dev)], x_v, in_sem.at[0])
    in_w = pltpu.make_async_copy(w_hbm, w_ref, in_sem.at[5])
    in_keys = [
        pltpu.make_async_copy(rows_hbm, keys_v.at[0], in_sem.at[6]),
        pltpu.make_async_copy(cols_hbm, keys_v.at[1], in_sem.at[7]),
        pltpu.make_async_copy(rows_hbm, rows_s, in_sem.at[8]),
        pltpu.make_async_copy(cols_hbm, cols_s, in_sem.at[9]),
    ]
    in_t = pltpu.make_async_copy(tiles_hbm.at[:, a], tiles_v, in_sem.at[1])
    in_c = pltpu.make_async_copy(
        cot_hbm.at[:, a, :, pl.ds(pl.multiple_of(b * 128, 128), 128)], cot_v, in_sem.at[2])
    in_x.start()
    in_w.start()
    for cp in in_keys:
        cp.start()
    in_t.start()
    in_c.start()
    in_xt = pltpu.make_async_copy(feat_hbm, xt_both.at[y_low], in_sem.at[11])
    in_xt.start()

    barrier = pltpu.get_barrier_semaphore()
    peers = list(feat_peers)
    for k in range(1, n_row):
        peers.append({"row": (r + k) % n_row})
        peers.append({"feat": (f + 2) % 4, "row": (r + k) % n_row})
    peers += [z_peer(k) for k in range(1, n_z)]
    peers.append(y_partner)
    peers += [{"row": (r + k) % n_row, "col": c + 1 - 2 * h} for k in range(n_row)]
    peers += [{"feat": (f + 2) % 4, "row": (r + k) % n_row, "col": c + 1 - 2 * h} for k in range(1, n_row)]
    for peer in peers:
        pl.semaphore_signal(barrier, inc=1, device_id=peer, device_id_type=MESH)

    in_x.wait()
    in_w.wait()
    y_part = lax.dot_general(
        x_v[...], w_ref[...], (((0,), (0,)), ((), ())), preferred_element_type=F32).astype(BF16)
    for q in range(2):
        for core in range(2):
            y_send[2 * q + core] = y_part[192 * q:192 * (q + 1), 128 * core:128 * (core + 1)].reshape(3, 64, 128)
    pl.semaphore_wait(barrier, len(peers))

    copies = []
    for k in range(1, 4):
        f2 = (f + k) % 4
        piece = ((f2 // 2 + h) % 2) * 2 + f2 % 2
        cp = remote(y_send.at[piece], y_recv.at[k - 1], p1_s.at[k - 1], p1_r.at[k - 1], feat_peers[k - 1])
        cp.start()
        copies.append(cp)
    for cp in in_keys:
        cp.wait()
    ids = lax.broadcasted_iota(jnp.int32, (slots, 128), 0)
    lanes = lax.broadcasted_iota(jnp.int32, (slots, 128), 1)
    live = ids < count_s[0, 0]
    for i in range(2):
        across = jnp.broadcast_to(keys_v[i], (slots, slots))
        across = jnp.concatenate([across, jnp.zeros((slots, 128 - slots), jnp.int32)], axis=1)
        down = jnp.sum(jnp.where(ids == lanes, across, 0), axis=1, keepdims=True)
        down = jnp.broadcast_to(down, (slots, 128))
        before = jnp.where(live & (ids < lanes) & (down == across), ids, -1)
        there = jnp.where(live & (down == lanes), ids, -1)
        for w, found in ((0, before), (1, there)):
            top = jnp.max(found, axis=0, keepdims=True)
            links_v[pl.ds(2 * i + w, 1), :] = jnp.where(top < 0, slots, top)
    links = pltpu.make_async_copy(links_v, links_s, in_sem.at[10])
    links.start()
    total = y_send[2 * a + b].astype(F32)
    for k in range(3):
        copies[k].wait_recv()
        total = total + y_recv[k].astype(F32)
    g = 2 * r + a
    y_buf[pl.ds(3 * g, 3)] = total.astype(BF16)

    p2 = []
    for k in range(1, n_g):
        _, dev = g_peer(k)
        cp = remote(y_buf.at[pl.ds(3 * g, 3)], y_buf.at[pl.ds(3 * g, 3)], p2_s.at[k - 1], p2_r.at[k - 1], dev)
        cp.start()
        p2.append(cp)
    prod_f[slots] = jnp.zeros((64, 128), F32)
    prod_b[slots] = jnp.zeros((128, 128), F32)
    in_t.wait()
    links.wait()
    for k in range(1, n_g):
        src = (g + n_g - k) % n_g
        remote(y_buf.at[pl.ds(3 * src, 3)], y_buf.at[pl.ds(3 * src, 3)], p2_s.at[k - 1], p2_r.at[k - 1],
               y_partner).wait_recv()

    xg = remote(feat_hbm, xt_both.at[y_low], xg_s.at[0], xg_r.at[0], {"feat": (f + 2) % 4})
    xg.start()

    def forward(s, _):
        block = y_buf[pl.ds(2 * cols_s[0, s], 2)].reshape(128, 128)
        prod_f[s] = jnp.dot(tiles_v[s], block, preferred_element_type=F32)
        return 0

    lax.fori_loop(0, slots, forward, 0, unroll=8)

    def chain_forward(s, _):
        prod_f[s] = prod_f[s] + prod_f[links_s[0, s]]
        return 0

    lax.fori_loop(0, slots, chain_forward, 0, unroll=4)

    def fill(c2):
        for w in range(3):
            s_buf[c2, w] = prod_f[links_s[1, 3 * c2 + w]].astype(BF16)

    offs = far_first(n_z) + [0]
    p3a = []
    for j, off in enumerate(offs):
        c2 = 2 * ((z + off) % n_z) + 1 - h
        fill(c2)
        cp = remote(s_buf.at[c2], yh_recv.at[j], p3a_s.at[j], p3a_r.at[j], y_partner)
        cp.start()
        p3a.append(cp)
    for j, off in enumerate(offs):
        fill(2 * ((z + off) % n_z) + h)
    p3b = []
    for j, off in enumerate(offs):
        c2 = 2 * ((z + off) % n_z) + h
        p3a[j].wait_recv()
        both = s_buf[c2].astype(F32) + yh_recv[j].astype(F32)
        if off:
            t_buf[j] = both.astype(BF16)
            cp = remote(t_buf.at[j], z_recv.at[j], p3b_s.at[j], p3b_r.at[j], z_peer(off))
            cp.start()
            p3b.append(cp)
        else:
            hidden = both
    for j in range(n_z - 1):
        p3b[j].wait_recv()
        hidden = hidden + z_recv[j].astype(F32)

    in_c.wait()
    sigma = jax.nn.sigmoid(hidden)
    grad = cot_v[...].astype(F32) * (sigma * (1.0 + hidden * (1.0 - sigma)))
    hg_buf[pl.ds(3 * c, 3)] = grad.astype(BF16)
    act_v[...] = (hidden * sigma).astype(BF16)

    own = hg_buf.at[pl.ds(3 * c, 3)]
    p4y = [remote(own, own, p4y_s.at[n_z - 1], p4y_r.at[n_z - 1], y_partner)]
    p4y[0].start()
    def z_got(dist):
        return hg_buf.at[pl.ds(3 * (2 * ((z + 2 * n_z - dist) % n_z) + h), 3)]

    p4z = []

    def z_send(what, j, off):
        cp = remote(what, what, p4z_s.at[j], p4z_r.at[j], z_peer(off))
        cp.start()
        p4z.append(cp)

    def arrived(j, dist):
        got = z_got(dist)
        remote(got, got, p4z_s.at[j], p4z_r.at[j], y_partner).wait_recv()
        return got

    def y_forward(got, j):
        cp = remote(got, got, p4y_s.at[j], p4y_r.at[j], y_partner)
        cp.start()
        p4y.append(cp)

    side = 1 - 2 * (z % 2)
    z_send(own, 2, 2)
    z_send(own, 3, n_z - 2)
    z_send(own, 0, 1)
    z_send(own, 1, n_z - 1)
    y_forward(arrived(0, 1), 0)
    y_forward(arrived(1, n_z - 1), 1)
    plus = arrived(2, 2)
    z_send(plus, 4, 1)
    minus = arrived(3, n_z - 2)
    z_send(minus, 5, n_z - 1)
    z_send(hg_buf.at[pl.ds(3 * (2 * ((z + n_z - 2 * side) % n_z) + h), 3)], 6, 2 * side + n_z)
    y_forward(plus, 2)
    y_forward(minus, 3)
    act_cols = pl.ds(pl.multiple_of(b * 128, 128), 128)
    act_dst = act_out.at[:, a, :, act_cols]
    local = pltpu.make_async_copy(act_v, act_dst, in_sem.at[3])
    local.start()
    acts = []
    for k in range(1, 4):
        cp = remote(act_v, act_dst, act_s.at[k - 1], act_r.at[k - 1], feat_peers[k - 1])
        cp.start()
        acts.append(cp)
    y_forward(arrived(4, 3), 4)
    y_forward(arrived(5, n_z - 3), 5)
    y_forward(arrived(6, 4), 6)
    for j, dist in enumerate([1, n_z - 1, 2, n_z - 2, 3, n_z - 3, 4, 0]):
        got = hg_buf.at[pl.ds(3 * (2 * ((z + n_z - dist) % n_z) + 1 - h), 3)]
        remote(got, got, p4y_s.at[j], p4y_r.at[j], y_partner).wait_recv()

    def backward(s, _):
        prod_b[s] = lax.dot_general(
            tiles_v[s], hg_buf[rows_s[0, s]], (((0,), (0,)), ((), ())), preferred_element_type=F32)
        return 0

    lax.fori_loop(0, slots, backward, 0, unroll=8)

    def chain_backward(s, _):
        prod_b[s] = prod_b[s] + prod_b[links_s[2, s]]
        return 0

    lax.fori_loop(0, slots, chain_backward, 0, unroll=4)

    for j in range(3 * n_row):
        b_both[b, pl.ds(2 * j, 2)] = prod_b[links_s[3, j]].astype(BF16).reshape(2, 64, 128)

    bc = remote(b_both.at[b], b_both.at[b], bc_s.at[0], bc_r.at[0], {"feat": f + 1 - 2 * b})
    bc.start()

    p5 = []
    for k in range(1, n_g):
        g2, dev = g_peer(k)
        cp = remote(b_both.at[b, pl.ds(3 * g2, 3)], b_recv.at[k - 1], p5_s.at[k - 1], p5_r.at[k - 1], dev)
        cp.start()
        p5.append(cp)

    piece_rows = u_send.shape[2]
    in_xt.wait()
    xg.wait_recv()
    got = b_both.at[1 - b]
    remote(got, got, bc_s.at[0], bc_r.at[0], y_partner).wait_recv()
    both = jnp.concatenate([b_both[0].reshape(n_row * node_dev, 128), b_both[1].reshape(n_row * node_dev, 128)], axis=1)
    for low in range(2):
        part = jnp.dot(xt_both[low], both, preferred_element_type=F32).astype(BF16)
        for core in range(2):
            u_send[low, n_row * core:n_row * (core + 1)] = part[:, 128 * core:128 * (core + 1)].reshape(
                n_row, piece_rows, 128)
    u = 2 * r + h
    k1 = []
    for k in range(1, 2 * n_g):
        q2 = (n_g * y_low + u + k) % (2 * n_g)
        low2, u2 = q2 // n_g, q2 % n_g
        dev = {"feat": 2 * low2 + b, "row": u2 // 2, "col": 2 * z + u2 % 2}
        cp = remote(u_send.at[low2, u2], u_recv.at[k - 1], k1_s.at[k - 1], k1_r.at[k - 1], dev)
        cp.start()
        k1.append(cp)

    total = b_both[b, pl.ds(3 * g, 3)].astype(F32)
    for k in range(n_g - 1):
        p5[k].wait_recv()
        total = total + b_recv[k].astype(F32)
    b_full[2 * b + a] = total.astype(BF16)
    mine = b_full.at[2 * b + a]
    p6 = []
    for k in range(1, 4):
        cp = remote(mine, mine, p6_s.at[k - 1], p6_r.at[k - 1], feat_peers[k - 1])
        cp.start()
        p6.append(cp)

    total = u_send[y_low, u].astype(F32)
    for k in range(2 * n_g - 1):
        k1[k].wait_recv()
        total = total + u_recv[k].astype(F32)
    v_buf[z] = total.astype(BF16)
    k2 = []
    for j, off in enumerate(offs[:-1]):
        cp = remote(v_buf.at[z], v_buf.at[z], k2_s.at[j], k2_r.at[j], z_peer(off))
        cp.start()
        k2.append(cp)

    for k in range(1, 4):
        f2 = (f + 4 - k) % 4
        got = b_full.at[2 * (f2 % 2) + (f2 // 2 + h) % 2]
        remote(got, got, p6_s.at[k - 1], p6_r.at[k - 1], y_partner).wait_recv()
    grad_t = jnp.zeros((w_ref.shape[0], node_dev), F32)
    for core in range(2):
        grad_t = grad_t + lax.dot_general(
            w_ref[:, 128 * core:128 * (core + 1)], b_full[2 * core:2 * core + 2].reshape(node_dev, 128),
            (((1,), (1,)), ((), ())), preferred_element_type=F32)
    fg_out[...] = grad_t.astype(BF16)

    for j, off in enumerate(offs[:-1]):
        got = v_buf.at[(z + n_z - off) % n_z]
        remote(got, got, k2_s.at[j], k2_r.at[j], y_partner).wait_recv()
    total = v_buf[0].astype(F32)
    for j in range(1, n_z):
        total = total + v_buf[j].astype(F32)
    wg_piece[...] = total * (1.0 / math.sqrt(total_nodes))

    def wg_place(piece):
        return wg_out.at[
            pl.ds(pl.multiple_of((piece % n_row) * piece_rows, piece_rows), piece_rows),
            pl.ds(pl.multiple_of((piece // n_row) * 128, 128), 128),
        ]

    local_wg = pltpu.make_async_copy(wg_piece, wg_place(u), in_sem.at[4])
    local_wg.start()
    k3 = []
    for k in range(1, n_g):
        _, dev = u_peer(k)
        cp = remote(wg_piece, wg_place(u), k3_s.at[k - 1], k3_r.at[k - 1], dev)
        cp.start()
        k3.append(cp)
    for k in range(1, n_g):
        got = wg_place((u + n_g - k) % n_g)
        remote(wg_piece, got, k3_s.at[k - 1], k3_r.at[k - 1], y_partner).wait_recv()
    for k in range(1, 4):
        f2 = (f + 4 - k) % 4
        got = act_out.at[:, (f2 // 2 + h) % 2, :, pl.ds(pl.multiple_of((f2 % 2) * 128, 128), 128)]
        remote(act_v, got, act_s.at[k - 1], act_r.at[k - 1], y_partner).wait_recv()
    local.wait()
    local_wg.wait()
    for cp in copies + p2 + p3a + p3b + p4y + p4z + acts + p5 + p6 + k1 + k2 + k3 + [xg, bc]:
        cp.wait_send()


def shards(n_row, n_z, features, weight, tile_values, tile_rows, tile_cols, tile_count, cotangent):
    slots = tile_values.shape[2]
    node_dev, out = cotangent.shape
    width = features.shape[1]
    n_g = 2 * n_row
    n_col = 2 * n_z
    piece_rows = 2 * width // n_g
    dma = pltpu.SemaphoreType.DMA
    smem = pl.BlockSpec(memory_space=pltpu.SMEM)
    vmem = pl.BlockSpec(memory_space=pltpu.VMEM)
    hbm = pl.BlockSpec(memory_space=pltpu.HBM)
    sem_counts = [12, 3, 3, n_g - 1, n_g - 1, n_z, n_z, n_z - 1, n_z - 1, 3, 3, n_z - 1, n_z - 1, n_z, n_z,
                  1, 1, 1, 1, n_g - 1, n_g - 1, 3, 3, 2 * n_g - 1, 2 * n_g - 1, n_z - 1, n_z - 1, n_g - 1, n_g - 1]
    act, fg, wg = pl.pallas_call(
        functools.partial(kernel, n_row, n_z, slots, node_dev * n_row * n_col),
        out_shape=[
            jax.ShapeDtypeStruct((3, 2, 64, out), BF16),
            jax.ShapeDtypeStruct((width, node_dev), BF16),
            jax.ShapeDtypeStruct((width, out), F32),
        ],
        in_specs=[hbm, hbm, smem, hbm, hbm, hbm, hbm],
        out_specs=[vmem] * 3,
        scratch_shapes=[
            pltpu.SMEM((1, slots), jnp.int32),
            pltpu.SMEM((1, slots), jnp.int32),
            pltpu.VMEM((2, 1, slots), jnp.int32),
            pltpu.VMEM((8, 128), jnp.int32),
            pltpu.SMEM((8, 128), jnp.int32),
            pltpu.VMEM((width, node_dev), BF16),
            pltpu.VMEM((width, out), BF16),
            pltpu.VMEM((slots, 64, 128), BF16),
            pltpu.VMEM((3, 64, 128), BF16),
            pltpu.VMEM((4, 3, 64, 128), BF16),
            pltpu.VMEM((3, 3, 64, 128), BF16),
            pltpu.VMEM((3 * n_g, 64, 128), BF16),
            pltpu.VMEM((slots + 1, 64, 128), F32),
            pltpu.VMEM((n_col, 3, 64, 128), BF16),
            pltpu.VMEM((n_z, 3, 64, 128), BF16),
            pltpu.VMEM((n_z - 1, 3, 64, 128), BF16),
            pltpu.VMEM((n_z - 1, 3, 64, 128), BF16),
            pltpu.VMEM((3 * n_col, 64, 128), BF16),
            pltpu.VMEM((3, 64, 128), BF16),
            pltpu.VMEM((slots + 1, 128, 128), F32),
            pltpu.VMEM((2, 3 * n_g, 64, 128), BF16),
            pltpu.VMEM((n_g - 1, 3, 64, 128), BF16),
            pltpu.VMEM((4, 3, 64, 128), BF16),
            pltpu.VMEM((2, width, n_row * node_dev), BF16),
            pltpu.VMEM((2, n_g, piece_rows, 128), BF16),
            pltpu.VMEM((2 * n_g - 1, piece_rows, 128), BF16),
            pltpu.VMEM((n_z, piece_rows, 128), BF16),
            pltpu.VMEM((piece_rows, 128), F32),
        ] + [dma((n,)) for n in sem_counts],
        compiler_params=pltpu.CompilerParams(
            collective_id=0, has_side_effects=True, vmem_limit_bytes=60 * 1024 * 1024),
    )(
        tile_rows.reshape(1, slots), tile_cols.reshape(1, slots), tile_count,
        features.T, weight, tile_values.reshape(slots, 2, 64, 128), cotangent.reshape(3, 2, 64, out),
    )
    return act.reshape(node_dev, out), fg.T.reshape(1, node_dev, width), wg


def solution(mesh):
    return jax.shard_map(
        functools.partial(shards, mesh.shape["row"], mesh.shape["col"] // 2),
        mesh=mesh,
        in_specs=(
            P("col", "feat"),
            P("feat", None),
            P("row", "col", None, None, None),
            P("row", "col", None),
            P("row", "col", None),
            P("row", "col"),
            P(("row", "col"), None),
        ),
        out_specs=(P(("row", "col"), None), P("col", "row", "feat"), P("feat", None)),
        check_vma=False,
    )
```

```python
import functools
import math

import jax
import jax.numpy as jnp
from jax import lax
from jax.experimental import pallas as pl
from jax.experimental.pallas import tpu as pltpu
from jax.sharding import PartitionSpec as P

MESH = pl.DeviceIdType.MESH
F32 = jnp.float32
BF16 = jnp.bfloat16


def far_first(n):
    return sorted(range(1, n), key=lambda k: (-min(k, n - k), k))


def kernel(
    n_row, n_z, slots, total_nodes,
    rows_hbm, cols_hbm, count_s, feat_hbm, w_hbm, tiles_hbm, cot_hbm,
    act_out, fg_out, wg_out,
    rows_s, cols_s, keys_v, links_v, links_s,
    x_v, w_ref, tiles_v, cot_v,
    y_send, y_recv, y_buf, prod_f,
    s_buf, yh_recv, t_buf, z_recv, hg_buf, act_v,
    prod_b, b_both, b_recv, b_full,
    xt_both, u_send, u_recv, v_buf, wg_piece,
    in_sem, p1_s, p1_r, p2_s, p2_r, p3a_s, p3a_r, p3b_s, p3b_r,
    act_s, act_r, p4z_s, p4z_r, p4y_s, p4y_r, xg_s, xg_r, bc_s, bc_r, p5_s, p5_r, p6_s, p6_r,
    k1_s, k1_r, k2_s, k2_r, k3_s, k3_r,
):
    f = lax.axis_index("feat")
    r = lax.axis_index("row")
    c = lax.axis_index("col")
    y_low, b = f // 2, f % 2
    z, h = c // 2, c % 2
    a = (y_low + h) % 2
    n_g = 2 * n_row

    def feat_of(role, core):
        return ((role + h) % 2) * 2 + core

    def remote(src, dst, send, recv, device):
        return pltpu.make_async_remote_copy(
            src_ref=src, dst_ref=dst, send_sem=send, recv_sem=recv, device_id=device, device_id_type=MESH
        )

    feat_peers = [{"feat": (f + k) % 4} for k in range(1, 4)]

    def g_peer(k):
        g2 = (2 * r + a + k) % n_g
        return g2, {"feat": feat_of(g2 % 2, b), "row": g2 // 2}

    def u_peer(k):
        u2 = (2 * r + h + k) % n_g
        return u2, {"row": u2 // 2, "col": 2 * z + u2 % 2}

    def z_peer(k):
        return {"col": 2 * ((z + k) % n_z) + h}

    y_partner = {"feat": (f + 2) % 4, "col": c + 1 - 2 * h}

    node_dev = x_v.shape[1]
    in_x = pltpu.make_async_copy(
        feat_hbm.at[:, pl.ds(pl.multiple_of(r * node_dev, node_dev), node_dev)], x_v, in_sem.at[0])
    in_w = pltpu.make_async_copy(w_hbm, w_ref, in_sem.at[5])
    in_keys = [
        pltpu.make_async_copy(rows_hbm, keys_v.at[0], in_sem.at[6]),
        pltpu.make_async_copy(cols_hbm, keys_v.at[1], in_sem.at[7]),
        pltpu.make_async_copy(rows_hbm, rows_s, in_sem.at[8]),
        pltpu.make_async_copy(cols_hbm, cols_s, in_sem.at[9]),
    ]
    in_t = pltpu.make_async_copy(tiles_hbm.at[:, a], tiles_v, in_sem.at[1])
    in_c = pltpu.make_async_copy(
        cot_hbm.at[:, a, :, pl.ds(pl.multiple_of(b * 128, 128), 128)], cot_v, in_sem.at[2])
    in_x.start()
    in_w.start()
    for cp in in_keys:
        cp.start()
    in_t.start()
    in_c.start()
    in_xt = pltpu.make_async_copy(feat_hbm, xt_both.at[y_low], in_sem.at[11])
    in_xt.start()

    barrier = pltpu.get_barrier_semaphore()
    peers = list(feat_peers)
    for k in range(1, n_row):
        peers.append({"row": (r + k) % n_row})
        peers.append({"feat": (f + 2) % 4, "row": (r + k) % n_row})
    peers += [z_peer(k) for k in range(1, n_z)]
    peers.append(y_partner)
    peers += [{"row": (r + k) % n_row, "col": c + 1 - 2 * h} for k in range(n_row)]
    peers += [{"feat": (f + 2) % 4, "row": (r + k) % n_row, "col": c + 1 - 2 * h} for k in range(1, n_row)]
    for peer in peers:
        pl.semaphore_signal(barrier, inc=1, device_id=peer, device_id_type=MESH)

    in_x.wait()
    in_w.wait()
    y_part = lax.dot_general(
        x_v[...], w_ref[...], (((0,), (0,)), ((), ())), preferred_element_type=F32).astype(BF16)
    for q in range(2):
        for core in range(2):
            y_send[2 * q + core] = y_part[192 * q:192 * (q + 1), 128 * core:128 * (core + 1)].reshape(3, 64, 128)
    pl.semaphore_wait(barrier, len(peers))

    copies = []
    for k in range(1, 4):
        f2 = (f + k) % 4
        piece = ((f2 // 2 + h) % 2) * 2 + f2 % 2
        cp = remote(y_send.at[piece], y_recv.at[k - 1], p1_s.at[k - 1], p1_r.at[k - 1], feat_peers[k - 1])
        cp.start()
        copies.append(cp)
    for cp in in_keys:
        cp.wait()
    ids = lax.broadcasted_iota(jnp.int32, (slots, 128), 0)
    lanes = lax.broadcasted_iota(jnp.int32, (slots, 128), 1)
    live = ids < count_s[0, 0]
    for i in range(2):
        across = jnp.broadcast_to(keys_v[i], (slots, slots))
        across = jnp.concatenate([across, jnp.zeros((slots, 128 - slots), jnp.int32)], axis=1)
        down = jnp.sum(jnp.where(ids == lanes, across, 0), axis=1, keepdims=True)
        down = jnp.broadcast_to(down, (slots, 128))
        before = jnp.where(live & (ids < lanes) & (down == across), ids, -1)
        there = jnp.where(live & (down == lanes), ids, -1)
        for w, found in ((0, before), (1, there)):
            top = jnp.max(found, axis=0, keepdims=True)
            links_v[pl.ds(2 * i + w, 1), :] = jnp.where(top < 0, slots, top)
    links = pltpu.make_async_copy(links_v, links_s, in_sem.at[10])
    links.start()
    total = y_send[2 * a + b].astype(F32)
    for k in range(3):
        copies[k].wait_recv()
        total = total + y_recv[k].astype(F32)
    g = 2 * r + a
    y_buf[pl.ds(3 * g, 3)] = total.astype(BF16)

    p2 = []
    for k in range(1, n_g):
        _, dev = g_peer(k)
        cp = remote(y_buf.at[pl.ds(3 * g, 3)], y_buf.at[pl.ds(3 * g, 3)], p2_s.at[k - 1], p2_r.at[k - 1], dev)
        cp.start()
        p2.append(cp)
    prod_f[slots] = jnp.zeros((64, 128), F32)
    prod_b[slots] = jnp.zeros((128, 128), F32)
    in_t.wait()
    links.wait()
    for k in range(1, n_g):
        src = (g + n_g - k) % n_g
        remote(y_buf.at[pl.ds(3 * src, 3)], y_buf.at[pl.ds(3 * src, 3)], p2_s.at[k - 1], p2_r.at[k - 1],
               y_partner).wait_recv()

    xg = remote(feat_hbm, xt_both.at[y_low], xg_s.at[0], xg_r.at[0], {"feat": (f + 2) % 4})
    xg.start()

    def forward(s, _):
        block = y_buf[pl.ds(2 * cols_s[0, s], 2)].reshape(128, 128)
        prod_f[s] = jnp.dot(tiles_v[s], block, preferred_element_type=F32)
        return 0

    lax.fori_loop(0, slots, forward, 0, unroll=8)

    def chain_forward(s, _):
        prod_f[s] = prod_f[s] + prod_f[links_s[0, s]]
        return 0

    lax.fori_loop(0, slots, chain_forward, 0, unroll=4)

    def fill(c2):
        for w in range(3):
            s_buf[c2, w] = prod_f[links_s[1, 3 * c2 + w]].astype(BF16)

    offs = far_first(n_z) + [0]
    p3a = []
    for j, off in enumerate(offs):
        c2 = 2 * ((z + off) % n_z) + 1 - h
        fill(c2)
        cp = remote(s_buf.at[c2], yh_recv.at[j], p3a_s.at[j], p3a_r.at[j], y_partner)
        cp.start()
        p3a.append(cp)
    for j, off in enumerate(offs):
        fill(2 * ((z + off) % n_z) + h)
    p3b = []
    for j, off in enumerate(offs):
        c2 = 2 * ((z + off) % n_z) + h
        p3a[j].wait_recv()
        both = s_buf[c2].astype(F32) + yh_recv[j].astype(F32)
        if off:
            t_buf[j] = both.astype(BF16)
            cp = remote(t_buf.at[j], z_recv.at[j], p3b_s.at[j], p3b_r.at[j], z_peer(off))
            cp.start()
            p3b.append(cp)
        else:
            hidden = both
    for j in range(n_z - 1):
        p3b[j].wait_recv()
        hidden = hidden + z_recv[j].astype(F32)

    in_c.wait()
    sigma = jax.nn.sigmoid(hidden)
    grad = cot_v[...].astype(F32) * (sigma * (1.0 + hidden * (1.0 - sigma)))
    hg_buf[pl.ds(3 * c, 3)] = grad.astype(BF16)
    act_v[...] = (hidden * sigma).astype(BF16)

    own = hg_buf.at[pl.ds(3 * c, 3)]
    p4y = [remote(own, own, p4y_s.at[n_z - 1], p4y_r.at[n_z - 1], y_partner)]
    p4y[0].start()
    def z_got(dist):
        return hg_buf.at[pl.ds(3 * (2 * ((z + 2 * n_z - dist) % n_z) + h), 3)]

    p4z = []

    def z_send(what, j, off):
        cp = remote(what, what, p4z_s.at[j], p4z_r.at[j], z_peer(off))
        cp.start()
        p4z.append(cp)

    def arrived(j, dist):
        got = z_got(dist)
        remote(got, got, p4z_s.at[j], p4z_r.at[j], y_partner).wait_recv()
        return got

    def y_forward(got, j):
        cp = remote(got, got, p4y_s.at[j], p4y_r.at[j], y_partner)
        cp.start()
        p4y.append(cp)

    side = 1 - 2 * (z % 2)
    z_send(own, 2, 2)
    z_send(own, 3, n_z - 2)
    z_send(own, 0, 1)
    z_send(own, 1, n_z - 1)
    y_forward(arrived(0, 1), 0)
    y_forward(arrived(1, n_z - 1), 1)
    plus = arrived(2, 2)
    z_send(plus, 4, 1)
    minus = arrived(3, n_z - 2)
    z_send(minus, 5, n_z - 1)
    z_send(hg_buf.at[pl.ds(3 * (2 * ((z + n_z - 2 * side) % n_z) + h), 3)], 6, 2 * side + n_z)
    y_forward(plus, 2)
    y_forward(minus, 3)
    act_cols = pl.ds(pl.multiple_of(b * 128, 128), 128)
    act_dst = act_out.at[:, a, :, act_cols]
    local = pltpu.make_async_copy(act_v, act_dst, in_sem.at[3])
    local.start()
    acts = []
    for k in range(1, 4):
        cp = remote(act_v, act_dst, act_s.at[k - 1], act_r.at[k - 1], feat_peers[k - 1])
        cp.start()
        acts.append(cp)
    y_forward(arrived(4, 3), 4)
    y_forward(arrived(5, n_z - 3), 5)
    y_forward(arrived(6, 4), 6)
    for j, dist in enumerate([1, n_z - 1, 2, n_z - 2, 3, n_z - 3, 4, 0]):
        got = hg_buf.at[pl.ds(3 * (2 * ((z + n_z - dist) % n_z) + 1 - h), 3)]
        remote(got, got, p4y_s.at[j], p4y_r.at[j], y_partner).wait_recv()

    def backward(s, _):
        prod_b[s] = lax.dot_general(
            tiles_v[s], hg_buf[rows_s[0, s]], (((0,), (0,)), ((), ())), preferred_element_type=F32)
        return 0

    lax.fori_loop(0, slots, backward, 0, unroll=8)

    def chain_backward(s, _):
        prod_b[s] = prod_b[s] + prod_b[links_s[2, s]]
        return 0

    lax.fori_loop(0, slots, chain_backward, 0, unroll=4)

    for j in range(3 * n_row):
        b_both[b, pl.ds(2 * j, 2)] = prod_b[links_s[3, j]].astype(BF16).reshape(2, 64, 128)

    bc = remote(b_both.at[b], b_both.at[b], bc_s.at[0], bc_r.at[0], {"feat": f + 1 - 2 * b})
    bc.start()

    piece_rows = u_send.shape[2]
    in_xt.wait()
    xg.wait_recv()
    got = b_both.at[1 - b]
    remote(got, got, bc_s.at[0], bc_r.at[0], y_partner).wait_recv()
    both = jnp.concatenate([b_both[0].reshape(n_row * node_dev, 128), b_both[1].reshape(n_row * node_dev, 128)], axis=1)
    for low in range(2):
        part = jnp.dot(xt_both[low], both, preferred_element_type=F32).astype(BF16)
        for core in range(2):
            u_send[low, n_row * core:n_row * (core + 1)] = part[:, 128 * core:128 * (core + 1)].reshape(
                n_row, piece_rows, 128)
    u = 2 * r + h
    k1 = []
    for k in range(1, 2 * n_g):
        q2 = (n_g * y_low + u + k) % (2 * n_g)
        low2, u2 = q2 // n_g, q2 % n_g
        dev = {"feat": 2 * low2 + b, "row": u2 // 2, "col": 2 * z + u2 % 2}
        cp = remote(u_send.at[low2, u2], u_recv.at[k - 1], k1_s.at[k - 1], k1_r.at[k - 1], dev)
        cp.start()
        k1.append(cp)

    p5 = []
    for k in range(1, n_g):
        g2, dev = g_peer(k)
        cp = remote(b_both.at[b, pl.ds(3 * g2, 3)], b_recv.at[k - 1], p5_s.at[k - 1], p5_r.at[k - 1], dev)
        cp.start()
        p5.append(cp)

    total = u_send[y_low, u].astype(F32)
    for k in range(2 * n_g - 1):
        k1[k].wait_recv()
        total = total + u_recv[k].astype(F32)
    v_buf[z] = total.astype(BF16)
    k2 = []
    for j, off in enumerate(offs[:-1]):
        cp = remote(v_buf.at[z], v_buf.at[z], k2_s.at[j], k2_r.at[j], z_peer(off))
        cp.start()
        k2.append(cp)

    total = b_both[b, pl.ds(3 * g, 3)].astype(F32)
    for k in range(n_g - 1):
        p5[k].wait_recv()
        total = total + b_recv[k].astype(F32)
    b_full[2 * b + a] = total.astype(BF16)
    mine = b_full.at[2 * b + a]
    p6 = []
    for k in range(1, 4):
        cp = remote(mine, mine, p6_s.at[k - 1], p6_r.at[k - 1], feat_peers[k - 1])
        cp.start()
        p6.append(cp)

    for j, off in enumerate(offs[:-1]):
        got = v_buf.at[(z + n_z - off) % n_z]
        remote(got, got, k2_s.at[j], k2_r.at[j], y_partner).wait_recv()
    total = v_buf[0].astype(F32)
    for j in range(1, n_z):
        total = total + v_buf[j].astype(F32)
    wg_piece[...] = total * (1.0 / math.sqrt(total_nodes))

    def wg_place(piece):
        return wg_out.at[
            pl.ds(pl.multiple_of((piece % n_row) * piece_rows, piece_rows), piece_rows),
            pl.ds(pl.multiple_of((piece // n_row) * 128, 128), 128),
        ]

    local_wg = pltpu.make_async_copy(wg_piece, wg_place(u), in_sem.at[4])
    local_wg.start()
    k3 = []
    for k in range(1, n_g):
        _, dev = u_peer(k)
        cp = remote(wg_piece, wg_place(u), k3_s.at[k - 1], k3_r.at[k - 1], dev)
        cp.start()
        k3.append(cp)
    for k in range(1, 4):
        f2 = (f + 4 - k) % 4
        got = b_full.at[2 * (f2 % 2) + (f2 // 2 + h) % 2]
        remote(got, got, p6_s.at[k - 1], p6_r.at[k - 1], y_partner).wait_recv()
    grad_t = jnp.zeros((w_ref.shape[0], node_dev), F32)
    for core in range(2):
        grad_t = grad_t + lax.dot_general(
            w_ref[:, 128 * core:128 * (core + 1)], b_full[2 * core:2 * core + 2].reshape(node_dev, 128),
            (((1,), (1,)), ((), ())), preferred_element_type=F32)
    fg_out[...] = grad_t.astype(BF16)

    for k in range(1, n_g):
        got = wg_place((u + n_g - k) % n_g)
        remote(wg_piece, got, k3_s.at[k - 1], k3_r.at[k - 1], y_partner).wait_recv()
    for k in range(1, 4):
        f2 = (f + 4 - k) % 4
        got = act_out.at[:, (f2 // 2 + h) % 2, :, pl.ds(pl.multiple_of((f2 % 2) * 128, 128), 128)]
        remote(act_v, got, act_s.at[k - 1], act_r.at[k - 1], y_partner).wait_recv()
    local.wait()
    local_wg.wait()
    for cp in copies + p2 + p3a + p3b + p4y + p4z + acts + p5 + p6 + k1 + k2 + k3 + [xg, bc]:
        cp.wait_send()


def shards(n_row, n_z, features, weight, tile_values, tile_rows, tile_cols, tile_count, cotangent):
    slots = tile_values.shape[2]
    node_dev, out = cotangent.shape
    width = features.shape[1]
    n_g = 2 * n_row
    n_col = 2 * n_z
    piece_rows = 2 * width // n_g
    dma = pltpu.SemaphoreType.DMA
    pin = lambda x: pltpu.with_memory_space_constraint(x, pltpu.HBM)
    smem = pl.BlockSpec(memory_space=pltpu.SMEM)
    vmem = pl.BlockSpec(memory_space=pltpu.VMEM)
    hbm = pl.BlockSpec(memory_space=pltpu.HBM)
    sem_counts = [12, 3, 3, n_g - 1, n_g - 1, n_z, n_z, n_z - 1, n_z - 1, 3, 3, n_z - 1, n_z - 1, n_z, n_z,
                  1, 1, 1, 1, n_g - 1, n_g - 1, 3, 3, 2 * n_g - 1, 2 * n_g - 1, n_z - 1, n_z - 1, n_g - 1, n_g - 1]
    act, fg, wg = pl.pallas_call(
        functools.partial(kernel, n_row, n_z, slots, node_dev * n_row * n_col),
        out_shape=[
            jax.ShapeDtypeStruct((3, 2, 64, out), BF16),
            jax.ShapeDtypeStruct((width, node_dev), BF16),
            jax.ShapeDtypeStruct((width, out), F32),
        ],
        in_specs=[hbm, hbm, smem, hbm, hbm, hbm, hbm],
        out_specs=[vmem] * 3,
        scratch_shapes=[
            pltpu.SMEM((1, slots), jnp.int32),
            pltpu.SMEM((1, slots), jnp.int32),
            pltpu.VMEM((2, 1, slots), jnp.int32),
            pltpu.VMEM((8, 128), jnp.int32),
            pltpu.SMEM((8, 128), jnp.int32),
            pltpu.VMEM((width, node_dev), BF16),
            pltpu.VMEM((width, out), BF16),
            pltpu.VMEM((slots, 64, 128), BF16),
            pltpu.VMEM((3, 64, 128), BF16),
            pltpu.VMEM((4, 3, 64, 128), BF16),
            pltpu.VMEM((3, 3, 64, 128), BF16),
            pltpu.VMEM((3 * n_g, 64, 128), BF16),
            pltpu.VMEM((slots + 1, 64, 128), F32),
            pltpu.VMEM((n_col, 3, 64, 128), BF16),
            pltpu.VMEM((n_z, 3, 64, 128), BF16),
            pltpu.VMEM((n_z - 1, 3, 64, 128), BF16),
            pltpu.VMEM((n_z - 1, 3, 64, 128), BF16),
            pltpu.VMEM((3 * n_col, 64, 128), BF16),
            pltpu.VMEM((3, 64, 128), BF16),
            pltpu.VMEM((slots + 1, 128, 128), F32),
            pltpu.VMEM((2, 3 * n_g, 64, 128), BF16),
            pltpu.VMEM((n_g - 1, 3, 64, 128), BF16),
            pltpu.VMEM((4, 3, 64, 128), BF16),
            pltpu.VMEM((2, width, n_row * node_dev), BF16),
            pltpu.VMEM((2, n_g, piece_rows, 128), BF16),
            pltpu.VMEM((2 * n_g - 1, piece_rows, 128), BF16),
            pltpu.VMEM((n_z, piece_rows, 128), BF16),
            pltpu.VMEM((piece_rows, 128), F32),
        ] + [dma((n,)) for n in sem_counts],
        compiler_params=pltpu.CompilerParams(
            collective_id=0, has_side_effects=True, vmem_limit_bytes=40 * 1024 * 1024),
    )(
        pin(tile_rows.reshape(1, slots)), pin(tile_cols.reshape(1, slots)), tile_count,
        pin(features.T), pin(weight), pin(tile_values.reshape(slots, 2, 64, 128)), pin(cotangent.reshape(3, 2, 64, out)),
    )
    return act.reshape(node_dev, out), fg.T.reshape(1, node_dev, width), wg


def solution(mesh):
    return jax.shard_map(
        functools.partial(shards, mesh.shape["row"], mesh.shape["col"] // 2),
        mesh=mesh,
        in_specs=(
            P("col", "feat"),
            P("feat", None),
            P("row", "col", None, None, None),
            P("row", "col", None),
            P("row", "col", None),
            P("row", "col"),
            P(("row", "col"), None),
        ),
        out_specs=(P(("row", "col"), None), P("col", "row", "feat"), P("feat", None)),
        check_vma=False,
    )
```

```python
import functools
import math

import jax
import jax.numpy as jnp
from jax import lax
from jax.experimental import pallas as pl
from jax.experimental.pallas import tpu as pltpu
from jax.sharding import PartitionSpec as P

MESH = pl.DeviceIdType.MESH
F32 = jnp.float32
BF16 = jnp.bfloat16


def far_first(n):
    return sorted(range(1, n), key=lambda k: (-min(k, n - k), k))


def kernel(
    n_row, n_z, slots, total_nodes,
    rows_hbm, cols_hbm, count_s, feat_hbm, w_hbm, tiles_hbm, cot_hbm,
    act_out, fg_out, wg_out,
    rows_s, cols_s, keys_v, links_v, links_s,
    x_v, w_ref, tiles_v, cot_v,
    y_send, y_recv, y_buf, prod_f,
    s_buf, yh_recv, t_buf, z_recv, hg_buf, act_v,
    prod_b, b_both, b_recv, b_full,
    xt_both, u_send, u_recv, v_buf, wg_piece,
    in_sem, p1_s, p1_r, p2_s, p2_r, p3a_s, p3a_r, p3b_s, p3b_r,
    act_s, act_r, p4z_s, p4z_r, p4y_s, p4y_r, xg_s, xg_r, bc_s, bc_r, p5_s, p5_r, p6_s, p6_r,
    k1_s, k1_r, k2_s, k2_r, k3_s, k3_r,
):
    f = lax.axis_index("feat")
    r = lax.axis_index("row")
    c = lax.axis_index("col")
    y_low, b = f // 2, f % 2
    z, h = c // 2, c % 2
    a = (y_low + h) % 2
    n_g = 2 * n_row

    def feat_of(role, core):
        return ((role + h) % 2) * 2 + core

    def remote(src, dst, send, recv, device):
        return pltpu.make_async_remote_copy(
            src_ref=src, dst_ref=dst, send_sem=send, recv_sem=recv, device_id=device, device_id_type=MESH
        )

    feat_peers = [{"feat": (f + k) % 4} for k in range(1, 4)]

    def g_peer(k):
        g2 = (2 * r + a + k) % n_g
        return g2, {"feat": feat_of(g2 % 2, b), "row": g2 // 2}

    def u_peer(k):
        u2 = (2 * r + h + k) % n_g
        return u2, {"row": u2 // 2, "col": 2 * z + u2 % 2}

    def z_peer(k):
        return {"col": 2 * ((z + k) % n_z) + h}

    y_partner = {"feat": (f + 2) % 4, "col": c + 1 - 2 * h}

    node_dev = x_v.shape[1]
    in_x = pltpu.make_async_copy(
        feat_hbm.at[:, pl.ds(pl.multiple_of(r * node_dev, node_dev), node_dev)], x_v, in_sem.at[0])
    in_w = pltpu.make_async_copy(w_hbm, w_ref, in_sem.at[5])
    in_keys = [
        pltpu.make_async_copy(rows_hbm, keys_v.at[0], in_sem.at[6]),
        pltpu.make_async_copy(cols_hbm, keys_v.at[1], in_sem.at[7]),
        pltpu.make_async_copy(rows_hbm, rows_s, in_sem.at[8]),
        pltpu.make_async_copy(cols_hbm, cols_s, in_sem.at[9]),
    ]
    in_t = pltpu.make_async_copy(tiles_hbm.at[:, a], tiles_v, in_sem.at[1])
    in_c = pltpu.make_async_copy(
        cot_hbm.at[:, a, :, pl.ds(pl.multiple_of(b * 128, 128), 128)], cot_v, in_sem.at[2])
    in_x.start()
    in_w.start()

    barrier = pltpu.get_barrier_semaphore()
    peers = list(feat_peers)
    for k in range(1, n_row):
        peers.append({"row": (r + k) % n_row})
        peers.append({"feat": (f + 2) % 4, "row": (r + k) % n_row})
    peers += [z_peer(k) for k in range(1, n_z)]
    peers.append(y_partner)
    peers += [{"row": (r + k) % n_row, "col": c + 1 - 2 * h} for k in range(n_row)]
    peers += [{"feat": (f + 2) % 4, "row": (r + k) % n_row, "col": c + 1 - 2 * h} for k in range(1, n_row)]
    for peer in reversed(peers):
        pl.semaphore_signal(barrier, inc=1, device_id=peer, device_id_type=MESH)
    for cp in in_keys:
        cp.start()
    in_t.start()
    in_c.start()
    in_xt = pltpu.make_async_copy(feat_hbm, xt_both.at[y_low], in_sem.at[11])
    in_xt.start()

    in_x.wait()
    in_w.wait()
    y_part = lax.dot_general(
        x_v[...], w_ref[...], (((0,), (0,)), ((), ())), preferred_element_type=F32).astype(BF16)
    for q in range(2):
        for core in range(2):
            y_send[2 * q + core] = y_part[192 * q:192 * (q + 1), 128 * core:128 * (core + 1)].reshape(3, 64, 128)
    pl.semaphore_wait(barrier, len(peers))

    copies = []
    for k in range(1, 4):
        f2 = (f + k) % 4
        piece = ((f2 // 2 + h) % 2) * 2 + f2 % 2
        cp = remote(y_send.at[piece], y_recv.at[k - 1], p1_s.at[k - 1], p1_r.at[k - 1], feat_peers[k - 1])
        cp.start()
        copies.append(cp)
    for cp in in_keys:
        cp.wait()
    ids = lax.broadcasted_iota(jnp.int32, (slots, 128), 0)
    lanes = lax.broadcasted_iota(jnp.int32, (slots, 128), 1)
    live = ids < count_s[0, 0]
    for i in range(2):
        across = jnp.broadcast_to(keys_v[i], (slots, slots))
        across = jnp.concatenate([across, jnp.zeros((slots, 128 - slots), jnp.int32)], axis=1)
        down = jnp.sum(jnp.where(ids == lanes, across, 0), axis=1, keepdims=True)
        down = jnp.broadcast_to(down, (slots, 128))
        before = jnp.where(live & (ids < lanes) & (down == across), ids, -1)
        there = jnp.where(live & (down == lanes), ids, -1)
        for w, found in ((0, before), (1, there)):
            top = jnp.max(found, axis=0, keepdims=True)
            links_v[pl.ds(2 * i + w, 1), :] = jnp.where(top < 0, slots, top)
    links = pltpu.make_async_copy(links_v, links_s, in_sem.at[10])
    links.start()
    total = y_send[2 * a + b].astype(F32)
    for k in range(3):
        copies[k].wait_recv()
        total = total + y_recv[k].astype(F32)
    g = 2 * r + a
    y_buf[pl.ds(3 * g, 3)] = total.astype(BF16)

    p2 = []
    for k in range(1, n_g):
        _, dev = g_peer(k)
        cp = remote(y_buf.at[pl.ds(3 * g, 3)], y_buf.at[pl.ds(3 * g, 3)], p2_s.at[k - 1], p2_r.at[k - 1], dev)
        cp.start()
        p2.append(cp)
    prod_f[slots] = jnp.zeros((64, 128), F32)
    prod_b[slots] = jnp.zeros((128, 128), F32)
    in_t.wait()
    links.wait()
    for k in range(1, n_g):
        src = (g + n_g - k) % n_g
        remote(y_buf.at[pl.ds(3 * src, 3)], y_buf.at[pl.ds(3 * src, 3)], p2_s.at[k - 1], p2_r.at[k - 1],
               y_partner).wait_recv()

    xg = remote(feat_hbm, xt_both.at[y_low], xg_s.at[0], xg_r.at[0], {"feat": (f + 2) % 4})
    xg.start()

    def forward(s, _):
        block = y_buf[pl.ds(2 * cols_s[0, s], 2)].reshape(128, 128)
        prod_f[s] = jnp.dot(tiles_v[s], block, preferred_element_type=F32) + prod_f[links_s[0, s]]
        return 0

    lax.fori_loop(0, slots, forward, 0, unroll=32)

    def fill(c2):
        for w in range(3):
            s_buf[c2, w] = prod_f[links_s[1, 3 * c2 + w]].astype(BF16)

    offs = far_first(n_z) + [0]
    p3a = []
    for j, off in enumerate(offs):
        c2 = 2 * ((z + off) % n_z) + 1 - h
        fill(c2)
        cp = remote(s_buf.at[c2], yh_recv.at[j], p3a_s.at[j], p3a_r.at[j], y_partner)
        cp.start()
        p3a.append(cp)
    for j, off in enumerate(offs):
        fill(2 * ((z + off) % n_z) + h)
    p3b = []
    for j, off in enumerate(offs):
        c2 = 2 * ((z + off) % n_z) + h
        p3a[j].wait_recv()
        both = s_buf[c2].astype(F32) + yh_recv[j].astype(F32)
        if off:
            t_buf[j] = both.astype(BF16)
            cp = remote(t_buf.at[j], z_recv.at[j], p3b_s.at[j], p3b_r.at[j], z_peer(off))
            cp.start()
            p3b.append(cp)
        else:
            hidden = both
    for j in range(n_z - 1):
        p3b[j].wait_recv()
        hidden = hidden + z_recv[j].astype(F32)

    in_c.wait()
    sigma = jax.nn.sigmoid(hidden)
    grad = cot_v[...].astype(F32) * (sigma * (1.0 + hidden * (1.0 - sigma)))
    hg_buf[pl.ds(3 * c, 3)] = grad.astype(BF16)
    act_v[...] = (hidden * sigma).astype(BF16)

    own = hg_buf.at[pl.ds(3 * c, 3)]
    p4y = [remote(own, own, p4y_s.at[n_z - 1], p4y_r.at[n_z - 1], y_partner)]
    p4y[0].start()
    def z_got(dist):
        return hg_buf.at[pl.ds(3 * (2 * ((z + 2 * n_z - dist) % n_z) + h), 3)]

    p4z = []

    def z_send(what, j, off):
        cp = remote(what, what, p4z_s.at[j], p4z_r.at[j], z_peer(off))
        cp.start()
        p4z.append(cp)

    def arrived(j, dist):
        got = z_got(dist)
        remote(got, got, p4z_s.at[j], p4z_r.at[j], y_partner).wait_recv()
        return got

    def y_forward(got, j):
        cp = remote(got, got, p4y_s.at[j], p4y_r.at[j], y_partner)
        cp.start()
        p4y.append(cp)

    side = 1 - 2 * (z % 2)
    z_send(own, 2, 2)
    z_send(own, 3, n_z - 2)
    z_send(own, 0, 1)
    z_send(own, 1, n_z - 1)
    y_forward(arrived(0, 1), 0)
    y_forward(arrived(1, n_z - 1), 1)
    plus = arrived(2, 2)
    z_send(plus, 4, 1)
    minus = arrived(3, n_z - 2)
    z_send(minus, 5, n_z - 1)
    z_send(hg_buf.at[pl.ds(3 * (2 * ((z + n_z - 2 * side) % n_z) + h), 3)], 6, 2 * side + n_z)
    y_forward(plus, 2)
    y_forward(minus, 3)
    act_cols = pl.ds(pl.multiple_of(b * 128, 128), 128)
    act_dst = act_out.at[:, a, :, act_cols]
    local = pltpu.make_async_copy(act_v, act_dst, in_sem.at[3])
    local.start()
    acts = []
    for k in range(1, 4):
        cp = remote(act_v, act_dst, act_s.at[k - 1], act_r.at[k - 1], feat_peers[k - 1])
        cp.start()
        acts.append(cp)
    y_forward(arrived(4, 3), 4)
    y_forward(arrived(5, n_z - 3), 5)
    y_forward(arrived(6, 4), 6)
    for j, dist in enumerate([1, n_z - 1, 2, n_z - 2, 3, n_z - 3, 4, 0]):
        got = hg_buf.at[pl.ds(3 * (2 * ((z + n_z - dist) % n_z) + 1 - h), 3)]
        remote(got, got, p4y_s.at[j], p4y_r.at[j], y_partner).wait_recv()

    def backward(s, _):
        prod_b[s] = lax.dot_general(
            tiles_v[s], hg_buf[rows_s[0, s]], (((0,), (0,)), ((), ())), preferred_element_type=F32) + prod_b[links_s[2, s]]
        return 0

    lax.fori_loop(0, slots, backward, 0, unroll=32)

    for j in range(3 * n_row):
        b_both[b, pl.ds(2 * j, 2)] = prod_b[links_s[3, j]].astype(BF16).reshape(2, 64, 128)

    bc = remote(b_both.at[b], b_both.at[b], bc_s.at[0], bc_r.at[0], {"feat": f + 1 - 2 * b})
    bc.start()

    piece_rows = u_send.shape[2]
    in_xt.wait()
    xg.wait_recv()
    got = b_both.at[1 - b]
    remote(got, got, bc_s.at[0], bc_r.at[0], y_partner).wait_recv()
    both = jnp.concatenate([b_both[0].reshape(n_row * node_dev, 128), b_both[1].reshape(n_row * node_dev, 128)], axis=1)
    for low in range(2):
        part = jnp.dot(xt_both[low], both, preferred_element_type=F32).astype(BF16)
        for core in range(2):
            u_send[low, n_row * core:n_row * (core + 1)] = part[:, 128 * core:128 * (core + 1)].reshape(
                n_row, piece_rows, 128)
    u = 2 * r + h
    k1 = []
    for k in range(1, 2 * n_g):
        q2 = (n_g * y_low + u + k) % (2 * n_g)
        low2, u2 = q2 // n_g, q2 % n_g
        dev = {"feat": 2 * low2 + b, "row": u2 // 2, "col": 2 * z + u2 % 2}
        cp = remote(u_send.at[low2, u2], u_recv.at[k - 1], k1_s.at[k - 1], k1_r.at[k - 1], dev)
        cp.start()
        k1.append(cp)

    p5 = []
    for k in range(1, n_g):
        g2, dev = g_peer(k)
        cp = remote(b_both.at[b, pl.ds(3 * g2, 3)], b_recv.at[k - 1], p5_s.at[k - 1], p5_r.at[k - 1], dev)
        cp.start()
        p5.append(cp)

    total = u_send[y_low, u].astype(F32)
    for k in range(2 * n_g - 1):
        k1[k].wait_recv()
        total = total + u_recv[k].astype(F32)
    v_buf[z] = total.astype(BF16)
    k2 = []
    for j, off in enumerate(offs[:-1]):
        cp = remote(v_buf.at[z], v_buf.at[z], k2_s.at[j], k2_r.at[j], z_peer(off))
        cp.start()
        k2.append(cp)

    total = b_both[b, pl.ds(3 * g, 3)].astype(F32)
    for k in range(n_g - 1):
        p5[k].wait_recv()
        total = total + b_recv[k].astype(F32)
    b_full[2 * b + a] = total.astype(BF16)
    mine = b_full.at[2 * b + a]
    p6 = []
    for k in range(1, 4):
        cp = remote(mine, mine, p6_s.at[k - 1], p6_r.at[k - 1], feat_peers[k - 1])
        cp.start()
        p6.append(cp)

    for j, off in enumerate(offs[:-1]):
        got = v_buf.at[(z + n_z - off) % n_z]
        remote(got, got, k2_s.at[j], k2_r.at[j], y_partner).wait_recv()
    total = v_buf[0].astype(F32)
    for j in range(1, n_z):
        total = total + v_buf[j].astype(F32)
    wg_piece[...] = total * (1.0 / math.sqrt(total_nodes))

    def wg_place(piece):
        return wg_out.at[
            pl.ds(pl.multiple_of((piece % n_row) * piece_rows, piece_rows), piece_rows),
            pl.ds(pl.multiple_of((piece // n_row) * 128, 128), 128),
        ]

    local_wg = pltpu.make_async_copy(wg_piece, wg_place(u), in_sem.at[4])
    local_wg.start()
    k3 = []
    for k in range(1, n_g):
        _, dev = u_peer(k)
        cp = remote(wg_piece, wg_place(u), k3_s.at[k - 1], k3_r.at[k - 1], dev)
        cp.start()
        k3.append(cp)
    for k in range(1, 4):
        f2 = (f + 4 - k) % 4
        got = b_full.at[2 * (f2 % 2) + (f2 // 2 + h) % 2]
        remote(got, got, p6_s.at[k - 1], p6_r.at[k - 1], y_partner).wait_recv()
    grad_t = jnp.zeros((w_ref.shape[0], node_dev), F32)
    for core in range(2):
        grad_t = grad_t + lax.dot_general(
            w_ref[:, 128 * core:128 * (core + 1)], b_full[2 * core:2 * core + 2].reshape(node_dev, 128),
            (((1,), (1,)), ((), ())), preferred_element_type=F32)
    fg_out[...] = grad_t.astype(BF16)

    for k in range(1, n_g):
        got = wg_place((u + n_g - k) % n_g)
        remote(wg_piece, got, k3_s.at[k - 1], k3_r.at[k - 1], y_partner).wait_recv()
    for k in range(1, 4):
        f2 = (f + 4 - k) % 4
        got = act_out.at[:, (f2 // 2 + h) % 2, :, pl.ds(pl.multiple_of((f2 % 2) * 128, 128), 128)]
        remote(act_v, got, act_s.at[k - 1], act_r.at[k - 1], y_partner).wait_recv()
    local.wait()
    local_wg.wait()
    for cp in copies + p2 + p3a + p3b + p4y + p4z + acts + p5 + p6 + k1 + k2 + k3 + [xg, bc]:
        cp.wait_send()


def shards(n_row, n_z, features, weight, tile_values, tile_rows, tile_cols, tile_count, cotangent):
    slots = tile_values.shape[2]
    node_dev, out = cotangent.shape
    width = features.shape[1]
    n_g = 2 * n_row
    n_col = 2 * n_z
    piece_rows = 2 * width // n_g
    dma = pltpu.SemaphoreType.DMA
    pin = lambda x: pltpu.with_memory_space_constraint(x, pltpu.HBM)
    smem = pl.BlockSpec(memory_space=pltpu.SMEM)
    vmem = pl.BlockSpec(memory_space=pltpu.VMEM)
    hbm = pl.BlockSpec(memory_space=pltpu.HBM)
    sem_counts = [12, 3, 3, n_g - 1, n_g - 1, n_z, n_z, n_z - 1, n_z - 1, 3, 3, n_z - 1, n_z - 1, n_z, n_z,
                  1, 1, 1, 1, n_g - 1, n_g - 1, 3, 3, 2 * n_g - 1, 2 * n_g - 1, n_z - 1, n_z - 1, n_g - 1, n_g - 1]
    act, fg, wg = pl.pallas_call(
        functools.partial(kernel, n_row, n_z, slots, node_dev * n_row * n_col),
        out_shape=[
            jax.ShapeDtypeStruct((3, 2, 64, out), BF16),
            jax.ShapeDtypeStruct((width, node_dev), BF16),
            jax.ShapeDtypeStruct((width, out), F32),
        ],
        in_specs=[hbm, hbm, smem, hbm, hbm, hbm, hbm],
        out_specs=[vmem] * 3,
        scratch_shapes=[
            pltpu.SMEM((1, slots), jnp.int32),
            pltpu.SMEM((1, slots), jnp.int32),
            pltpu.VMEM((2, 1, slots), jnp.int32),
            pltpu.VMEM((8, 128), jnp.int32),
            pltpu.SMEM((8, 128), jnp.int32),
            pltpu.VMEM((width, node_dev), BF16),
            pltpu.VMEM((width, out), BF16),
            pltpu.VMEM((slots, 64, 128), BF16),
            pltpu.VMEM((3, 64, 128), BF16),
            pltpu.VMEM((4, 3, 64, 128), BF16),
            pltpu.VMEM((3, 3, 64, 128), BF16),
            pltpu.VMEM((3 * n_g, 64, 128), BF16),
            pltpu.VMEM((slots + 1, 64, 128), F32),
            pltpu.VMEM((n_col, 3, 64, 128), BF16),
            pltpu.VMEM((n_z, 3, 64, 128), BF16),
            pltpu.VMEM((n_z - 1, 3, 64, 128), BF16),
            pltpu.VMEM((n_z - 1, 3, 64, 128), BF16),
            pltpu.VMEM((3 * n_col, 64, 128), BF16),
            pltpu.VMEM((3, 64, 128), BF16),
            pltpu.VMEM((slots + 1, 128, 128), F32),
            pltpu.VMEM((2, 3 * n_g, 64, 128), BF16),
            pltpu.VMEM((n_g - 1, 3, 64, 128), BF16),
            pltpu.VMEM((4, 3, 64, 128), BF16),
            pltpu.VMEM((2, width, n_row * node_dev), BF16),
            pltpu.VMEM((2, n_g, piece_rows, 128), BF16),
            pltpu.VMEM((2 * n_g - 1, piece_rows, 128), BF16),
            pltpu.VMEM((n_z, piece_rows, 128), BF16),
            pltpu.VMEM((piece_rows, 128), F32),
        ] + [dma((n,)) for n in sem_counts],
        compiler_params=pltpu.CompilerParams(
            collective_id=0, has_side_effects=True, vmem_limit_bytes=40 * 1024 * 1024),
    )(
        pin(tile_rows.reshape(1, slots)), pin(tile_cols.reshape(1, slots)), tile_count,
        pin(features.T), pin(weight), pin(tile_values.reshape(slots, 2, 64, 128)), pin(cotangent.reshape(3, 2, 64, out)),
    )
    return act.reshape(node_dev, out), fg.T.reshape(1, node_dev, width), wg


def solution(mesh):
    return jax.shard_map(
        functools.partial(shards, mesh.shape["row"], mesh.shape["col"] // 2),
        mesh=mesh,
        in_specs=(
            P("col", "feat"),
            P("feat", None),
            P("row", "col", None, None, None),
            P("row", "col", None),
            P("row", "col", None),
            P("row", "col"),
            P(("row", "col"), None),
        ),
        out_specs=(P(("row", "col"), None), P("col", "row", "feat"), P("feat", None)),
        check_vma=False,
    )
```

```python
import functools
import math

import jax
import jax.numpy as jnp
from jax import lax
from jax.experimental import pallas as pl
from jax.experimental.pallas import tpu as pltpu
from jax.sharding import PartitionSpec as P

MESH = pl.DeviceIdType.MESH
F32 = jnp.float32
BF16 = jnp.bfloat16


def far_first(n):
    return sorted(range(1, n), key=lambda k: (-min(k, n - k), k))


def kernel(
    n_row, n_z, slots, total_nodes,
    rows_hbm, cols_hbm, count_s, feat_hbm, w_hbm, tiles_hbm, cot_hbm,
    act_out, fg_out, wg_out,
    rows_s, cols_s, keys_v, links_v, links_s,
    x_v, w_ref, tiles_v, cot_v,
    y_send, y_recv, y_buf, prod_f,
    s_buf, yh_recv, t_buf, z_recv, hg_buf, act_v,
    prod_b, b_both, b_recv, b_full,
    xt_both, u_send, u_recv, v_buf, wg_piece,
    in_sem, p1_s, p1_r, p2_s, p2_r, p3a_s, p3a_r, p3b_s, p3b_r,
    act_s, act_r, p4z_s, p4z_r, p4y_s, p4y_r, xg_s, xg_r, bc_s, bc_r, p5_s, p5_r, p6_s, p6_r,
    k1_s, k1_r, k2_s, k2_r, k3_s, k3_r,
):
    f = lax.axis_index("feat")
    r = lax.axis_index("row")
    c = lax.axis_index("col")
    y_low, b = f // 2, f % 2
    z, h = c // 2, c % 2
    a = (y_low + h) % 2
    n_g = 2 * n_row

    def feat_of(role, core):
        return ((role + h) % 2) * 2 + core

    def remote(src, dst, send, recv, device):
        return pltpu.make_async_remote_copy(
            src_ref=src, dst_ref=dst, send_sem=send, recv_sem=recv, device_id=device, device_id_type=MESH
        )

    feat_peers = [{"feat": (f + k) % 4} for k in range(1, 4)]

    def g_peer(k):
        g2 = (2 * r + a + k) % n_g
        return g2, {"feat": feat_of(g2 % 2, b), "row": g2 // 2}

    def u_peer(k):
        u2 = (2 * r + h + k) % n_g
        return u2, {"row": u2 // 2, "col": 2 * z + u2 % 2}

    def z_peer(k):
        return {"col": 2 * ((z + k) % n_z) + h}

    y_partner = {"feat": (f + 2) % 4, "col": c + 1 - 2 * h}

    node_dev = x_v.shape[1]
    in_x = pltpu.make_async_copy(
        feat_hbm.at[:, pl.ds(pl.multiple_of(r * node_dev, node_dev), node_dev)], x_v, in_sem.at[0])
    in_w = pltpu.make_async_copy(w_hbm, w_ref, in_sem.at[5])
    in_keys = [
        pltpu.make_async_copy(rows_hbm, keys_v.at[0], in_sem.at[6]),
        pltpu.make_async_copy(cols_hbm, keys_v.at[1], in_sem.at[7]),
        pltpu.make_async_copy(rows_hbm, rows_s, in_sem.at[8]),
        pltpu.make_async_copy(cols_hbm, cols_s, in_sem.at[9]),
    ]
    in_t = pltpu.make_async_copy(tiles_hbm.at[:, a], tiles_v, in_sem.at[1])
    in_c = pltpu.make_async_copy(
        cot_hbm.at[:, a, :, pl.ds(pl.multiple_of(b * 128, 128), 128)], cot_v, in_sem.at[2])
    in_x.start()
    in_w.start()

    barrier = pltpu.get_barrier_semaphore()
    peers = list(feat_peers)
    for k in range(1, n_row):
        peers.append({"row": (r + k) % n_row})
        peers.append({"feat": (f + 2) % 4, "row": (r + k) % n_row})
    peers += [z_peer(k) for k in range(1, n_z)]
    peers.append(y_partner)
    peers += [{"row": (r + k) % n_row, "col": c + 1 - 2 * h} for k in range(n_row)]
    peers += [{"feat": (f + 2) % 4, "row": (r + k) % n_row, "col": c + 1 - 2 * h} for k in range(1, n_row)]
    for peer in reversed(peers):
        pl.semaphore_signal(barrier, inc=1, device_id=peer, device_id_type=MESH)
    for cp in in_keys:
        cp.start()
    in_t.start()
    in_c.start()
    in_xt = pltpu.make_async_copy(feat_hbm, xt_both.at[y_low], in_sem.at[11])
    in_xt.start()

    in_x.wait()
    in_w.wait()
    y_part = lax.dot_general(
        x_v[...], w_ref[...], (((0,), (0,)), ((), ())), preferred_element_type=F32).astype(BF16)
    for q in range(2):
        for core in range(2):
            y_send[2 * q + core] = y_part[192 * q:192 * (q + 1), 128 * core:128 * (core + 1)].reshape(3, 64, 128)
    pl.semaphore_wait(barrier, len(peers))

    copies = []
    p1 = [[], [], []]
    for w in range(3):
        for k in range(1, 4):
            f2 = (f + k) % 4
            piece = ((f2 // 2 + h) % 2) * 2 + f2 % 2
            cp = remote(y_send.at[piece, w], y_recv.at[k - 1, w], p1_s.at[k - 1, w], p1_r.at[k - 1, w], feat_peers[k - 1])
            cp.start()
            copies.append(cp)
            p1[w].append(cp)
    for cp in in_keys:
        cp.wait()
    ids = lax.broadcasted_iota(jnp.int32, (slots, 128), 0)
    lanes = lax.broadcasted_iota(jnp.int32, (slots, 128), 1)
    live = ids < count_s[0, 0]
    for i in range(2):
        across = jnp.broadcast_to(keys_v[i], (slots, slots))
        across = jnp.concatenate([across, jnp.zeros((slots, 128 - slots), jnp.int32)], axis=1)
        down = jnp.sum(jnp.where(ids == lanes, across, 0), axis=1, keepdims=True)
        down = jnp.broadcast_to(down, (slots, 128))
        before = jnp.where(live & (ids < lanes) & (down == across), ids, -1)
        there = jnp.where(live & (down == lanes), ids, -1)
        for w, found in ((0, before), (1, there)):
            top = jnp.max(found, axis=0, keepdims=True)
            links_v[pl.ds(2 * i + w, 1), :] = jnp.where(top < 0, slots, top)
    links = pltpu.make_async_copy(links_v, links_s, in_sem.at[10])
    links.start()
    g = 2 * r + a
    p2 = []
    for w in range(3):
        total = y_send[2 * a + b, w].astype(F32)
        for k in range(3):
            p1[w][k].wait_recv()
            total = total + y_recv[k, w].astype(F32)
        y_buf[3 * g + w] = total.astype(BF16)
        mine = y_buf.at[3 * g + w]
        for k in range(1, n_g):
            _, dev = g_peer(k)
            cp = remote(mine, mine, p2_s.at[k - 1, w], p2_r.at[k - 1, w], dev)
            cp.start()
            p2.append(cp)
    prod_f[slots] = jnp.zeros((64, 128), F32)
    prod_b[slots] = jnp.zeros((128, 128), F32)
    in_t.wait()
    links.wait()
    for w in range(3):
        for k in range(1, n_g):
            got = y_buf.at[3 * ((g + n_g - k) % n_g) + w]
            remote(got, got, p2_s.at[k - 1, w], p2_r.at[k - 1, w], y_partner).wait_recv()

    xg = remote(feat_hbm, xt_both.at[y_low], xg_s.at[0], xg_r.at[0], {"feat": (f + 2) % 4})
    xg.start()

    def forward(s, _):
        block = y_buf[pl.ds(2 * cols_s[0, s], 2)].reshape(128, 128)
        prod_f[s] = jnp.dot(tiles_v[s], block, preferred_element_type=F32) + prod_f[links_s[0, s]]
        return 0

    lax.fori_loop(0, slots, forward, 0, unroll=32)

    def fill(c2, w):
        s_buf[c2, w] = prod_f[links_s[1, 3 * c2 + w]].astype(BF16)

    sent = []

    def send(src, dst, send_sem, recv_sem, device):
        cp = remote(src, dst, send_sem, recv_sem, device)
        cp.start()
        sent.append(cp)
        return cp

    offs = far_first(n_z) + [0]
    p3a = [[], [], []]
    for w in range(3):
        for j, off in enumerate(offs):
            c2 = 2 * ((z + off) % n_z) + 1 - h
            fill(c2, w)
            p3a[w].append(send(s_buf.at[c2, w], yh_recv.at[j, w], p3a_s.at[j, w], p3a_r.at[j, w], y_partner))
    for w in range(3):
        for off in offs:
            fill(2 * ((z + off) % n_z) + h, w)
    p3b = [[], [], []]
    own_part = [None] * 3

    def sum_h(w):
        for j, off in enumerate(offs):
            c2 = 2 * ((z + off) % n_z) + h
            p3a[w][j].wait_recv()
            both = s_buf[c2, w].astype(F32) + yh_recv[j, w].astype(F32)
            if off:
                t_buf[j, w] = both.astype(BF16)
                p3b[w].append(send(t_buf.at[j, w], z_recv.at[j, w], p3b_s.at[j, w], p3b_r.at[j, w], z_peer(off)))
            else:
                own_part[w] = both

    def place(dist, w):
        return hg_buf.at[3 * (2 * ((z + 2 * n_z - dist) % n_z) + h) + w]

    def z_send(what, j, off, w):
        send(what, what, p4z_s.at[j, w], p4z_r.at[j, w], z_peer(off))

    def y_send_on(what, j, w):
        send(what, what, p4y_s.at[j, w], p4y_r.at[j, w], y_partner)

    def arrived(j, dist, w):
        got = place(dist, w)
        remote(got, got, p4z_s.at[j, w], p4z_r.at[j, w], y_partner).wait_recv()
        return got

    def activate(w):
        hidden = own_part[w]
        for j in range(n_z - 1):
            p3b[w][j].wait_recv()
            hidden = hidden + z_recv[j, w].astype(F32)
        sigma = jax.nn.sigmoid(hidden)
        grad = cot_v[w].astype(F32) * (sigma * (1.0 + hidden * (1.0 - sigma)))
        hg_buf[3 * c + w] = grad.astype(BF16)
        act_v[w] = (hidden * sigma).astype(BF16)
        own = hg_buf.at[3 * c + w]
        if w == 2:
            z_send(own, 6, 4, w)
            z_send(own, 4, 3, w)
            z_send(own, 5, n_z - 3, w)
        z_send(own, 2, 2, w)
        z_send(own, 3, n_z - 2, w)
        z_send(own, 0, 1, w)
        z_send(own, 1, n_z - 1, w)
        y_send_on(own, n_z - 1, w)

    side = 1 - 2 * (z % 2)

    def pass_on(w):
        if w < 2:
            plus = arrived(2, 2, w)
            z_send(plus, 4, 1, w)
            minus = arrived(3, n_z - 2, w)
            z_send(minus, 5, n_z - 1, w)
            z_send(place(2 * side + n_z, w), 6, 2 * side + n_z, w)
        y_send_on(arrived(0, 1, w), 0, w)
        y_send_on(arrived(1, n_z - 1, w), 1, w)
        if w == 2:
            plus = arrived(2, 2, w)
            minus = arrived(3, n_z - 2, w)
        y_send_on(plus, 2, w)
        y_send_on(minus, 3, w)

    def last_on(w):
        y_send_on(arrived(4, 3, w), 4, w)
        y_send_on(arrived(5, n_z - 3, w), 5, w)
        y_send_on(arrived(6, 4, w), 6, w)

    sum_h(0)
    sum_h(1)
    sum_h(2)
    in_c.wait()
    activate(0)
    activate(1)
    pass_on(0)
    activate(2)
    act_cols = pl.ds(pl.multiple_of(b * 128, 128), 128)
    act_dst = act_out.at[:, a, :, act_cols]
    local = pltpu.make_async_copy(act_v, act_dst, in_sem.at[3])
    local.start()
    pass_on(1)
    last_on(0)
    pass_on(2)
    acts = []
    for k in range(1, 4):
        cp = remote(act_v, act_dst, act_s.at[k - 1], act_r.at[k - 1], feat_peers[k - 1])
        cp.start()
        acts.append(cp)
    last_on(1)
    last_on(2)
    for w in range(3):
        for j, dist in enumerate([1, n_z - 1, 2, n_z - 2, 3, n_z - 3, 4, 0]):
            got = hg_buf.at[3 * (2 * ((z + n_z - dist) % n_z) + 1 - h) + w]
            remote(got, got, p4y_s.at[j, w], p4y_r.at[j, w], y_partner).wait_recv()

    def backward(s, _):
        prod_b[s] = lax.dot_general(
            tiles_v[s], hg_buf[rows_s[0, s]], (((0,), (0,)), ((), ())), preferred_element_type=F32) + prod_b[links_s[2, s]]
        return 0

    lax.fori_loop(0, slots, backward, 0, unroll=32)

    for j in range(3 * n_row):
        b_both[b, pl.ds(2 * j, 2)] = prod_b[links_s[3, j]].astype(BF16).reshape(2, 64, 128)

    bc = remote(b_both.at[b], b_both.at[b], bc_s.at[0], bc_r.at[0], {"feat": f + 1 - 2 * b})
    bc.start()

    piece_rows = u_send.shape[2]
    in_xt.wait()
    xg.wait_recv()
    got = b_both.at[1 - b]
    remote(got, got, bc_s.at[0], bc_r.at[0], y_partner).wait_recv()
    both = jnp.concatenate([b_both[0].reshape(n_row * node_dev, 128), b_both[1].reshape(n_row * node_dev, 128)], axis=1)
    for low in range(2):
        part = jnp.dot(xt_both[low], both, preferred_element_type=F32).astype(BF16)
        for core in range(2):
            u_send[low, n_row * core:n_row * (core + 1)] = part[:, 128 * core:128 * (core + 1)].reshape(
                n_row, piece_rows, 128)
    u = 2 * r + h
    k1 = []
    for k in range(1, 2 * n_g):
        q2 = (n_g * y_low + u + k) % (2 * n_g)
        low2, u2 = q2 // n_g, q2 % n_g
        dev = {"feat": 2 * low2 + b, "row": u2 // 2, "col": 2 * z + u2 % 2}
        cp = remote(u_send.at[low2, u2], u_recv.at[k - 1], k1_s.at[k - 1], k1_r.at[k - 1], dev)
        cp.start()
        k1.append(cp)

    p5 = []
    for k in range(1, n_g):
        g2, dev = g_peer(k)
        cp = remote(b_both.at[b, pl.ds(3 * g2, 3)], b_recv.at[k - 1], p5_s.at[k - 1], p5_r.at[k - 1], dev)
        cp.start()
        p5.append(cp)

    total = u_send[y_low, u].astype(F32)
    for k in range(2 * n_g - 1):
        k1[k].wait_recv()
        total = total + u_recv[k].astype(F32)
    v_buf[z] = total.astype(BF16)
    k2 = []
    for j, off in enumerate(offs[:-1]):
        cp = remote(v_buf.at[z], v_buf.at[z], k2_s.at[j], k2_r.at[j], z_peer(off))
        cp.start()
        k2.append(cp)

    total = b_both[b, pl.ds(3 * g, 3)].astype(F32)
    for k in range(n_g - 1):
        p5[k].wait_recv()
        total = total + b_recv[k].astype(F32)
    b_full[2 * b + a] = total.astype(BF16)
    mine = b_full.at[2 * b + a]
    p6 = []
    for k in range(1, 4):
        cp = remote(mine, mine, p6_s.at[k - 1], p6_r.at[k - 1], feat_peers[k - 1])
        cp.start()
        p6.append(cp)

    for j, off in enumerate(offs[:-1]):
        got = v_buf.at[(z + n_z - off) % n_z]
        remote(got, got, k2_s.at[j], k2_r.at[j], y_partner).wait_recv()
    total = v_buf[0].astype(F32)
    for j in range(1, n_z):
        total = total + v_buf[j].astype(F32)
    wg_piece[...] = total * (1.0 / math.sqrt(total_nodes))

    def wg_place(piece):
        return wg_out.at[
            pl.ds(pl.multiple_of((piece % n_row) * piece_rows, piece_rows), piece_rows),
            pl.ds(pl.multiple_of((piece // n_row) * 128, 128), 128),
        ]

    local_wg = pltpu.make_async_copy(wg_piece, wg_place(u), in_sem.at[4])
    local_wg.start()
    k3 = []
    for k in range(1, n_g):
        _, dev = u_peer(k)
        cp = remote(wg_piece, wg_place(u), k3_s.at[k - 1], k3_r.at[k - 1], dev)
        cp.start()
        k3.append(cp)
    for k in range(1, 4):
        f2 = (f + 4 - k) % 4
        got = b_full.at[2 * (f2 % 2) + (f2 // 2 + h) % 2]
        remote(got, got, p6_s.at[k - 1], p6_r.at[k - 1], y_partner).wait_recv()
    grad_t = jnp.zeros((w_ref.shape[0], node_dev), F32)
    for core in range(2):
        grad_t = grad_t + lax.dot_general(
            w_ref[:, 128 * core:128 * (core + 1)], b_full[2 * core:2 * core + 2].reshape(node_dev, 128),
            (((1,), (1,)), ((), ())), preferred_element_type=F32)
    fg_out[...] = grad_t.astype(BF16)

    for k in range(1, n_g):
        got = wg_place((u + n_g - k) % n_g)
        remote(wg_piece, got, k3_s.at[k - 1], k3_r.at[k - 1], y_partner).wait_recv()
    for k in range(1, 4):
        f2 = (f + 4 - k) % 4
        got = act_out.at[:, (f2 // 2 + h) % 2, :, pl.ds(pl.multiple_of((f2 % 2) * 128, 128), 128)]
        remote(act_v, got, act_s.at[k - 1], act_r.at[k - 1], y_partner).wait_recv()
    local.wait()
    local_wg.wait()
    for cp in copies + p2 + sent + acts + p5 + p6 + k1 + k2 + k3 + [xg, bc]:
        cp.wait_send()


def shards(n_row, n_z, features, weight, tile_values, tile_rows, tile_cols, tile_count, cotangent):
    slots = tile_values.shape[2]
    node_dev, out = cotangent.shape
    width = features.shape[1]
    n_g = 2 * n_row
    n_col = 2 * n_z
    piece_rows = 2 * width // n_g
    dma = pltpu.SemaphoreType.DMA
    pin = lambda x: pltpu.with_memory_space_constraint(x, pltpu.HBM)
    smem = pl.BlockSpec(memory_space=pltpu.SMEM)
    vmem = pl.BlockSpec(memory_space=pltpu.VMEM)
    hbm = pl.BlockSpec(memory_space=pltpu.HBM)
    sem_counts = [12, (3, 3), (3, 3), (n_g - 1, 3), (n_g - 1, 3), (n_z, 3), (n_z, 3), (n_z - 1, 3), (n_z - 1, 3),
                  3, 3, (n_z - 1, 3), (n_z - 1, 3), (n_z, 3), (n_z, 3),
                  1, 1, 1, 1, n_g - 1, n_g - 1, 3, 3, 2 * n_g - 1, 2 * n_g - 1, n_z - 1, n_z - 1, n_g - 1, n_g - 1]
    act, fg, wg = pl.pallas_call(
        functools.partial(kernel, n_row, n_z, slots, node_dev * n_row * n_col),
        out_shape=[
            jax.ShapeDtypeStruct((3, 2, 64, out), BF16),
            jax.ShapeDtypeStruct((width, node_dev), BF16),
            jax.ShapeDtypeStruct((width, out), F32),
        ],
        in_specs=[hbm, hbm, smem, hbm, hbm, hbm, hbm],
        out_specs=[vmem] * 3,
        scratch_shapes=[
            pltpu.SMEM((1, slots), jnp.int32),
            pltpu.SMEM((1, slots), jnp.int32),
            pltpu.VMEM((2, 1, slots), jnp.int32),
            pltpu.VMEM((8, 128), jnp.int32),
            pltpu.SMEM((8, 128), jnp.int32),
            pltpu.VMEM((width, node_dev), BF16),
            pltpu.VMEM((width, out), BF16),
            pltpu.VMEM((slots, 64, 128), BF16),
            pltpu.VMEM((3, 64, 128), BF16),
            pltpu.VMEM((4, 3, 64, 128), BF16),
            pltpu.VMEM((3, 3, 64, 128), BF16),
            pltpu.VMEM((3 * n_g, 64, 128), BF16),
            pltpu.VMEM((slots + 1, 64, 128), F32),
            pltpu.VMEM((n_col, 3, 64, 128), BF16),
            pltpu.VMEM((n_z, 3, 64, 128), BF16),
            pltpu.VMEM((n_z - 1, 3, 64, 128), BF16),
            pltpu.VMEM((n_z - 1, 3, 64, 128), BF16),
            pltpu.VMEM((3 * n_col, 64, 128), BF16),
            pltpu.VMEM((3, 64, 128), BF16),
            pltpu.VMEM((slots + 1, 128, 128), F32),
            pltpu.VMEM((2, 3 * n_g, 64, 128), BF16),
            pltpu.VMEM((n_g - 1, 3, 64, 128), BF16),
            pltpu.VMEM((4, 3, 64, 128), BF16),
            pltpu.VMEM((2, width, n_row * node_dev), BF16),
            pltpu.VMEM((2, n_g, piece_rows, 128), BF16),
            pltpu.VMEM((2 * n_g - 1, piece_rows, 128), BF16),
            pltpu.VMEM((n_z, piece_rows, 128), BF16),
            pltpu.VMEM((piece_rows, 128), F32),
        ] + [dma(n if isinstance(n, tuple) else (n,)) for n in sem_counts],
        compiler_params=pltpu.CompilerParams(
            collective_id=0, has_side_effects=True, vmem_limit_bytes=40 * 1024 * 1024),
    )(
        pin(tile_rows.reshape(1, slots)), pin(tile_cols.reshape(1, slots)), tile_count,
        pin(features.T), pin(weight), pin(tile_values.reshape(slots, 2, 64, 128)), pin(cotangent.reshape(3, 2, 64, out)),
    )
    return act.reshape(node_dev, out), fg.T.reshape(1, node_dev, width), wg


def solution(mesh):
    return jax.shard_map(
        functools.partial(shards, mesh.shape["row"], mesh.shape["col"] // 2),
        mesh=mesh,
        in_specs=(
            P("col", "feat"),
            P("feat", None),
            P("row", "col", None, None, None),
            P("row", "col", None),
            P("row", "col", None),
            P("row", "col"),
            P(("row", "col"), None),
        ),
        out_specs=(P(("row", "col"), None), P("col", "row", "feat"), P("feat", None)),
        check_vma=False,
    )
```

```python
import functools
import math

import jax
import jax.numpy as jnp
from jax import lax
from jax.experimental import pallas as pl
from jax.experimental.pallas import tpu as pltpu
from jax.sharding import PartitionSpec as P

MESH = pl.DeviceIdType.MESH
F32 = jnp.float32
BF16 = jnp.bfloat16


def far_first(n):
    return sorted(range(1, n), key=lambda k: (-min(k, n - k), k))


def kernel(
    n_row, n_z, slots, total_nodes,
    rows_hbm, cols_hbm, count_s, feat_hbm, w_hbm, tiles_hbm, cot_hbm,
    act_out, fg_out, wg_out,
    rows_s, cols_s, keys_v, links_v, links_s,
    x_v, w_ref, tiles_v, cot_v,
    y_send, y_recv, y_buf, prod_f,
    s_buf, yh_recv, t_buf, z_recv, hg_buf, act_v,
    prod_b, b_both, b_recv, b_full,
    xt_both, u_send, u_recv, v_buf, wg_piece,
    here_sem, in_sem, p1_s, p1_r, p2_s, p2_r, p3a_s, p3a_r, p3b_s, p3b_r,
    act_s, act_r, p4z_s, p4z_r, p4y_s, p4y_r, xg_s, xg_r, bc_s, bc_r, p5_s, p5_r, p6_s, p6_r,
    k1_s, k1_r, k2_s, k2_r, k3_s, k3_r,
):
    f = lax.axis_index("feat")
    r = lax.axis_index("row")
    c = lax.axis_index("col")
    y_low, b = f // 2, f % 2
    z, h = c // 2, c % 2
    a = (y_low + h) % 2
    n_g = 2 * n_row

    def feat_of(role, core):
        return ((role + h) % 2) * 2 + core

    def remote(src, dst, send, recv, device):
        return pltpu.make_async_remote_copy(
            src_ref=src, dst_ref=dst, send_sem=send, recv_sem=recv, device_id=device, device_id_type=MESH
        )

    feat_peers = [{"feat": (f + k) % 4} for k in range(1, 4)]

    def g_peer(k):
        g2 = (2 * r + a + k) % n_g
        return g2, {"feat": feat_of(g2 % 2, b), "row": g2 // 2}

    def u_peer(k):
        u2 = (2 * r + h + k) % n_g
        return u2, {"row": u2 // 2, "col": 2 * z + u2 % 2}

    def z_peer(k):
        return {"col": 2 * ((z + k) % n_z) + h}

    y_partner = {"feat": (f + 2) % 4, "col": c + 1 - 2 * h}

    node_dev = x_v.shape[1]
    in_x = pltpu.make_async_copy(
        feat_hbm.at[:, pl.ds(pl.multiple_of(r * node_dev, node_dev), node_dev)], x_v, in_sem.at[0])
    in_w = pltpu.make_async_copy(w_hbm, w_ref, in_sem.at[5])
    in_keys = [
        pltpu.make_async_copy(rows_hbm, keys_v.at[0], in_sem.at[6]),
        pltpu.make_async_copy(cols_hbm, keys_v.at[1], in_sem.at[7]),
        pltpu.make_async_copy(rows_hbm, rows_s, in_sem.at[8]),
        pltpu.make_async_copy(cols_hbm, cols_s, in_sem.at[9]),
    ]
    in_t = pltpu.make_async_copy(tiles_hbm.at[:, a], tiles_v, in_sem.at[1])
    in_c = pltpu.make_async_copy(
        cot_hbm.at[:, a, :, pl.ds(pl.multiple_of(b * 128, 128), 128)], cot_v, in_sem.at[2])
    in_x.start()
    in_w.start()

    barrier = pltpu.get_barrier_semaphore()
    peers = list(feat_peers)
    for k in range(1, n_row):
        peers.append({"row": (r + k) % n_row})
        peers.append({"feat": (f + 2) % 4, "row": (r + k) % n_row})
    peers += [z_peer(k) for k in (1, n_z - 1)]
    peers.append(y_partner)
    for peer in reversed(peers):
        pl.semaphore_signal(barrier, inc=1, device_id=peer, device_id_type=MESH)
    for cp in in_keys:
        cp.start()
    in_t.start()
    in_c.start()
    in_xt = pltpu.make_async_copy(feat_hbm, xt_both.at[y_low], in_sem.at[11])
    in_xt.start()

    in_x.wait()
    in_w.wait()
    y_part = lax.dot_general(
        x_v[...], w_ref[...], (((0,), (0,)), ((), ())), preferred_element_type=F32).astype(BF16)
    for q in range(2):
        for core in range(2):
            y_send[2 * q + core] = y_part[192 * q:192 * (q + 1), 128 * core:128 * (core + 1)].reshape(3, 64, 128)
    pl.semaphore_wait(barrier, len(peers))
    for k in (1, n_z - 1):
        pl.semaphore_signal(here_sem.at[0], inc=1, device_id=z_peer(k), device_id_type=MESH)

    copies = []
    p1 = [[], [], []]
    for w in range(3):
        for k in range(1, 4):
            f2 = (f + k) % 4
            piece = ((f2 // 2 + h) % 2) * 2 + f2 % 2
            cp = remote(y_send.at[piece, w], y_recv.at[k - 1, w], p1_s.at[k - 1, w], p1_r.at[k - 1, w], feat_peers[k - 1])
            cp.start()
            copies.append(cp)
            p1[w].append(cp)
    for cp in in_keys:
        cp.wait()
    ids = lax.broadcasted_iota(jnp.int32, (slots, 128), 0)
    lanes = lax.broadcasted_iota(jnp.int32, (slots, 128), 1)
    live = ids < count_s[0, 0]
    for i in range(2):
        across = jnp.broadcast_to(keys_v[i], (slots, slots))
        across = jnp.concatenate([across, jnp.zeros((slots, 128 - slots), jnp.int32)], axis=1)
        down = jnp.sum(jnp.where(ids == lanes, across, 0), axis=1, keepdims=True)
        down = jnp.broadcast_to(down, (slots, 128))
        before = jnp.where(live & (ids < lanes) & (down == across), ids, -1)
        there = jnp.where(live & (down == lanes), ids, -1)
        for w, found in ((0, before), (1, there)):
            top = jnp.max(found, axis=0, keepdims=True)
            links_v[pl.ds(2 * i + w, 1), :] = jnp.where(top < 0, slots, top)
    links = pltpu.make_async_copy(links_v, links_s, in_sem.at[10])
    links.start()
    pl.semaphore_wait(here_sem.at[0], 2)
    for k in (2, n_z - 2):
        pl.semaphore_signal(here_sem.at[1], inc=1, device_id=z_peer(k), device_id_type=MESH)

    g = 2 * r + a
    p2 = []
    for w in range(3):
        total = y_send[2 * a + b, w].astype(F32)
        for k in range(3):
            p1[w][k].wait_recv()
            total = total + y_recv[k, w].astype(F32)
        y_buf[3 * g + w] = total.astype(BF16)
        mine = y_buf.at[3 * g + w]
        for k in range(1, n_g):
            _, dev = g_peer(k)
            cp = remote(mine, mine, p2_s.at[k - 1, w], p2_r.at[k - 1, w], dev)
            cp.start()
            p2.append(cp)
    prod_f[slots] = jnp.zeros((64, 128), F32)
    prod_b[slots] = jnp.zeros((128, 128), F32)
    in_t.wait()
    links.wait()
    for w in range(3):
        for k in range(1, n_g):
            got = y_buf.at[3 * ((g + n_g - k) % n_g) + w]
            remote(got, got, p2_s.at[k - 1, w], p2_r.at[k - 1, w], y_partner).wait_recv()

    pl.semaphore_wait(here_sem.at[1], 2)

    xg = remote(feat_hbm, xt_both.at[y_low], xg_s.at[0], xg_r.at[0], {"feat": (f + 2) % 4})
    xg.start()

    def forward(s, _):
        block = y_buf[pl.ds(2 * cols_s[0, s], 2)].reshape(128, 128)
        prod_f[s] = jnp.dot(tiles_v[s], block, preferred_element_type=F32) + prod_f[links_s[0, s]]
        return 0

    lax.fori_loop(0, slots, forward, 0, unroll=32)

    def fill(c2, w):
        s_buf[c2, w] = prod_f[links_s[1, 3 * c2 + w]].astype(BF16)

    sent = []

    def send(src, dst, send_sem, recv_sem, device):
        cp = remote(src, dst, send_sem, recv_sem, device)
        cp.start()
        sent.append(cp)
        return cp

    offs = far_first(n_z) + [0]
    p3a = [[], [], []]
    for w in range(3):
        for j, off in enumerate(offs):
            c2 = 2 * ((z + off) % n_z) + 1 - h
            fill(c2, w)
            p3a[w].append(send(s_buf.at[c2, w], yh_recv.at[j, w], p3a_s.at[j, w], p3a_r.at[j, w], y_partner))
    for w in range(3):
        for off in offs:
            fill(2 * ((z + off) % n_z) + h, w)
    p3b = [[], [], []]
    own_part = [None] * 3

    def sum_h(w):
        for j, off in enumerate(offs):
            c2 = 2 * ((z + off) % n_z) + h
            p3a[w][j].wait_recv()
            both = s_buf[c2, w].astype(F32) + yh_recv[j, w].astype(F32)
            if off:
                t_buf[j, w] = both.astype(BF16)
                p3b[w].append(send(t_buf.at[j, w], z_recv.at[j, w], p3b_s.at[j, w], p3b_r.at[j, w], z_peer(off)))
            else:
                own_part[w] = both

    def place(dist, w):
        return hg_buf.at[3 * (2 * ((z + 2 * n_z - dist) % n_z) + h) + w]

    def z_send(what, j, off, w):
        send(what, what, p4z_s.at[j, w], p4z_r.at[j, w], z_peer(off))

    def y_send_on(what, j, w):
        send(what, what, p4y_s.at[j, w], p4y_r.at[j, w], y_partner)

    def arrived(j, dist, w):
        got = place(dist, w)
        remote(got, got, p4z_s.at[j, w], p4z_r.at[j, w], y_partner).wait_recv()
        return got

    def activate(w):
        hidden = own_part[w]
        for j in range(n_z - 1):
            p3b[w][j].wait_recv()
            hidden = hidden + z_recv[j, w].astype(F32)
        sigma = jax.nn.sigmoid(hidden)
        grad = cot_v[w].astype(F32) * (sigma * (1.0 + hidden * (1.0 - sigma)))
        hg_buf[3 * c + w] = grad.astype(BF16)
        act_v[w] = (hidden * sigma).astype(BF16)
        own = hg_buf.at[3 * c + w]
        if w == 2:
            z_send(own, 6, 4, w)
            z_send(own, 4, 3, w)
            z_send(own, 5, n_z - 3, w)
        z_send(own, 2, 2, w)
        z_send(own, 3, n_z - 2, w)
        z_send(own, 0, 1, w)
        z_send(own, 1, n_z - 1, w)
        y_send_on(own, n_z - 1, w)

    side = 1 - 2 * (z % 2)

    def pass_on(w):
        if w < 2:
            plus = arrived(2, 2, w)
            z_send(plus, 4, 1, w)
            minus = arrived(3, n_z - 2, w)
            z_send(minus, 5, n_z - 1, w)
            z_send(place(2 * side + n_z, w), 6, 2 * side + n_z, w)
        y_send_on(arrived(0, 1, w), 0, w)
        y_send_on(arrived(1, n_z - 1, w), 1, w)
        if w == 2:
            plus = arrived(2, 2, w)
            minus = arrived(3, n_z - 2, w)
        y_send_on(plus, 2, w)
        y_send_on(minus, 3, w)

    def last_on(w):
        y_send_on(arrived(4, 3, w), 4, w)
        y_send_on(arrived(5, n_z - 3, w), 5, w)
        y_send_on(arrived(6, 4, w), 6, w)

    in_c.wait()
    sum_h(0)
    sum_h(1)
    activate(0)
    sum_h(2)
    activate(1)
    pass_on(0)
    activate(2)
    act_cols = pl.ds(pl.multiple_of(b * 128, 128), 128)
    act_dst = act_out.at[:, a, :, act_cols]
    local = pltpu.make_async_copy(act_v, act_dst, in_sem.at[3])
    local.start()
    pass_on(1)
    last_on(0)
    pass_on(2)
    acts = []
    for k in range(1, 4):
        cp = remote(act_v, act_dst, act_s.at[k - 1], act_r.at[k - 1], feat_peers[k - 1])
        cp.start()
        acts.append(cp)
    last_on(1)
    last_on(2)
    for w in range(3):
        for j, dist in enumerate([1, n_z - 1, 2, n_z - 2, 3, n_z - 3, 4, 0]):
            got = hg_buf.at[3 * (2 * ((z + n_z - dist) % n_z) + 1 - h) + w]
            remote(got, got, p4y_s.at[j, w], p4y_r.at[j, w], y_partner).wait_recv()

    def backward(s, _):
        prod_b[s] = lax.dot_general(
            tiles_v[s], hg_buf[rows_s[0, s]], (((0,), (0,)), ((), ())), preferred_element_type=F32) + prod_b[links_s[2, s]]
        return 0

    lax.fori_loop(0, slots, backward, 0, unroll=32)

    for j in range(3 * n_row):
        b_both[b, pl.ds(2 * j, 2)] = prod_b[links_s[3, j]].astype(BF16).reshape(2, 64, 128)

    bc = remote(b_both.at[b], b_both.at[b], bc_s.at[0], bc_r.at[0], {"feat": f + 1 - 2 * b})
    bc.start()

    piece_rows = u_send.shape[2]
    in_xt.wait()
    xg.wait_recv()
    got = b_both.at[1 - b]
    remote(got, got, bc_s.at[0], bc_r.at[0], y_partner).wait_recv()
    both = jnp.concatenate([b_both[0].reshape(n_row * node_dev, 128), b_both[1].reshape(n_row * node_dev, 128)], axis=1)
    for low in range(2):
        part = jnp.dot(xt_both[low], both, preferred_element_type=F32).astype(BF16)
        for core in range(2):
            u_send[low, n_row * core:n_row * (core + 1)] = part[:, 128 * core:128 * (core + 1)].reshape(
                n_row, piece_rows, 128)
    u = 2 * r + h
    k1 = []
    for k in range(1, 2 * n_g):
        q2 = (n_g * y_low + u + k) % (2 * n_g)
        low2, u2 = q2 // n_g, q2 % n_g
        dev = {"feat": 2 * low2 + b, "row": u2 // 2, "col": 2 * z + u2 % 2}
        cp = remote(u_send.at[low2, u2], u_recv.at[k - 1], k1_s.at[k - 1], k1_r.at[k - 1], dev)
        cp.start()
        k1.append(cp)

    p5 = []
    for k in range(1, n_g):
        g2, dev = g_peer(k)
        cp = remote(b_both.at[b, pl.ds(3 * g2, 3)], b_recv.at[k - 1], p5_s.at[k - 1], p5_r.at[k - 1], dev)
        cp.start()
        p5.append(cp)

    total = u_send[y_low, u].astype(F32)
    for k in range(2 * n_g - 1):
        k1[k].wait_recv()
        total = total + u_recv[k].astype(F32)
    v_buf[z] = total.astype(BF16)
    k2 = []
    for j, off in enumerate(offs[:-1]):
        cp = remote(v_buf.at[z], v_buf.at[z], k2_s.at[j], k2_r.at[j], z_peer(off))
        cp.start()
        k2.append(cp)

    total = b_both[b, pl.ds(3 * g, 3)].astype(F32)
    for k in range(n_g - 1):
        p5[k].wait_recv()
        total = total + b_recv[k].astype(F32)
    b_full[2 * b + a] = total.astype(BF16)
    mine = b_full.at[2 * b + a]
    p6 = []
    for k in range(1, 4):
        cp = remote(mine, mine, p6_s.at[k - 1], p6_r.at[k - 1], feat_peers[k - 1])
        cp.start()
        p6.append(cp)

    for j, off in enumerate(offs[:-1]):
        got = v_buf.at[(z + n_z - off) % n_z]
        remote(got, got, k2_s.at[j], k2_r.at[j], y_partner).wait_recv()
    total = v_buf[0].astype(F32)
    for j in range(1, n_z):
        total = total + v_buf[j].astype(F32)
    wg_piece[...] = total * (1.0 / math.sqrt(total_nodes))

    def wg_place(piece):
        return wg_out.at[
            pl.ds(pl.multiple_of((piece % n_row) * piece_rows, piece_rows), piece_rows),
            pl.ds(pl.multiple_of((piece // n_row) * 128, 128), 128),
        ]

    local_wg = pltpu.make_async_copy(wg_piece, wg_place(u), in_sem.at[4])
    local_wg.start()
    k3 = []
    for k in range(1, n_g):
        _, dev = u_peer(k)
        cp = remote(wg_piece, wg_place(u), k3_s.at[k - 1], k3_r.at[k - 1], dev)
        cp.start()
        k3.append(cp)
    for k in range(1, 4):
        f2 = (f + 4 - k) % 4
        got = b_full.at[2 * (f2 % 2) + (f2 // 2 + h) % 2]
        remote(got, got, p6_s.at[k - 1], p6_r.at[k - 1], y_partner).wait_recv()
    grad_t = jnp.zeros((w_ref.shape[0], node_dev), F32)
    for core in range(2):
        grad_t = grad_t + lax.dot_general(
            w_ref[:, 128 * core:128 * (core + 1)], b_full[2 * core:2 * core + 2].reshape(node_dev, 128),
            (((1,), (1,)), ((), ())), preferred_element_type=F32)
    fg_out[...] = grad_t.astype(BF16)

    for k in range(1, n_g):
        got = wg_place((u + n_g - k) % n_g)
        remote(wg_piece, got, k3_s.at[k - 1], k3_r.at[k - 1], y_partner).wait_recv()
    for k in range(1, 4):
        f2 = (f + 4 - k) % 4
        got = act_out.at[:, (f2 // 2 + h) % 2, :, pl.ds(pl.multiple_of((f2 % 2) * 128, 128), 128)]
        remote(act_v, got, act_s.at[k - 1], act_r.at[k - 1], y_partner).wait_recv()
    local.wait()
    local_wg.wait()
    for cp in copies + p2 + sent + acts + p5 + p6 + k1 + k2 + k3 + [xg, bc]:
        cp.wait_send()


def shards(n_row, n_z, features, weight, tile_values, tile_rows, tile_cols, tile_count, cotangent):
    slots = tile_values.shape[2]
    node_dev, out = cotangent.shape
    width = features.shape[1]
    n_g = 2 * n_row
    n_col = 2 * n_z
    piece_rows = 2 * width // n_g
    dma = pltpu.SemaphoreType.DMA
    pin = lambda x: pltpu.with_memory_space_constraint(x, pltpu.HBM)
    smem = pl.BlockSpec(memory_space=pltpu.SMEM)
    vmem = pl.BlockSpec(memory_space=pltpu.VMEM)
    hbm = pl.BlockSpec(memory_space=pltpu.HBM)
    sem_counts = [12, (3, 3), (3, 3), (n_g - 1, 3), (n_g - 1, 3), (n_z, 3), (n_z, 3), (n_z - 1, 3), (n_z - 1, 3),
                  3, 3, (n_z - 1, 3), (n_z - 1, 3), (n_z, 3), (n_z, 3),
                  1, 1, 1, 1, n_g - 1, n_g - 1, 3, 3, 2 * n_g - 1, 2 * n_g - 1, n_z - 1, n_z - 1, n_g - 1, n_g - 1]
    act, fg, wg = pl.pallas_call(
        functools.partial(kernel, n_row, n_z, slots, node_dev * n_row * n_col),
        out_shape=[
            jax.ShapeDtypeStruct((3, 2, 64, out), BF16),
            jax.ShapeDtypeStruct((width, node_dev), BF16),
            jax.ShapeDtypeStruct((width, out), F32),
        ],
        in_specs=[hbm, hbm, smem, hbm, hbm, hbm, hbm],
        out_specs=[vmem] * 3,
        scratch_shapes=[
            pltpu.SMEM((1, slots), jnp.int32),
            pltpu.SMEM((1, slots), jnp.int32),
            pltpu.VMEM((2, 1, slots), jnp.int32),
            pltpu.VMEM((8, 128), jnp.int32),
            pltpu.SMEM((8, 128), jnp.int32),
            pltpu.VMEM((width, node_dev), BF16),
            pltpu.VMEM((width, out), BF16),
            pltpu.VMEM((slots, 64, 128), BF16),
            pltpu.VMEM((3, 64, 128), BF16),
            pltpu.VMEM((4, 3, 64, 128), BF16),
            pltpu.VMEM((3, 3, 64, 128), BF16),
            pltpu.VMEM((3 * n_g, 64, 128), BF16),
            pltpu.VMEM((slots + 1, 64, 128), F32),
            pltpu.VMEM((n_col, 3, 64, 128), BF16),
            pltpu.VMEM((n_z, 3, 64, 128), BF16),
            pltpu.VMEM((n_z - 1, 3, 64, 128), BF16),
            pltpu.VMEM((n_z - 1, 3, 64, 128), BF16),
            pltpu.VMEM((3 * n_col, 64, 128), BF16),
            pltpu.VMEM((3, 64, 128), BF16),
            pltpu.VMEM((slots + 1, 128, 128), F32),
            pltpu.VMEM((2, 3 * n_g, 64, 128), BF16),
            pltpu.VMEM((n_g - 1, 3, 64, 128), BF16),
            pltpu.VMEM((4, 3, 64, 128), BF16),
            pltpu.VMEM((2, width, n_row * node_dev), BF16),
            pltpu.VMEM((2, n_g, piece_rows, 128), BF16),
            pltpu.VMEM((2 * n_g - 1, piece_rows, 128), BF16),
            pltpu.VMEM((n_z, piece_rows, 128), BF16),
            pltpu.VMEM((piece_rows, 128), F32),
            pltpu.SemaphoreType.REGULAR((2,)),
        ] + [dma(n if isinstance(n, tuple) else (n,)) for n in sem_counts],
        compiler_params=pltpu.CompilerParams(
            collective_id=0, has_side_effects=True, vmem_limit_bytes=40 * 1024 * 1024),
    )(
        pin(tile_rows.reshape(1, slots)), pin(tile_cols.reshape(1, slots)), tile_count,
        pin(features.T), pin(weight), pin(tile_values.reshape(slots, 2, 64, 128)), pin(cotangent.reshape(3, 2, 64, out)),
    )
    return act.reshape(node_dev, out), fg.T.reshape(1, node_dev, width), wg


def solution(mesh):
    return jax.shard_map(
        functools.partial(shards, mesh.shape["row"], mesh.shape["col"] // 2),
        mesh=mesh,
        in_specs=(
            P("col", "feat"),
            P("feat", None),
            P("row", "col", None, None, None),
            P("row", "col", None),
            P("row", "col", None),
            P("row", "col"),
            P(("row", "col"), None),
        ),
        out_specs=(P(("row", "col"), None), P("col", "row", "feat"), P("feat", None)),
        check_vma=False,
    )
```

```python
import functools
import math

import jax
import jax.numpy as jnp
from jax import lax
from jax.experimental import pallas as pl
from jax.experimental.pallas import tpu as pltpu
from jax.sharding import PartitionSpec as P

MESH = pl.DeviceIdType.MESH
F32 = jnp.float32
BF16 = jnp.bfloat16


def far_first(n):
    return sorted(range(1, n), key=lambda k: (-min(k, n - k), k))


def kernel(
    n_row, n_z, slots, total_nodes,
    rows_hbm, cols_hbm, count_s, feat_hbm, w_hbm, tiles_hbm, cot_hbm,
    act_out, fg_out, wg_out,
    rows_s, cols_s, keys_v, links_v, links_s,
    x_v, w_ref, tiles_v, cot_v,
    y_send, y_recv, y_buf, prod_f,
    s_buf, yh_recv, t_buf, z_recv, hg_buf, act_v,
    prod_b, b_both, b_recv, b_full,
    xt_both, u_send, u_recv, v_buf, wg_piece,
    here_sem, in_sem, p1_s, p1_r, p2_s, p2_r, p3a_s, p3a_r, p3b_s, p3b_r,
    act_s, act_r, p4z_s, p4z_r, p4y_s, p4y_r, xg_s, xg_r, bc_s, bc_r, p5_s, p5_r, p6_s, p6_r,
    k1_s, k1_r, k2_s, k2_r, k3_s, k3_r,
):
    f = lax.axis_index("feat")
    r = lax.axis_index("row")
    c = lax.axis_index("col")
    y_low, b = f // 2, f % 2
    z, h = c // 2, c % 2
    a = (y_low + h) % 2
    n_g = 2 * n_row

    def feat_of(role, core):
        return ((role + h) % 2) * 2 + core

    def remote(src, dst, send, recv, device):
        return pltpu.make_async_remote_copy(
            src_ref=src, dst_ref=dst, send_sem=send, recv_sem=recv, device_id=device, device_id_type=MESH
        )

    feat_peers = [{"feat": (f + k) % 4} for k in range(1, 4)]

    def g_peer(k):
        g2 = (2 * r + a + k) % n_g
        return g2, {"feat": feat_of(g2 % 2, b), "row": g2 // 2}

    def u_peer(k):
        u2 = (2 * r + h + k) % n_g
        return u2, {"row": u2 // 2, "col": 2 * z + u2 % 2}

    def z_peer(k):
        return {"col": 2 * ((z + k) % n_z) + h}

    y_partner = {"feat": (f + 2) % 4, "col": c + 1 - 2 * h}

    node_dev = x_v.shape[1]
    in_x = pltpu.make_async_copy(
        feat_hbm.at[:, pl.ds(pl.multiple_of(r * node_dev, node_dev), node_dev)], x_v, in_sem.at[0])
    in_w = pltpu.make_async_copy(w_hbm, w_ref, in_sem.at[5])
    in_keys = [
        pltpu.make_async_copy(rows_hbm, keys_v.at[0], in_sem.at[6]),
        pltpu.make_async_copy(cols_hbm, keys_v.at[1], in_sem.at[7]),
        pltpu.make_async_copy(rows_hbm, rows_s, in_sem.at[8]),
        pltpu.make_async_copy(cols_hbm, cols_s, in_sem.at[9]),
    ]
    in_t = pltpu.make_async_copy(tiles_hbm.at[:, a], tiles_v, in_sem.at[1])
    in_c = pltpu.make_async_copy(
        cot_hbm.at[:, a, :, pl.ds(pl.multiple_of(b * 128, 128), 128)], cot_v, in_sem.at[2])
    in_x.start()
    in_w.start()

    barrier = pltpu.get_barrier_semaphore()
    peers = list(feat_peers)
    x_sides = (1, n_row - 1) if n_row > 1 else ()
    for k in x_sides:
        peers.append({"row": (r + k) % n_row})
        peers.append({"feat": (f + 2) % 4, "row": (r + k) % n_row})
    peers += [z_peer(k) for k in (1, n_z - 1)]
    peers.append(y_partner)
    for peer in reversed(peers):
        pl.semaphore_signal(barrier, inc=1, device_id=peer, device_id_type=MESH)
    for cp in in_keys:
        cp.start()
    in_t.start()
    in_c.start()
    in_xt = pltpu.make_async_copy(feat_hbm, xt_both.at[y_low], in_sem.at[11])
    in_xt.start()

    in_x.wait()
    in_w.wait()
    y_part = lax.dot_general(
        x_v[...], w_ref[...], (((0,), (0,)), ((), ())), preferred_element_type=F32).astype(BF16)
    for q in range(2):
        for core in range(2):
            y_send[2 * q + core] = y_part[192 * q:192 * (q + 1), 128 * core:128 * (core + 1)].reshape(3, 64, 128)
    pl.semaphore_wait(barrier, len(peers))
    for k in (1, n_z - 1):
        pl.semaphore_signal(here_sem.at[0], inc=1, device_id=z_peer(k), device_id_type=MESH)
    for k in x_sides:
        pl.semaphore_signal(here_sem.at[2], inc=1, device_id={"row": (r + k) % n_row}, device_id_type=MESH)

    copies = []
    p1 = [[], [], []]
    for w in range(3):
        for k in range(1, 4):
            f2 = (f + k) % 4
            piece = ((f2 // 2 + h) % 2) * 2 + f2 % 2
            cp = remote(y_send.at[piece, w], y_recv.at[k - 1, w], p1_s.at[k - 1, w], p1_r.at[k - 1, w], feat_peers[k - 1])
            cp.start()
            copies.append(cp)
            p1[w].append(cp)
    for cp in in_keys:
        cp.wait()
    ids = lax.broadcasted_iota(jnp.int32, (slots, 128), 0)
    lanes = lax.broadcasted_iota(jnp.int32, (slots, 128), 1)
    live = ids < count_s[0, 0]
    for i in range(2):
        across = jnp.broadcast_to(keys_v[i], (slots, slots))
        across = jnp.concatenate([across, jnp.zeros((slots, 128 - slots), jnp.int32)], axis=1)
        down = jnp.sum(jnp.where(ids == lanes, across, 0), axis=1, keepdims=True)
        down = jnp.broadcast_to(down, (slots, 128))
        before = jnp.where(live & (ids < lanes) & (down == across), ids, -1)
        there = jnp.where(live & (down == lanes), ids, -1)
        for w, found in ((0, before), (1, there)):
            top = jnp.max(found, axis=0, keepdims=True)
            links_v[pl.ds(2 * i + w, 1), :] = jnp.where(top < 0, slots, top)
    links = pltpu.make_async_copy(links_v, links_s, in_sem.at[10])
    links.start()
    pl.semaphore_wait(here_sem.at[0], 2)
    if x_sides:
        pl.semaphore_wait(here_sem.at[2], 2)
    for k in (2, n_z - 2):
        pl.semaphore_signal(here_sem.at[1], inc=1, device_id=z_peer(k), device_id_type=MESH)

    g = 2 * r + a
    p2 = []
    for w in range(3):
        total = y_send[2 * a + b, w].astype(F32)
        for k in range(3):
            p1[w][k].wait_recv()
            total = total + y_recv[k, w].astype(F32)
        y_buf[3 * g + w] = total.astype(BF16)
        mine = y_buf.at[3 * g + w]
        for k in range(1, n_g):
            _, dev = g_peer(k)
            cp = remote(mine, mine, p2_s.at[k - 1, w], p2_r.at[k - 1, w], dev)
            cp.start()
            p2.append(cp)
    prod_f[slots] = jnp.zeros((64, 128), F32)
    prod_b[slots] = jnp.zeros((128, 128), F32)
    in_t.wait()
    links.wait()
    for w in range(3):
        for k in range(1, n_g):
            got = y_buf.at[3 * ((g + n_g - k) % n_g) + w]
            remote(got, got, p2_s.at[k - 1, w], p2_r.at[k - 1, w], y_partner).wait_recv()

    pl.semaphore_wait(here_sem.at[1], 2)

    xg = remote(feat_hbm, xt_both.at[y_low], xg_s.at[0], xg_r.at[0], {"feat": (f + 2) % 4})
    xg.start()

    def forward(s, _):
        block = y_buf[pl.ds(2 * cols_s[0, s], 2)].reshape(128, 128)
        prod_f[s] = jnp.dot(tiles_v[s], block, preferred_element_type=F32) + prod_f[links_s[0, s]]
        return 0

    lax.fori_loop(0, slots, forward, 0, unroll=32)

    def fill(c2, w):
        s_buf[c2, w] = prod_f[links_s[1, 3 * c2 + w]].astype(BF16)

    sent = []

    def send(src, dst, send_sem, recv_sem, device):
        cp = remote(src, dst, send_sem, recv_sem, device)
        cp.start()
        sent.append(cp)
        return cp

    offs = far_first(n_z) + [0]
    p3a = [[], [], []]
    for w in range(3):
        for j, off in enumerate(offs):
            c2 = 2 * ((z + off) % n_z) + 1 - h
            fill(c2, w)
            p3a[w].append(send(s_buf.at[c2, w], yh_recv.at[j, w], p3a_s.at[j, w], p3a_r.at[j, w], y_partner))
    for w in range(3):
        for off in offs:
            fill(2 * ((z + off) % n_z) + h, w)
    p3b = [[], [], []]
    own_part = [None] * 3

    def sum_h(w):
        for j, off in enumerate(offs):
            c2 = 2 * ((z + off) % n_z) + h
            p3a[w][j].wait_recv()
            both = s_buf[c2, w].astype(F32) + yh_recv[j, w].astype(F32)
            if off:
                t_buf[j, w] = both.astype(BF16)
                p3b[w].append(send(t_buf.at[j, w], z_recv.at[j, w], p3b_s.at[j, w], p3b_r.at[j, w], z_peer(off)))
            else:
                own_part[w] = both

    def place(dist, w):
        return hg_buf.at[3 * (2 * ((z + 2 * n_z - dist) % n_z) + h) + w]

    def z_send(what, j, off, w):
        send(what, what, p4z_s.at[j, w], p4z_r.at[j, w], z_peer(off))

    def y_send_on(what, j, w):
        send(what, what, p4y_s.at[j, w], p4y_r.at[j, w], y_partner)

    def arrived(j, dist, w):
        got = place(dist, w)
        remote(got, got, p4z_s.at[j, w], p4z_r.at[j, w], y_partner).wait_recv()
        return got

    def activate(w):
        hidden = own_part[w]
        for j in range(n_z - 1):
            p3b[w][j].wait_recv()
            hidden = hidden + z_recv[j, w].astype(F32)
        sigma = jax.nn.sigmoid(hidden)
        grad = cot_v[w].astype(F32) * (sigma * (1.0 + hidden * (1.0 - sigma)))
        hg_buf[3 * c + w] = grad.astype(BF16)
        act_v[w] = (hidden * sigma).astype(BF16)
        own = hg_buf.at[3 * c + w]
        if w == 2:
            z_send(own, 6, 4, w)
            z_send(own, 4, 3, w)
            z_send(own, 5, n_z - 3, w)
        z_send(own, 2, 2, w)
        z_send(own, 3, n_z - 2, w)
        z_send(own, 0, 1, w)
        z_send(own, 1, n_z - 1, w)
        y_send_on(own, n_z - 1, w)

    side = 1 - 2 * (z % 2)

    def pass_on(w):
        if w < 2:
            plus = arrived(2, 2, w)
            z_send(plus, 4, 1, w)
            minus = arrived(3, n_z - 2, w)
            z_send(minus, 5, n_z - 1, w)
            z_send(place(2 * side + n_z, w), 6, 2 * side + n_z, w)
        y_send_on(arrived(0, 1, w), 0, w)
        y_send_on(arrived(1, n_z - 1, w), 1, w)
        if w == 2:
            plus = arrived(2, 2, w)
            minus = arrived(3, n_z - 2, w)
        y_send_on(plus, 2, w)
        y_send_on(minus, 3, w)

    def last_on(w):
        y_send_on(arrived(4, 3, w), 4, w)
        y_send_on(arrived(5, n_z - 3, w), 5, w)
        y_send_on(arrived(6, 4, w), 6, w)

    in_c.wait()
    sum_h(0)
    sum_h(1)
    activate(0)
    sum_h(2)
    activate(1)
    pass_on(0)
    activate(2)
    act_cols = pl.ds(pl.multiple_of(b * 128, 128), 128)
    act_dst = act_out.at[:, a, :, act_cols]
    local = pltpu.make_async_copy(act_v, act_dst, in_sem.at[3])
    local.start()
    pass_on(1)
    last_on(0)
    pass_on(2)
    last_on(1)
    last_on(2)
    acts = []
    for k in range(1, 4):
        cp = remote(act_v, act_dst, act_s.at[k - 1], act_r.at[k - 1], feat_peers[k - 1])
        cp.start()
        acts.append(cp)
    for w in range(3):
        for j, dist in enumerate([1, n_z - 1, 2, n_z - 2, 3, n_z - 3, 4, 0]):
            got = hg_buf.at[3 * (2 * ((z + n_z - dist) % n_z) + 1 - h) + w]
            remote(got, got, p4y_s.at[j, w], p4y_r.at[j, w], y_partner).wait_recv()

    def backward(s, _):
        prod_b[s] = lax.dot_general(
            tiles_v[s], hg_buf[rows_s[0, s]], (((0,), (0,)), ((), ())), preferred_element_type=F32) + prod_b[links_s[2, s]]
        return 0

    lax.fori_loop(0, slots, backward, 0, unroll=32)

    for j in range(3 * n_row):
        b_both[b, pl.ds(2 * j, 2)] = prod_b[links_s[3, j]].astype(BF16).reshape(2, 64, 128)

    bc = remote(b_both.at[b], b_both.at[b], bc_s.at[0], bc_r.at[0], {"feat": f + 1 - 2 * b})
    bc.start()

    piece_rows = u_send.shape[2]
    in_xt.wait()
    xg.wait_recv()
    got = b_both.at[1 - b]
    remote(got, got, bc_s.at[0], bc_r.at[0], y_partner).wait_recv()
    both = jnp.concatenate([b_both[0].reshape(n_row * node_dev, 128), b_both[1].reshape(n_row * node_dev, 128)], axis=1)
    for low in range(2):
        part = jnp.dot(xt_both[low], both, preferred_element_type=F32).astype(BF16)
        for core in range(2):
            u_send[low, n_row * core:n_row * (core + 1)] = part[:, 128 * core:128 * (core + 1)].reshape(
                n_row, piece_rows, 128)
    u = 2 * r + h
    k1 = []
    for k in range(1, 2 * n_g):
        q2 = (n_g * y_low + u + k) % (2 * n_g)
        low2, u2 = q2 // n_g, q2 % n_g
        dev = {"feat": 2 * low2 + b, "row": u2 // 2, "col": 2 * z + u2 % 2}
        cp = remote(u_send.at[low2, u2], u_recv.at[k - 1], k1_s.at[k - 1], k1_r.at[k - 1], dev)
        cp.start()
        k1.append(cp)

    p5 = []
    for k in range(1, n_g):
        g2, dev = g_peer(k)
        cp = remote(b_both.at[b, pl.ds(3 * g2, 3)], b_recv.at[k - 1], p5_s.at[k - 1], p5_r.at[k - 1], dev)
        cp.start()
        p5.append(cp)

    total = u_send[y_low, u].astype(F32)
    for k in range(2 * n_g - 1):
        k1[k].wait_recv()
        total = total + u_recv[k].astype(F32)
    v_buf[z] = total.astype(BF16)
    k2 = []
    for j, off in enumerate(offs[:-1]):
        cp = remote(v_buf.at[z], v_buf.at[z], k2_s.at[j], k2_r.at[j], z_peer(off))
        cp.start()
        k2.append(cp)

    total = b_both[b, pl.ds(3 * g, 3)].astype(F32)
    for k in range(n_g - 1):
        p5[k].wait_recv()
        total = total + b_recv[k].astype(F32)
    b_full[2 * b + a] = total.astype(BF16)
    mine = b_full.at[2 * b + a]
    p6 = []
    for k in range(1, 4):
        cp = remote(mine, mine, p6_s.at[k - 1], p6_r.at[k - 1], feat_peers[k - 1])
        cp.start()
        p6.append(cp)

    for j, off in enumerate(offs[:-1]):
        got = v_buf.at[(z + n_z - off) % n_z]
        remote(got, got, k2_s.at[j], k2_r.at[j], y_partner).wait_recv()
    total = v_buf[0].astype(F32)
    for j in range(1, n_z):
        total = total + v_buf[j].astype(F32)
    wg_piece[...] = total * (1.0 / math.sqrt(total_nodes))

    def wg_place(piece):
        return wg_out.at[
            pl.ds(pl.multiple_of((piece % n_row) * piece_rows, piece_rows), piece_rows),
            pl.ds(pl.multiple_of((piece // n_row) * 128, 128), 128),
        ]

    local_wg = pltpu.make_async_copy(wg_piece, wg_place(u), in_sem.at[4])
    local_wg.start()
    k3 = []
    for k in range(1, n_g):
        _, dev = u_peer(k)
        cp = remote(wg_piece, wg_place(u), k3_s.at[k - 1], k3_r.at[k - 1], dev)
        cp.start()
        k3.append(cp)
    for k in range(1, 4):
        f2 = (f + 4 - k) % 4
        got = b_full.at[2 * (f2 % 2) + (f2 // 2 + h) % 2]
        remote(got, got, p6_s.at[k - 1], p6_r.at[k - 1], y_partner).wait_recv()
    grad_t = jnp.zeros((w_ref.shape[0], node_dev), F32)
    for core in range(2):
        grad_t = grad_t + lax.dot_general(
            w_ref[:, 128 * core:128 * (core + 1)], b_full[2 * core:2 * core + 2].reshape(node_dev, 128),
            (((1,), (1,)), ((), ())), preferred_element_type=F32)
    fg_out[...] = grad_t.astype(BF16)

    for k in range(1, n_g):
        got = wg_place((u + n_g - k) % n_g)
        remote(wg_piece, got, k3_s.at[k - 1], k3_r.at[k - 1], y_partner).wait_recv()
    for k in range(1, 4):
        f2 = (f + 4 - k) % 4
        got = act_out.at[:, (f2 // 2 + h) % 2, :, pl.ds(pl.multiple_of((f2 % 2) * 128, 128), 128)]
        remote(act_v, got, act_s.at[k - 1], act_r.at[k - 1], y_partner).wait_recv()
    local.wait()
    local_wg.wait()
    for cp in copies + p2 + sent + acts + p5 + p6 + k1 + k2 + k3 + [xg, bc]:
        cp.wait_send()


def shards(n_row, n_z, features, weight, tile_values, tile_rows, tile_cols, tile_count, cotangent):
    slots = tile_values.shape[2]
    node_dev, out = cotangent.shape
    width = features.shape[1]
    n_g = 2 * n_row
    n_col = 2 * n_z
    piece_rows = 2 * width // n_g
    dma = pltpu.SemaphoreType.DMA
    pin = lambda x: pltpu.with_memory_space_constraint(x, pltpu.HBM)
    smem = pl.BlockSpec(memory_space=pltpu.SMEM)
    vmem = pl.BlockSpec(memory_space=pltpu.VMEM)
    hbm = pl.BlockSpec(memory_space=pltpu.HBM)
    sem_counts = [12, (3, 3), (3, 3), (n_g - 1, 3), (n_g - 1, 3), (n_z, 3), (n_z, 3), (n_z - 1, 3), (n_z - 1, 3),
                  3, 3, (n_z - 1, 3), (n_z - 1, 3), (n_z, 3), (n_z, 3),
                  1, 1, 1, 1, n_g - 1, n_g - 1, 3, 3, 2 * n_g - 1, 2 * n_g - 1, n_z - 1, n_z - 1, n_g - 1, n_g - 1]
    act, fg, wg = pl.pallas_call(
        functools.partial(kernel, n_row, n_z, slots, node_dev * n_row * n_col),
        out_shape=[
            jax.ShapeDtypeStruct((3, 2, 64, out), BF16),
            jax.ShapeDtypeStruct((width, node_dev), BF16),
            jax.ShapeDtypeStruct((width, out), F32),
        ],
        in_specs=[hbm, hbm, smem, hbm, hbm, hbm, hbm],
        out_specs=[vmem] * 3,
        scratch_shapes=[
            pltpu.SMEM((1, slots), jnp.int32),
            pltpu.SMEM((1, slots), jnp.int32),
            pltpu.VMEM((2, 1, slots), jnp.int32),
            pltpu.VMEM((8, 128), jnp.int32),
            pltpu.SMEM((8, 128), jnp.int32),
            pltpu.VMEM((width, node_dev), BF16),
            pltpu.VMEM((width, out), BF16),
            pltpu.VMEM((slots, 64, 128), BF16),
            pltpu.VMEM((3, 64, 128), BF16),
            pltpu.VMEM((4, 3, 64, 128), BF16),
            pltpu.VMEM((3, 3, 64, 128), BF16),
            pltpu.VMEM((3 * n_g, 64, 128), BF16),
            pltpu.VMEM((slots + 1, 64, 128), F32),
            pltpu.VMEM((n_col, 3, 64, 128), BF16),
            pltpu.VMEM((n_z, 3, 64, 128), BF16),
            pltpu.VMEM((n_z - 1, 3, 64, 128), BF16),
            pltpu.VMEM((n_z - 1, 3, 64, 128), BF16),
            pltpu.VMEM((3 * n_col, 64, 128), BF16),
            pltpu.VMEM((3, 64, 128), BF16),
            pltpu.VMEM((slots + 1, 128, 128), F32),
            pltpu.VMEM((2, 3 * n_g, 64, 128), BF16),
            pltpu.VMEM((n_g - 1, 3, 64, 128), BF16),
            pltpu.VMEM((4, 3, 64, 128), BF16),
            pltpu.VMEM((2, width, n_row * node_dev), BF16),
            pltpu.VMEM((2, n_g, piece_rows, 128), BF16),
            pltpu.VMEM((2 * n_g - 1, piece_rows, 128), BF16),
            pltpu.VMEM((n_z, piece_rows, 128), BF16),
            pltpu.VMEM((piece_rows, 128), F32),
            pltpu.SemaphoreType.REGULAR((3,)),
        ] + [dma(n if isinstance(n, tuple) else (n,)) for n in sem_counts],
        compiler_params=pltpu.CompilerParams(
            collective_id=0, has_side_effects=True, vmem_limit_bytes=40 * 1024 * 1024),
    )(
        pin(tile_rows.reshape(1, slots)), pin(tile_cols.reshape(1, slots)), tile_count,
        pin(features.T), pin(weight), pin(tile_values.reshape(slots, 2, 64, 128)), pin(cotangent.reshape(3, 2, 64, out)),
    )
    return act.reshape(node_dev, out), fg.T.reshape(1, node_dev, width), wg


def solution(mesh):
    return jax.shard_map(
        functools.partial(shards, mesh.shape["row"], mesh.shape["col"] // 2),
        mesh=mesh,
        in_specs=(
            P("col", "feat"),
            P("feat", None),
            P("row", "col", None, None, None),
            P("row", "col", None),
            P("row", "col", None),
            P("row", "col"),
            P(("row", "col"), None),
        ),
        out_specs=(P(("row", "col"), None), P("col", "row", "feat"), P("feat", None)),
        check_vma=False,
    )
```

```python
import functools
import math

import jax
import jax.numpy as jnp
from jax import lax
from jax.experimental import pallas as pl
from jax.experimental.pallas import tpu as pltpu
from jax.sharding import PartitionSpec as P

MESH = pl.DeviceIdType.MESH
F32 = jnp.float32
BF16 = jnp.bfloat16


def far_first(n):
    return sorted(range(1, n), key=lambda k: (-min(k, n - k), k))


def kernel(
    n_row, n_z, slots, total_nodes,
    rows_hbm, cols_hbm, count_s, feat_hbm, w_hbm, tiles_hbm, cot_hbm,
    act_out, fg_out, wg_out,
    rows_s, cols_s, keys_v, links_v, links_s,
    x_v, w_ref, tiles_v, cot_v,
    y_send, y_recv, y_buf, prod_f,
    s_buf, yh_recv, t_buf, z_recv, hg_buf, act_v,
    prod_b, b_both, b_recv, b_full,
    xt_both, u_send, u_recv, v_buf, wg_piece,
    here_sem, in_sem, p1_s, p1_r, p2_s, p2_r, p3a_s, p3a_r, p3b_s, p3b_r,
    act_s, act_r, p4z_s, p4z_r, p4y_s, p4y_r, xg_s, xg_r, bc_s, bc_r, p5_s, p5_r, p6_s, p6_r,
    k1_s, k1_r, k2_s, k2_r, k3_s, k3_r,
):
    f = lax.axis_index("feat")
    r = lax.axis_index("row")
    c = lax.axis_index("col")
    y_low, b = f // 2, f % 2
    z, h = c // 2, c % 2
    a = (y_low + h) % 2
    n_g = 2 * n_row

    def feat_of(role, core):
        return ((role + h) % 2) * 2 + core

    def remote(src, dst, send, recv, device):
        return pltpu.make_async_remote_copy(
            src_ref=src, dst_ref=dst, send_sem=send, recv_sem=recv, device_id=device, device_id_type=MESH
        )

    feat_peers = [{"feat": (f + k) % 4} for k in range(1, 4)]

    def g_peer(k):
        g2 = (2 * r + a + k) % n_g
        return g2, {"feat": feat_of(g2 % 2, b), "row": g2 // 2}

    def u_peer(k):
        u2 = (2 * r + h + k) % n_g
        return u2, {"row": u2 // 2, "col": 2 * z + u2 % 2}

    def z_peer(k):
        return {"col": 2 * ((z + k) % n_z) + h}

    y_partner = {"feat": (f + 2) % 4, "col": c + 1 - 2 * h}

    node_dev = x_v.shape[1]
    in_x = pltpu.make_async_copy(
        feat_hbm.at[:, pl.ds(pl.multiple_of(r * node_dev, node_dev), node_dev)], x_v, in_sem.at[0])
    in_w = pltpu.make_async_copy(w_hbm, w_ref, in_sem.at[5])
    in_keys = [
        pltpu.make_async_copy(rows_hbm, keys_v.at[0], in_sem.at[6]),
        pltpu.make_async_copy(cols_hbm, keys_v.at[1], in_sem.at[7]),
        pltpu.make_async_copy(rows_hbm, rows_s, in_sem.at[8]),
        pltpu.make_async_copy(cols_hbm, cols_s, in_sem.at[9]),
    ]
    in_t = pltpu.make_async_copy(tiles_hbm.at[:, a], tiles_v, in_sem.at[1])
    in_c = pltpu.make_async_copy(
        cot_hbm.at[:, a, :, pl.ds(pl.multiple_of(b * 128, 128), 128)], cot_v, in_sem.at[2])
    in_x.start()
    in_w.start()

    barrier = pltpu.get_barrier_semaphore()
    peers = list(feat_peers)
    x_sides = (1, n_row - 1) if n_row > 1 else ()
    for k in x_sides:
        peers.append({"row": (r + k) % n_row})
        peers.append({"feat": (f + 2) % 4, "row": (r + k) % n_row})
    peers += [z_peer(k) for k in (1, n_z - 1)]
    peers.append(y_partner)
    for peer in reversed(peers):
        pl.semaphore_signal(barrier, inc=1, device_id=peer, device_id_type=MESH)
    for cp in in_keys:
        cp.start()
    in_t.start()
    in_c.start()
    in_xt = pltpu.make_async_copy(feat_hbm, xt_both.at[y_low], in_sem.at[11])
    in_xt.start()

    in_x.wait()
    in_w.wait()
    y_part = lax.dot_general(
        x_v[...], w_ref[...], (((0,), (0,)), ((), ())), preferred_element_type=F32).astype(BF16)
    for q in range(2):
        for core in range(2):
            y_send[2 * q + core] = y_part[192 * q:192 * (q + 1), 128 * core:128 * (core + 1)].reshape(3, 64, 128)
    pl.semaphore_wait(barrier, len(peers))
    for k in (1, n_z - 1):
        pl.semaphore_signal(here_sem.at[0], inc=1, device_id=z_peer(k), device_id_type=MESH)
    for k in x_sides:
        pl.semaphore_signal(here_sem.at[2], inc=1, device_id={"row": (r + k) % n_row}, device_id_type=MESH)

    copies = []
    p1 = [[], [], []]
    for w in range(3):
        for k in range(1, 4):
            f2 = (f + k) % 4
            piece = ((f2 // 2 + h) % 2) * 2 + f2 % 2
            cp = remote(y_send.at[piece, w], y_recv.at[k - 1, w], p1_s.at[k - 1, w], p1_r.at[k - 1, w], feat_peers[k - 1])
            cp.start()
            copies.append(cp)
            p1[w].append(cp)
    for cp in in_keys:
        cp.wait()
    ids = lax.broadcasted_iota(jnp.int32, (slots, 128), 0)
    lanes = lax.broadcasted_iota(jnp.int32, (slots, 128), 1)
    live = ids < count_s[0, 0]
    for i in range(2):
        across = jnp.broadcast_to(keys_v[i], (slots, slots))
        across = jnp.concatenate([across, jnp.zeros((slots, 128 - slots), jnp.int32)], axis=1)
        down = jnp.sum(jnp.where(ids == lanes, across, 0), axis=1, keepdims=True)
        down = jnp.broadcast_to(down, (slots, 128))
        before = jnp.where(live & (ids < lanes) & (down == across), ids, -1)
        there = jnp.where(live & (down == lanes), ids, -1)
        for w, found in ((0, before), (1, there)):
            top = jnp.max(found, axis=0, keepdims=True)
            links_v[pl.ds(2 * i + w, 1), :] = jnp.where(top < 0, slots, top)
    links = pltpu.make_async_copy(links_v, links_s, in_sem.at[10])
    links.start()
    pl.semaphore_wait(here_sem.at[0], 2)
    if x_sides:
        pl.semaphore_wait(here_sem.at[2], 2)
    for k in (2, n_z - 2):
        pl.semaphore_signal(here_sem.at[1], inc=1, device_id=z_peer(k), device_id_type=MESH)

    g = 2 * r + a
    p2 = []
    g_order = sorted(range(1, n_g), key=lambda k: -min(k, n_g - k))
    for w in range(3):
        total = y_send[2 * a + b, w].astype(F32)
        for k in range(3):
            p1[w][k].wait_recv()
            total = total + y_recv[k, w].astype(F32)
        y_buf[3 * g + w] = total.astype(BF16)
        mine = y_buf.at[3 * g + w]
        for k in g_order:
            _, dev = g_peer(k)
            cp = remote(mine, mine, p2_s.at[k - 1, w], p2_r.at[0], dev)
            cp.start()
            p2.append(cp)
    prod_f[slots] = jnp.zeros((64, 128), F32)
    prod_b[slots] = jnp.zeros((128, 128), F32)
    in_t.wait()
    links.wait()
    got = y_buf.at[pl.ds(0, 3 * (n_g - 1))]
    remote(got, got, p2_s.at[0, 0], p2_r.at[0], y_partner).wait_recv()

    pl.semaphore_wait(here_sem.at[1], 2)

    xg = remote(feat_hbm, xt_both.at[y_low], xg_s.at[0], xg_r.at[0], {"feat": (f + 2) % 4})
    xg.start()

    def forward(s, _):
        block = y_buf[pl.ds(2 * cols_s[0, s], 2)].reshape(128, 128)
        prod_f[s] = jnp.dot(tiles_v[s], block, preferred_element_type=F32) + prod_f[links_s[0, s]]
        return 0

    lax.fori_loop(0, slots, forward, 0, unroll=32)

    def fill(c2, w):
        s_buf[c2, w] = prod_f[links_s[1, 3 * c2 + w]].astype(BF16)

    sent = []

    def send(src, dst, send_sem, recv_sem, device):
        cp = remote(src, dst, send_sem, recv_sem, device)
        cp.start()
        sent.append(cp)
        return cp

    offs = far_first(n_z) + [0]
    p3a = [[], [], []]
    for w in range(3):
        for j, off in enumerate(offs):
            c2 = 2 * ((z + off) % n_z) + 1 - h
            fill(c2, w)
            p3a[w].append(send(s_buf.at[c2, w], yh_recv.at[j, w], p3a_s.at[j, w], p3a_r.at[j, w], y_partner))
    for w in range(3):
        for off in offs:
            fill(2 * ((z + off) % n_z) + h, w)
    p3b = [[], [], []]
    own_part = [None] * 3

    def sum_h(w):
        for j, off in enumerate(offs):
            c2 = 2 * ((z + off) % n_z) + h
            p3a[w][j].wait_recv()
            both = s_buf[c2, w].astype(F32) + yh_recv[j, w].astype(F32)
            if off:
                t_buf[j, w] = both.astype(BF16)
                p3b[w].append(send(t_buf.at[j, w], z_recv.at[j, w], p3b_s.at[j, w], p3b_r.at[j, w], z_peer(off)))
            else:
                own_part[w] = both

    def place(dist, w):
        return hg_buf.at[3 * (2 * ((z + 2 * n_z - dist) % n_z) + h) + w]

    def z_send(what, j, off, w):
        send(what, what, p4z_s.at[j, w], p4z_r.at[j, w], z_peer(off))

    def y_send_on(what, j, w):
        send(what, what, p4y_s.at[j, w], p4y_r.at[0], y_partner)

    def arrived(j, dist, w):
        got = place(dist, w)
        remote(got, got, p4z_s.at[j, w], p4z_r.at[j, w], y_partner).wait_recv()
        return got

    def activate(w):
        hidden = own_part[w]
        for j in range(n_z - 1):
            p3b[w][j].wait_recv()
            hidden = hidden + z_recv[j, w].astype(F32)
        sigma = jax.nn.sigmoid(hidden)
        grad = cot_v[w].astype(F32) * (sigma * (1.0 + hidden * (1.0 - sigma)))
        hg_buf[3 * c + w] = grad.astype(BF16)
        act_v[w] = (hidden * sigma).astype(BF16)
        own = hg_buf.at[3 * c + w]
        if w == 2:
            z_send(own, 6, 4, w)
            z_send(own, 4, 3, w)
            z_send(own, 5, n_z - 3, w)
        z_send(own, 2, 2, w)
        z_send(own, 3, n_z - 2, w)
        z_send(own, 0, 1, w)
        z_send(own, 1, n_z - 1, w)
        y_send_on(own, n_z - 1, w)

    side = 1 - 2 * (z % 2)

    def pass_on(w):
        if w < 2:
            plus = arrived(2, 2, w)
            z_send(plus, 4, 1, w)
            minus = arrived(3, n_z - 2, w)
            z_send(minus, 5, n_z - 1, w)
            z_send(place(2 * side + n_z, w), 6, 2 * side + n_z, w)
        y_send_on(arrived(0, 1, w), 0, w)
        y_send_on(arrived(1, n_z - 1, w), 1, w)
        if w == 2:
            plus = arrived(2, 2, w)
            minus = arrived(3, n_z - 2, w)
        y_send_on(plus, 2, w)
        y_send_on(minus, 3, w)

    def last_on(w):
        y_send_on(arrived(4, 3, w), 4, w)
        y_send_on(arrived(5, n_z - 3, w), 5, w)
        y_send_on(arrived(6, 4, w), 6, w)

    in_c.wait()
    sum_h(0)
    sum_h(1)
    activate(0)
    sum_h(2)
    activate(1)
    pass_on(0)
    activate(2)
    act_cols = pl.ds(pl.multiple_of(b * 128, 128), 128)
    act_dst = act_out.at[:, a, :, act_cols]
    local = pltpu.make_async_copy(act_v, act_dst, in_sem.at[3])
    local.start()
    pass_on(1)
    last_on(0)
    pass_on(2)
    last_on(1)
    last_on(2)
    acts = []
    for k in range(1, 4):
        cp = remote(act_v, act_dst, act_s.at[k - 1], act_r.at[k - 1], feat_peers[k - 1])
        cp.start()
        acts.append(cp)
    got = hg_buf.at[pl.ds(0, 3 * n_z)]
    remote(got, got, p4y_s.at[0, 0], p4y_r.at[0], y_partner).wait_recv()

    def backward(s, _):
        prod_b[s] = lax.dot_general(
            tiles_v[s], hg_buf[rows_s[0, s]], (((0,), (0,)), ((), ())), preferred_element_type=F32) + prod_b[links_s[2, s]]
        return 0

    lax.fori_loop(0, slots, backward, 0, unroll=32)

    for j in range(3 * n_row):
        b_both[b, pl.ds(2 * j, 2)] = prod_b[links_s[3, j]].astype(BF16).reshape(2, 64, 128)

    bc = remote(b_both.at[b], b_both.at[b], bc_s.at[0], bc_r.at[0], {"feat": f + 1 - 2 * b})
    bc.start()

    piece_rows = u_send.shape[2]
    in_xt.wait()
    xg.wait_recv()
    got = b_both.at[1 - b]
    remote(got, got, bc_s.at[0], bc_r.at[0], y_partner).wait_recv()
    both = jnp.concatenate([b_both[0].reshape(n_row * node_dev, 128), b_both[1].reshape(n_row * node_dev, 128)], axis=1)
    for low in range(2):
        part = jnp.dot(xt_both[low], both, preferred_element_type=F32).astype(BF16)
        for core in range(2):
            u_send[low, n_row * core:n_row * (core + 1)] = part[:, 128 * core:128 * (core + 1)].reshape(
                n_row, piece_rows, 128)
    u = 2 * r + h
    k1 = []
    for k in range(1, 2 * n_g):
        q2 = (n_g * y_low + u + k) % (2 * n_g)
        low2, u2 = q2 // n_g, q2 % n_g
        dev = {"feat": 2 * low2 + b, "row": u2 // 2, "col": 2 * z + u2 % 2}
        cp = remote(u_send.at[low2, u2], u_recv.at[k - 1], k1_s.at[k - 1], k1_r.at[k - 1], dev)
        cp.start()
        k1.append(cp)

    p5 = []
    for k in range(1, n_g):
        g2, dev = g_peer(k)
        cp = remote(b_both.at[b, pl.ds(3 * g2, 3)], b_recv.at[k - 1], p5_s.at[k - 1], p5_r.at[k - 1], dev)
        cp.start()
        p5.append(cp)

    total = u_send[y_low, u].astype(F32)
    for k in range(2 * n_g - 1):
        k1[k].wait_recv()
        total = total + u_recv[k].astype(F32)
    v_buf[z] = total.astype(BF16)
    k2 = []
    for j, off in enumerate(offs[:-1]):
        cp = remote(v_buf.at[z], v_buf.at[z], k2_s.at[j], k2_r.at[j], z_peer(off))
        cp.start()
        k2.append(cp)
    for cp in copies + p2 + sent + acts + p5 + k1 + [xg, bc]:
        cp.wait_send()

    total = b_both[b, pl.ds(3 * g, 3)].astype(F32)
    for k in range(n_g - 1):
        p5[k].wait_recv()
        total = total + b_recv[k].astype(F32)
    b_full[2 * b + a] = total.astype(BF16)
    mine = b_full.at[2 * b + a]
    p6 = []
    for k in range(1, 4):
        cp = remote(mine, mine, p6_s.at[k - 1], p6_r.at[k - 1], feat_peers[k - 1])
        cp.start()
        p6.append(cp)

    for j, off in enumerate(offs[:-1]):
        got = v_buf.at[(z + n_z - off) % n_z]
        remote(got, got, k2_s.at[j], k2_r.at[j], y_partner).wait_recv()
    total = v_buf[0].astype(F32)
    for j in range(1, n_z):
        total = total + v_buf[j].astype(F32)
    wg_piece[...] = total * (1.0 / math.sqrt(total_nodes))

    def wg_place(piece):
        return wg_out.at[
            pl.ds(pl.multiple_of((piece % n_row) * piece_rows, piece_rows), piece_rows),
            pl.ds(pl.multiple_of((piece // n_row) * 128, 128), 128),
        ]

    local_wg = pltpu.make_async_copy(wg_piece, wg_place(u), in_sem.at[4])
    local_wg.start()
    k3 = []
    for k in range(1, n_g):
        _, dev = u_peer(k)
        cp = remote(wg_piece, wg_place(u), k3_s.at[k - 1], k3_r.at[k - 1], dev)
        cp.start()
        k3.append(cp)
    for k in range(1, 4):
        f2 = (f + 4 - k) % 4
        got = b_full.at[2 * (f2 % 2) + (f2 // 2 + h) % 2]
        remote(got, got, p6_s.at[k - 1], p6_r.at[k - 1], y_partner).wait_recv()
    grad_t = jnp.zeros((w_ref.shape[0], node_dev), F32)
    for core in range(2):
        grad_t = grad_t + lax.dot_general(
            w_ref[:, 128 * core:128 * (core + 1)], b_full[2 * core:2 * core + 2].reshape(node_dev, 128),
            (((1,), (1,)), ((), ())), preferred_element_type=F32)
    fg_out[...] = grad_t.astype(BF16)

    for k in range(1, n_g):
        got = wg_place((u + n_g - k) % n_g)
        remote(wg_piece, got, k3_s.at[k - 1], k3_r.at[k - 1], y_partner).wait_recv()
    for k in range(1, 4):
        f2 = (f + 4 - k) % 4
        got = act_out.at[:, (f2 // 2 + h) % 2, :, pl.ds(pl.multiple_of((f2 % 2) * 128, 128), 128)]
        remote(act_v, got, act_s.at[k - 1], act_r.at[k - 1], y_partner).wait_recv()
    local.wait()
    local_wg.wait()
    for cp in p6 + k2 + k3:
        cp.wait_send()


def shards(n_row, n_z, features, weight, tile_values, tile_rows, tile_cols, tile_count, cotangent):
    slots = tile_values.shape[2]
    node_dev, out = cotangent.shape
    width = features.shape[1]
    n_g = 2 * n_row
    n_col = 2 * n_z
    piece_rows = 2 * width // n_g
    dma = pltpu.SemaphoreType.DMA
    pin = lambda x: pltpu.with_memory_space_constraint(x, pltpu.HBM)
    smem = pl.BlockSpec(memory_space=pltpu.SMEM)
    vmem = pl.BlockSpec(memory_space=pltpu.VMEM)
    hbm = pl.BlockSpec(memory_space=pltpu.HBM)
    sem_counts = [12, (3, 3), (3, 3), (n_g - 1, 3), 1, (n_z, 3), (n_z, 3), (n_z - 1, 3), (n_z - 1, 3),
                  3, 3, (n_z - 1, 3), (n_z - 1, 3), (n_z, 3), 1,
                  1, 1, 1, 1, n_g - 1, n_g - 1, 3, 3, 2 * n_g - 1, 2 * n_g - 1, n_z - 1, n_z - 1, n_g - 1, n_g - 1]
    act, fg, wg = pl.pallas_call(
        functools.partial(kernel, n_row, n_z, slots, node_dev * n_row * n_col),
        out_shape=[
            jax.ShapeDtypeStruct((3, 2, 64, out), BF16),
            jax.ShapeDtypeStruct((width, node_dev), BF16),
            jax.ShapeDtypeStruct((width, out), F32),
        ],
        in_specs=[hbm, hbm, smem, hbm, hbm, hbm, hbm],
        out_specs=[vmem] * 3,
        scratch_shapes=[
            pltpu.SMEM((1, slots), jnp.int32),
            pltpu.SMEM((1, slots), jnp.int32),
            pltpu.VMEM((2, 1, slots), jnp.int32),
            pltpu.VMEM((8, 128), jnp.int32),
            pltpu.SMEM((8, 128), jnp.int32),
            pltpu.VMEM((width, node_dev), BF16),
            pltpu.VMEM((width, out), BF16),
            pltpu.VMEM((slots, 64, 128), BF16),
            pltpu.VMEM((3, 64, 128), BF16),
            pltpu.VMEM((4, 3, 64, 128), BF16),
            pltpu.VMEM((3, 3, 64, 128), BF16),
            pltpu.VMEM((3 * n_g, 64, 128), BF16),
            pltpu.VMEM((slots + 1, 64, 128), F32),
            pltpu.VMEM((n_col, 3, 64, 128), BF16),
            pltpu.VMEM((n_z, 3, 64, 128), BF16),
            pltpu.VMEM((n_z - 1, 3, 64, 128), BF16),
            pltpu.VMEM((n_z - 1, 3, 64, 128), BF16),
            pltpu.VMEM((3 * n_col, 64, 128), BF16),
            pltpu.VMEM((3, 64, 128), BF16),
            pltpu.VMEM((slots + 1, 128, 128), F32),
            pltpu.VMEM((2, 3 * n_g, 64, 128), BF16),
            pltpu.VMEM((n_g - 1, 3, 64, 128), BF16),
            pltpu.VMEM((4, 3, 64, 128), BF16),
            pltpu.VMEM((2, width, n_row * node_dev), BF16),
            pltpu.VMEM((2, n_g, piece_rows, 128), BF16),
            pltpu.VMEM((2 * n_g - 1, piece_rows, 128), BF16),
            pltpu.VMEM((n_z, piece_rows, 128), BF16),
            pltpu.VMEM((piece_rows, 128), F32),
            pltpu.SemaphoreType.REGULAR((3,)),
        ] + [dma(n if isinstance(n, tuple) else (n,)) for n in sem_counts],
        compiler_params=pltpu.CompilerParams(
            collective_id=0, has_side_effects=True, vmem_limit_bytes=40 * 1024 * 1024),
    )(
        pin(tile_rows.reshape(1, slots)), pin(tile_cols.reshape(1, slots)), tile_count,
        pin(features.T), pin(weight), pin(tile_values.reshape(slots, 2, 64, 128)), pin(cotangent.reshape(3, 2, 64, out)),
    )
    return act.reshape(node_dev, out), fg.T.reshape(1, node_dev, width), wg


def solution(mesh):
    return jax.shard_map(
        functools.partial(shards, mesh.shape["row"], mesh.shape["col"] // 2),
        mesh=mesh,
        in_specs=(
            P("col", "feat"),
            P("feat", None),
            P("row", "col", None, None, None),
            P("row", "col", None),
            P("row", "col", None),
            P("row", "col"),
            P(("row", "col"), None),
        ),
        out_specs=(P(("row", "col"), None), P("col", "row", "feat"), P("feat", None)),
        check_vma=False,
    )
```

```python
import functools
import math

import jax
import jax.numpy as jnp
from jax import lax
from jax.experimental import pallas as pl
from jax.experimental.pallas import tpu as pltpu
from jax.sharding import PartitionSpec as P

MESH = pl.DeviceIdType.MESH
F32 = jnp.float32
BF16 = jnp.bfloat16


def far_first(n):
    return sorted(range(1, n), key=lambda k: (-min(k, n - k), k))


def kernel(
    n_row, n_z, slots, total_nodes,
    rows_hbm, cols_hbm, count_s, feat_hbm, w_hbm, tiles_hbm, cot_hbm,
    act_out, fg_out, wg_out,
    rows_s, cols_s, keys_v, links_v, links_s,
    x_v, w_ref, tiles_v, cot_v,
    y_send, y_recv, y_buf, prod_f,
    s_buf, yh_recv, t_buf, z_recv, hg_buf, act_v,
    prod_b, b_both, b_recv, b_full,
    xt_both, u_send, u_recv, v_buf, wg_piece,
    here_sem, in_sem, p1_s, p1_r, p2_s, p2_r, p3a_s, p3a_r, p3b_s, p3b_r,
    act_s, act_r, p4z_s, p4z_r, p4y_s, p4y_r, xg_s, xg_r, bc_s, bc_r, p5_s, p5_r, p6_s, p6_r,
    k1_s, k1_r, k2_s, k2_r, k3_s, k3_r,
):
    f = lax.axis_index("feat")
    r = lax.axis_index("row")
    c = lax.axis_index("col")
    y_low, b = f // 2, f % 2
    z, h = c // 2, c % 2
    a = (y_low + h) % 2
    n_g = 2 * n_row

    def feat_of(role, core):
        return ((role + h) % 2) * 2 + core

    def remote(src, dst, send, recv, device):
        return pltpu.make_async_remote_copy(
            src_ref=src, dst_ref=dst, send_sem=send, recv_sem=recv, device_id=device, device_id_type=MESH
        )

    feat_peers = [{"feat": (f + k) % 4} for k in range(1, 4)]

    def g_peer(k):
        g2 = (2 * r + a + k) % n_g
        return g2, {"feat": feat_of(g2 % 2, b), "row": g2 // 2}

    def u_peer(k):
        u2 = (2 * r + h + k) % n_g
        return u2, {"row": u2 // 2, "col": 2 * z + u2 % 2}

    def z_peer(k):
        return {"col": 2 * ((z + k) % n_z) + h}

    y_partner = {"feat": (f + 2) % 4, "col": c + 1 - 2 * h}

    node_dev = x_v.shape[1]
    in_x = pltpu.make_async_copy(
        feat_hbm.at[:, pl.ds(pl.multiple_of(r * node_dev, node_dev), node_dev)], x_v, in_sem.at[0])
    in_w = pltpu.make_async_copy(w_hbm, w_ref, in_sem.at[5])
    in_keys = [
        pltpu.make_async_copy(rows_hbm, keys_v.at[0], in_sem.at[6]),
        pltpu.make_async_copy(cols_hbm, keys_v.at[1], in_sem.at[7]),
        pltpu.make_async_copy(rows_hbm, rows_s, in_sem.at[8]),
        pltpu.make_async_copy(cols_hbm, cols_s, in_sem.at[9]),
    ]
    in_t = pltpu.make_async_copy(tiles_hbm.at[:, a], tiles_v, in_sem.at[1])
    in_c = pltpu.make_async_copy(
        cot_hbm.at[:, a, :, pl.ds(pl.multiple_of(b * 128, 128), 128)], cot_v, in_sem.at[2])
    in_x.start()
    in_w.start()

    barrier = pltpu.get_barrier_semaphore()
    peers = list(feat_peers)
    x_sides = (1, n_row - 1) if n_row > 1 else ()
    for k in x_sides:
        peers.append({"row": (r + k) % n_row})
        peers.append({"feat": (f + 2) % 4, "row": (r + k) % n_row})
    peers += [z_peer(k) for k in (1, n_z - 1)]
    peers.append(y_partner)
    for peer in reversed(peers):
        pl.semaphore_signal(barrier, inc=1, device_id=peer, device_id_type=MESH)
    for cp in in_keys:
        cp.start()
    in_t.start()
    in_c.start()
    in_xt = pltpu.make_async_copy(feat_hbm, xt_both.at[y_low], in_sem.at[11])
    in_xt.start()

    in_x.wait()
    in_w.wait()
    y_part = lax.dot_general(
        x_v[...], w_ref[...], (((0,), (0,)), ((), ())), preferred_element_type=F32).astype(BF16)
    for q in range(2):
        for core in range(2):
            y_send[2 * q + core] = y_part[192 * q:192 * (q + 1), 128 * core:128 * (core + 1)].reshape(3, 64, 128)
    pl.semaphore_wait(barrier, len(peers))
    for k in (1, n_z - 1):
        pl.semaphore_signal(here_sem.at[0], inc=1, device_id=z_peer(k), device_id_type=MESH)
    for k in x_sides:
        pl.semaphore_signal(here_sem.at[2], inc=1, device_id={"row": (r + k) % n_row}, device_id_type=MESH)

    copies = []
    p1 = [[], [], []]
    for w in range(3):
        for k in range(1, 4):
            f2 = (f + k) % 4
            piece = ((f2 // 2 + h) % 2) * 2 + f2 % 2
            cp = remote(y_send.at[piece, w], y_recv.at[k - 1, w], p1_s.at[k - 1, w], p1_r.at[k - 1, w], feat_peers[k - 1])
            cp.start()
            copies.append(cp)
            p1[w].append(cp)
    for cp in in_keys:
        cp.wait()
    ids = lax.broadcasted_iota(jnp.int32, (slots, 128), 0)
    lanes = lax.broadcasted_iota(jnp.int32, (slots, 128), 1)
    live = ids < count_s[0, 0]
    for i in range(2):
        across = jnp.broadcast_to(keys_v[i], (slots, slots))
        across = jnp.concatenate([across, jnp.zeros((slots, 128 - slots), jnp.int32)], axis=1)
        down = jnp.sum(jnp.where(ids == lanes, across, 0), axis=1, keepdims=True)
        down = jnp.broadcast_to(down, (slots, 128))
        before = jnp.where(live & (ids < lanes) & (down == across), ids, -1)
        there = jnp.where(live & (down == lanes), ids, -1)
        for w, found in ((0, before), (1, there)):
            top = jnp.max(found, axis=0, keepdims=True)
            links_v[pl.ds(2 * i + w, 1), :] = jnp.where(top < 0, slots, top)
    links = pltpu.make_async_copy(links_v, links_s, in_sem.at[10])
    links.start()
    pl.semaphore_wait(here_sem.at[0], 2)
    if x_sides:
        pl.semaphore_wait(here_sem.at[2], 2)
    for k in (2, n_z - 2):
        pl.semaphore_signal(here_sem.at[1], inc=1, device_id=z_peer(k), device_id_type=MESH)

    g = 2 * r + a
    p2 = []
    g_order = sorted(range(1, n_g), key=lambda k: -min(k, n_g - k))
    for w in range(3):
        total = y_send[2 * a + b, w].astype(F32)
        for k in range(3):
            p1[w][k].wait_recv()
            total = total + y_recv[k, w].astype(F32)
        y_buf[3 * g + w] = total.astype(BF16)
        mine = y_buf.at[3 * g + w]
        for k in g_order:
            _, dev = g_peer(k)
            cp = remote(mine, mine, p2_s.at[k - 1, w], p2_r.at[0], dev)
            cp.start()
            p2.append(cp)
    prod_f[slots] = jnp.zeros((64, 128), F32)
    prod_b[slots] = jnp.zeros((128, 128), F32)
    in_t.wait()
    links.wait()
    got = y_buf.at[pl.ds(0, 3 * (n_g - 1))]
    remote(got, got, p2_s.at[0, 0], p2_r.at[0], y_partner).wait_recv()

    pl.semaphore_wait(here_sem.at[1], 2)

    xg = remote(feat_hbm, xt_both.at[y_low], xg_s.at[0], xg_r.at[0], {"feat": (f + 2) % 4})
    xg.start()

    def forward(s, _):
        block = y_buf[pl.ds(2 * cols_s[0, s], 2)].reshape(128, 128)
        prod_f[s] = jnp.dot(tiles_v[s], block, preferred_element_type=F32) + prod_f[links_s[0, s]]
        return 0

    lax.fori_loop(0, slots, forward, 0, unroll=32)

    def fill(c2, w):
        s_buf[c2, w] = prod_f[links_s[1, 3 * c2 + w]].astype(BF16)

    sent = []

    def send(src, dst, send_sem, recv_sem, device):
        cp = remote(src, dst, send_sem, recv_sem, device)
        cp.start()
        sent.append(cp)
        return cp

    offs = far_first(n_z) + [0]
    p3a = [[], [], []]
    for w in range(3):
        for j, off in enumerate(offs):
            c2 = 2 * ((z + off) % n_z) + 1 - h
            fill(c2, w)
            p3a[w].append(send(s_buf.at[c2, w], yh_recv.at[j, w], p3a_s.at[j, w], p3a_r.at[j, w], y_partner))
    for w in range(3):
        for off in offs:
            fill(2 * ((z + off) % n_z) + h, w)
    p3b = [[], [], []]
    own_part = [None] * 3

    def sum_h(w):
        for j, off in enumerate(offs):
            c2 = 2 * ((z + off) % n_z) + h
            p3a[w][j].wait_recv()
            both = s_buf[c2, w].astype(F32) + yh_recv[j, w].astype(F32)
            if off:
                t_buf[j, w] = both.astype(BF16)
                p3b[w].append(send(t_buf.at[j, w], z_recv.at[j, w], p3b_s.at[j, w], p3b_r.at[w], z_peer(off)))
            else:
                own_part[w] = both

    def place(dist, w):
        return hg_buf.at[3 * (2 * ((z + 2 * n_z - dist) % n_z) + h) + w]

    def z_send(what, j, off, w):
        send(what, what, p4z_s.at[j, w], p4z_r.at[j, w], z_peer(off))

    def y_send_on(what, j, w):
        send(what, what, p4y_s.at[j, w], p4y_r.at[0], y_partner)

    def arrived(j, dist, w):
        got = place(dist, w)
        remote(got, got, p4z_s.at[j, w], p4z_r.at[j, w], y_partner).wait_recv()
        return got

    def activate(w):
        hidden = own_part[w]
        got = z_recv.at[pl.ds(0, n_z - 1), w]
        remote(got, got, p3b_s.at[0, w], p3b_r.at[w], y_partner).wait_recv()
        for j in range(n_z - 1):
            hidden = hidden + z_recv[j, w].astype(F32)
        sigma = jax.nn.sigmoid(hidden)
        grad = cot_v[w].astype(F32) * (sigma * (1.0 + hidden * (1.0 - sigma)))
        hg_buf[3 * c + w] = grad.astype(BF16)
        act_v[w] = (hidden * sigma).astype(BF16)
        own = hg_buf.at[3 * c + w]
        if w == 2:
            z_send(own, 6, 4, w)
            z_send(own, 4, 3, w)
            z_send(own, 5, n_z - 3, w)
        z_send(own, 2, 2, w)
        z_send(own, 3, n_z - 2, w)
        z_send(own, 0, 1, w)
        z_send(own, 1, n_z - 1, w)
        y_send_on(own, n_z - 1, w)

    side = 1 - 2 * (z % 2)

    def pass_on(w):
        if w < 2:
            plus = arrived(2, 2, w)
            z_send(plus, 4, 1, w)
            minus = arrived(3, n_z - 2, w)
            z_send(minus, 5, n_z - 1, w)
            z_send(place(2 * side + n_z, w), 6, 2 * side + n_z, w)
        y_send_on(arrived(0, 1, w), 0, w)
        y_send_on(arrived(1, n_z - 1, w), 1, w)
        if w == 2:
            plus = arrived(2, 2, w)
            minus = arrived(3, n_z - 2, w)
        y_send_on(plus, 2, w)
        y_send_on(minus, 3, w)

    def last_on(w):
        y_send_on(arrived(4, 3, w), 4, w)
        y_send_on(arrived(5, n_z - 3, w), 5, w)
        y_send_on(arrived(6, 4, w), 6, w)

    in_c.wait()
    sum_h(0)
    sum_h(1)
    activate(0)
    sum_h(2)
    activate(1)
    pass_on(0)
    activate(2)
    act_cols = pl.ds(pl.multiple_of(b * 128, 128), 128)
    act_dst = act_out.at[:, a, :, act_cols]
    local = pltpu.make_async_copy(act_v, act_dst, in_sem.at[3])
    local.start()
    pass_on(1)
    last_on(0)
    pass_on(2)
    last_on(1)
    last_on(2)
    acts = []
    for k in range(1, 4):
        cp = remote(act_v, act_dst, act_s.at[k - 1], act_r.at[k - 1], feat_peers[k - 1])
        cp.start()
        acts.append(cp)
    got = hg_buf.at[pl.ds(0, 3 * n_z)]
    remote(got, got, p4y_s.at[0, 0], p4y_r.at[0], y_partner).wait_recv()

    def backward(s, _):
        prod_b[s] = lax.dot_general(
            tiles_v[s], hg_buf[rows_s[0, s]], (((0,), (0,)), ((), ())), preferred_element_type=F32) + prod_b[links_s[2, s]]
        return 0

    lax.fori_loop(0, slots, backward, 0, unroll=32)

    for j in range(3 * n_row):
        b_both[b, pl.ds(2 * j, 2)] = prod_b[links_s[3, j]].astype(BF16).reshape(2, 64, 128)

    bc = remote(b_both.at[b], b_both.at[b], bc_s.at[0], bc_r.at[0], {"feat": f + 1 - 2 * b})
    bc.start()

    piece_rows = u_send.shape[2]
    in_xt.wait()
    xg.wait_recv()
    got = b_both.at[1 - b]
    remote(got, got, bc_s.at[0], bc_r.at[0], y_partner).wait_recv()
    both = jnp.concatenate([b_both[0].reshape(n_row * node_dev, 128), b_both[1].reshape(n_row * node_dev, 128)], axis=1)
    for low in range(2):
        part = jnp.dot(xt_both[low], both, preferred_element_type=F32).astype(BF16)
        for core in range(2):
            u_send[low, n_row * core:n_row * (core + 1)] = part[:, 128 * core:128 * (core + 1)].reshape(
                n_row, piece_rows, 128)
    u = 2 * r + h
    k1 = []
    for k in range(1, 2 * n_g):
        q2 = (n_g * y_low + u + k) % (2 * n_g)
        low2, u2 = q2 // n_g, q2 % n_g
        dev = {"feat": 2 * low2 + b, "row": u2 // 2, "col": 2 * z + u2 % 2}
        cp = remote(u_send.at[low2, u2], u_recv.at[k - 1], k1_s.at[k - 1], k1_r.at[0], dev)
        cp.start()
        k1.append(cp)

    p5 = []
    for k in range(1, n_g):
        g2, dev = g_peer(k)
        cp = remote(b_both.at[b, pl.ds(3 * g2, 3)], b_recv.at[k - 1], p5_s.at[k - 1], p5_r.at[0], dev)
        cp.start()
        p5.append(cp)

    total = u_send[y_low, u].astype(F32)
    remote(u_recv, u_recv, k1_s.at[0], k1_r.at[0], y_partner).wait_recv()
    for k in range(2 * n_g - 1):
        total = total + u_recv[k].astype(F32)
    v_buf[z] = total.astype(BF16)
    k2 = []
    for j, off in enumerate(offs[:-1]):
        cp = remote(v_buf.at[z], v_buf.at[z], k2_s.at[j], k2_r.at[0], z_peer(off))
        cp.start()
        k2.append(cp)
    for cp in copies + p2 + sent + acts + p5 + k1 + [xg, bc]:
        cp.wait_send()

    total = b_both[b, pl.ds(3 * g, 3)].astype(F32)
    remote(b_recv, b_recv, p5_s.at[0], p5_r.at[0], y_partner).wait_recv()
    for k in range(n_g - 1):
        total = total + b_recv[k].astype(F32)
    b_full[2 * b + a] = total.astype(BF16)
    mine = b_full.at[2 * b + a]
    p6 = []
    for k in range(1, 4):
        cp = remote(mine, mine, p6_s.at[k - 1], p6_r.at[k - 1], feat_peers[k - 1])
        cp.start()
        p6.append(cp)

    got = v_buf.at[pl.ds(0, n_z - 1)]
    remote(got, got, k2_s.at[0], k2_r.at[0], y_partner).wait_recv()
    total = v_buf[0].astype(F32)
    for j in range(1, n_z):
        total = total + v_buf[j].astype(F32)
    wg_piece[...] = total * (1.0 / math.sqrt(total_nodes))

    def wg_place(piece):
        return wg_out.at[
            pl.ds(pl.multiple_of((piece % n_row) * piece_rows, piece_rows), piece_rows),
            pl.ds(pl.multiple_of((piece // n_row) * 128, 128), 128),
        ]

    local_wg = pltpu.make_async_copy(wg_piece, wg_place(u), in_sem.at[4])
    local_wg.start()
    k3 = []
    for k in range(1, n_g):
        _, dev = u_peer(k)
        cp = remote(wg_piece, wg_place(u), k3_s.at[k - 1], k3_r.at[k - 1], dev)
        cp.start()
        k3.append(cp)
    for k in range(1, 4):
        f2 = (f + 4 - k) % 4
        got = b_full.at[2 * (f2 % 2) + (f2 // 2 + h) % 2]
        remote(got, got, p6_s.at[k - 1], p6_r.at[k - 1], y_partner).wait_recv()
    grad_t = jnp.zeros((w_ref.shape[0], node_dev), F32)
    for core in range(2):
        grad_t = grad_t + lax.dot_general(
            w_ref[:, 128 * core:128 * (core + 1)], b_full[2 * core:2 * core + 2].reshape(node_dev, 128),
            (((1,), (1,)), ((), ())), preferred_element_type=F32)
    fg_out[...] = grad_t.astype(BF16)

    for k in range(1, n_g):
        got = wg_place((u + n_g - k) % n_g)
        remote(wg_piece, got, k3_s.at[k - 1], k3_r.at[k - 1], y_partner).wait_recv()
    for k in range(1, 4):
        f2 = (f + 4 - k) % 4
        got = act_out.at[:, (f2 // 2 + h) % 2, :, pl.ds(pl.multiple_of((f2 % 2) * 128, 128), 128)]
        remote(act_v, got, act_s.at[k - 1], act_r.at[k - 1], y_partner).wait_recv()
    local.wait()
    local_wg.wait()
    for cp in p6 + k2 + k3:
        cp.wait_send()


def shards(n_row, n_z, features, weight, tile_values, tile_rows, tile_cols, tile_count, cotangent):
    slots = tile_values.shape[2]
    node_dev, out = cotangent.shape
    width = features.shape[1]
    n_g = 2 * n_row
    n_col = 2 * n_z
    piece_rows = 2 * width // n_g
    dma = pltpu.SemaphoreType.DMA
    pin = lambda x: pltpu.with_memory_space_constraint(x, pltpu.HBM)
    smem = pl.BlockSpec(memory_space=pltpu.SMEM)
    vmem = pl.BlockSpec(memory_space=pltpu.VMEM)
    hbm = pl.BlockSpec(memory_space=pltpu.HBM)
    sem_counts = [12, (3, 3), (3, 3), (n_g - 1, 3), 1, (n_z, 3), (n_z, 3), (n_z - 1, 3), 3,
                  3, 3, (n_z - 1, 3), (n_z - 1, 3), (n_z, 3), 1,
                  1, 1, 1, 1, n_g - 1, 1, 3, 3, 2 * n_g - 1, 1, n_z - 1, 1, n_g - 1, n_g - 1]
    act, fg, wg = pl.pallas_call(
        functools.partial(kernel, n_row, n_z, slots, node_dev * n_row * n_col),
        out_shape=[
            jax.ShapeDtypeStruct((3, 2, 64, out), BF16),
            jax.ShapeDtypeStruct((width, node_dev), BF16),
            jax.ShapeDtypeStruct((width, out), F32),
        ],
        in_specs=[hbm, hbm, smem, hbm, hbm, hbm, hbm],
        out_specs=[vmem] * 3,
        scratch_shapes=[
            pltpu.SMEM((1, slots), jnp.int32),
            pltpu.SMEM((1, slots), jnp.int32),
            pltpu.VMEM((2, 1, slots), jnp.int32),
            pltpu.VMEM((8, 128), jnp.int32),
            pltpu.SMEM((8, 128), jnp.int32),
            pltpu.VMEM((width, node_dev), BF16),
            pltpu.VMEM((width, out), BF16),
            pltpu.VMEM((slots, 64, 128), BF16),
            pltpu.VMEM((3, 64, 128), BF16),
            pltpu.VMEM((4, 3, 64, 128), BF16),
            pltpu.VMEM((3, 3, 64, 128), BF16),
            pltpu.VMEM((3 * n_g, 64, 128), BF16),
            pltpu.VMEM((slots + 1, 64, 128), F32),
            pltpu.VMEM((n_col, 3, 64, 128), BF16),
            pltpu.VMEM((n_z, 3, 64, 128), BF16),
            pltpu.VMEM((n_z - 1, 3, 64, 128), BF16),
            pltpu.VMEM((n_z - 1, 3, 64, 128), BF16),
            pltpu.VMEM((3 * n_col, 64, 128), BF16),
            pltpu.VMEM((3, 64, 128), BF16),
            pltpu.VMEM((slots + 1, 128, 128), F32),
            pltpu.VMEM((2, 3 * n_g, 64, 128), BF16),
            pltpu.VMEM((n_g - 1, 3, 64, 128), BF16),
            pltpu.VMEM((4, 3, 64, 128), BF16),
            pltpu.VMEM((2, width, n_row * node_dev), BF16),
            pltpu.VMEM((2, n_g, piece_rows, 128), BF16),
            pltpu.VMEM((2 * n_g - 1, piece_rows, 128), BF16),
            pltpu.VMEM((n_z, piece_rows, 128), BF16),
            pltpu.VMEM((piece_rows, 128), F32),
            pltpu.SemaphoreType.REGULAR((3,)),
        ] + [dma(n if isinstance(n, tuple) else (n,)) for n in sem_counts],
        compiler_params=pltpu.CompilerParams(
            collective_id=0, has_side_effects=True, vmem_limit_bytes=40 * 1024 * 1024),
    )(
        pin(tile_rows.reshape(1, slots)), pin(tile_cols.reshape(1, slots)), tile_count,
        pin(features.T), pin(weight), pin(tile_values.reshape(slots, 2, 64, 128)), pin(cotangent.reshape(3, 2, 64, out)),
    )
    return act.reshape(node_dev, out), fg.T.reshape(1, node_dev, width), wg


def solution(mesh):
    return jax.shard_map(
        functools.partial(shards, mesh.shape["row"], mesh.shape["col"] // 2),
        mesh=mesh,
        in_specs=(
            P("col", "feat"),
            P("feat", None),
            P("row", "col", None, None, None),
            P("row", "col", None),
            P("row", "col", None),
            P("row", "col"),
            P(("row", "col"), None),
        ),
        out_specs=(P(("row", "col"), None), P("col", "row", "feat"), P("feat", None)),
        check_vma=False,
    )
```

```python
import functools
import math

import jax
import jax.numpy as jnp
from jax import lax
from jax.experimental import pallas as pl
from jax.experimental.pallas import tpu as pltpu
from jax.sharding import PartitionSpec as P

MESH = pl.DeviceIdType.MESH
F32 = jnp.float32
BF16 = jnp.bfloat16


def far_first(n):
    return sorted(range(1, n), key=lambda k: (-min(k, n - k), k))


def kernel(
    n_row, n_z, slots, total_nodes,
    rows_hbm, cols_hbm, count_s, feat_hbm, w_hbm, tiles_hbm, cot_hbm,
    act_out, fg_out, wg_out,
    rows_s, cols_s, keys_v, links_v, links_s,
    x_v, w_ref, tiles_v, cot_v,
    y_send, y_recv, y_buf, prod_f,
    s_buf, yh_recv, t_buf, z_recv, hg_buf, act_v,
    prod_b, b_both, b_recv, b_full,
    xt_both, u_send, u_recv, v_buf, wg_piece,
    here_sem, in_sem, p1_s, p1_r, p2_s, p2_r, p3a_s, p3a_r, p3b_s, p3b_r,
    act_s, act_r, p4z_s, p4z_r, p4y_s, p4y_r, xg_s, xg_r, bc_s, bc_r, p5_s, p5_r, p6_s, p6_r,
    k1_s, k1_r, k2_s, k2_r, k3_s, k3_r,
):
    f = lax.axis_index("feat")
    r = lax.axis_index("row")
    c = lax.axis_index("col")
    y_low, b = f // 2, f % 2
    z, h = c // 2, c % 2
    a = (y_low + h) % 2
    n_g = 2 * n_row

    def feat_of(role, core):
        return ((role + h) % 2) * 2 + core

    def remote(src, dst, send, recv, device):
        return pltpu.make_async_remote_copy(
            src_ref=src, dst_ref=dst, send_sem=send, recv_sem=recv, device_id=device, device_id_type=MESH
        )

    feat_peers = [{"feat": (f + k) % 4} for k in range(1, 4)]

    def g_peer(k):
        g2 = (2 * r + a + k) % n_g
        return g2, {"feat": feat_of(g2 % 2, b), "row": g2 // 2}

    def u_peer(k):
        u2 = (2 * r + h + k) % n_g
        return u2, {"row": u2 // 2, "col": 2 * z + u2 % 2}

    def z_peer(k):
        return {"col": 2 * ((z + k) % n_z) + h}

    y_partner = {"feat": (f + 2) % 4, "col": c + 1 - 2 * h}

    node_dev = x_v.shape[1]
    in_x = pltpu.make_async_copy(
        feat_hbm.at[:, pl.ds(pl.multiple_of(r * node_dev, node_dev), node_dev)], x_v, in_sem.at[0])
    in_w = pltpu.make_async_copy(w_hbm, w_ref, in_sem.at[5])
    in_keys = [
        pltpu.make_async_copy(rows_hbm, keys_v.at[0], in_sem.at[6]),
        pltpu.make_async_copy(cols_hbm, keys_v.at[1], in_sem.at[7]),
        pltpu.make_async_copy(rows_hbm, rows_s, in_sem.at[8]),
        pltpu.make_async_copy(cols_hbm, cols_s, in_sem.at[9]),
    ]
    in_t = pltpu.make_async_copy(tiles_hbm.at[:, a], tiles_v, in_sem.at[1])
    in_c = pltpu.make_async_copy(
        cot_hbm.at[:, a, :, pl.ds(pl.multiple_of(b * 128, 128), 128)], cot_v, in_sem.at[2])
    in_x.start()
    in_w.start()

    barrier = pltpu.get_barrier_semaphore()
    peers = list(feat_peers)
    x_sides = (1, n_row - 1) if n_row > 1 else ()
    for k in x_sides:
        peers.append({"row": (r + k) % n_row})
        peers.append({"feat": (f + 2) % 4, "row": (r + k) % n_row})
    peers += [z_peer(k) for k in (1, n_z - 1)]
    peers.append(y_partner)
    for peer in reversed(peers):
        pl.semaphore_signal(barrier, inc=1, device_id=peer, device_id_type=MESH)
    for cp in in_keys:
        cp.start()
    in_t.start()
    in_c.start()
    in_xt = pltpu.make_async_copy(feat_hbm, xt_both.at[y_low], in_sem.at[11])
    in_xt.start()

    in_x.wait()
    in_w.wait()
    y_part = lax.dot_general(
        x_v[...], w_ref[...], (((0,), (0,)), ((), ())), preferred_element_type=F32).astype(BF16)
    for q in range(2):
        for core in range(2):
            y_send[2 * q + core] = y_part[192 * q:192 * (q + 1), 128 * core:128 * (core + 1)].reshape(3, 64, 128)
    pl.semaphore_wait(barrier, len(peers))
    for k in (1, n_z - 1):
        pl.semaphore_signal(here_sem.at[0], inc=1, device_id=z_peer(k), device_id_type=MESH)
    for k in x_sides:
        pl.semaphore_signal(here_sem.at[2], inc=1, device_id={"row": (r + k) % n_row}, device_id_type=MESH)

    copies = []
    for w in range(3):
        for k in range(1, 4):
            f2 = (f + k) % 4
            piece = ((f2 // 2 + h) % 2) * 2 + f2 % 2
            cp = remote(y_send.at[piece, w], y_recv.at[k - 1, w], p1_s.at[k - 1, w], p1_r.at[w], feat_peers[k - 1])
            cp.start()
            copies.append(cp)
    for cp in in_keys:
        cp.wait()
    ids = lax.broadcasted_iota(jnp.int32, (slots, 128), 0)
    lanes = lax.broadcasted_iota(jnp.int32, (slots, 128), 1)
    live = ids < count_s[0, 0]
    for i in range(2):
        across = jnp.broadcast_to(keys_v[i], (slots, slots))
        across = jnp.concatenate([across, jnp.zeros((slots, 128 - slots), jnp.int32)], axis=1)
        down = jnp.sum(jnp.where(ids == lanes, across, 0), axis=1, keepdims=True)
        down = jnp.broadcast_to(down, (slots, 128))
        before = jnp.where(live & (ids < lanes) & (down == across), ids, -1)
        there = jnp.where(live & (down == lanes), ids, -1)
        for w, found in ((0, before), (1, there)):
            top = jnp.max(found, axis=0, keepdims=True)
            links_v[pl.ds(2 * i + w, 1), :] = jnp.where(top < 0, slots, top)
    links = pltpu.make_async_copy(links_v, links_s, in_sem.at[10])
    links.start()
    pl.semaphore_wait(here_sem.at[0], 2)
    if x_sides:
        pl.semaphore_wait(here_sem.at[2], 2)
    for k in (2, n_z - 2):
        pl.semaphore_signal(here_sem.at[1], inc=1, device_id=z_peer(k), device_id_type=MESH)

    g = 2 * r + a
    p2 = []
    g_order = sorted(range(1, n_g), key=lambda k: -min(k, n_g - k))
    for w in range(3):
        total = y_send[2 * a + b, w].astype(F32)
        got = y_recv.at[:, w]
        remote(got, got, p1_s.at[0, w], p1_r.at[w], y_partner).wait_recv()
        for k in range(3):
            total = total + y_recv[k, w].astype(F32)
        y_buf[3 * g + w] = total.astype(BF16)
        mine = y_buf.at[3 * g + w]
        for k in g_order:
            _, dev = g_peer(k)
            cp = remote(mine, mine, p2_s.at[k - 1, w], p2_r.at[0], dev)
            cp.start()
            p2.append(cp)
    prod_f[slots] = jnp.zeros((64, 128), F32)
    prod_b[slots] = jnp.zeros((128, 128), F32)
    in_t.wait()
    links.wait()
    got = y_buf.at[pl.ds(0, 3 * (n_g - 1))]
    remote(got, got, p2_s.at[0, 0], p2_r.at[0], y_partner).wait_recv()

    pl.semaphore_wait(here_sem.at[1], 2)

    xg = remote(feat_hbm, xt_both.at[y_low], xg_s.at[0], xg_r.at[0], {"feat": (f + 2) % 4})
    xg.start()

    def forward(s, _):
        block = y_buf[pl.ds(2 * cols_s[0, s], 2)].reshape(128, 128)
        prod_f[s] = jnp.dot(tiles_v[s], block, preferred_element_type=F32) + prod_f[links_s[0, s]]
        return 0

    lax.fori_loop(0, slots, forward, 0, unroll=32)

    def fill(c2, w):
        s_buf[c2, w] = prod_f[links_s[1, 3 * c2 + w]].astype(BF16)

    sent = []

    def send(src, dst, send_sem, recv_sem, device):
        cp = remote(src, dst, send_sem, recv_sem, device)
        cp.start()
        sent.append(cp)
        return cp

    offs = far_first(n_z) + [0]
    p3a = [[], [], []]
    for w in range(3):
        for j, off in enumerate(offs):
            c2 = 2 * ((z + off) % n_z) + 1 - h
            fill(c2, w)
            p3a[w].append(send(s_buf.at[c2, w], yh_recv.at[j, w], p3a_s.at[j, w], p3a_r.at[j, w], y_partner))
    for w in range(3):
        for off in offs:
            fill(2 * ((z + off) % n_z) + h, w)
    p3b = [[], [], []]
    own_part = [None] * 3

    def sum_h(w):
        for j, off in enumerate(offs):
            c2 = 2 * ((z + off) % n_z) + h
            p3a[w][j].wait_recv()
            both = s_buf[c2, w].astype(F32) + yh_recv[j, w].astype(F32)
            if off:
                t_buf[j, w] = both.astype(BF16)
                p3b[w].append(send(t_buf.at[j, w], z_recv.at[j, w], p3b_s.at[j, w], p3b_r.at[w], z_peer(off)))
            else:
                own_part[w] = both

    def place(dist, w):
        return hg_buf.at[3 * (2 * ((z + 2 * n_z - dist) % n_z) + h) + w]

    def z_send(what, j, off, w):
        send(what, what, p4z_s.at[j, w], p4z_r.at[j, w], z_peer(off))

    def y_send_on(what, j, w):
        send(what, what, p4y_s.at[j, w], p4y_r.at[0], y_partner)

    def arrived(j, dist, w):
        got = place(dist, w)
        remote(got, got, p4z_s.at[j, w], p4z_r.at[j, w], y_partner).wait_recv()
        return got

    def activate(w):
        hidden = own_part[w]
        got = z_recv.at[pl.ds(0, n_z - 1), w]
        remote(got, got, p3b_s.at[0, w], p3b_r.at[w], y_partner).wait_recv()
        for j in range(n_z - 1):
            hidden = hidden + z_recv[j, w].astype(F32)
        sigma = jax.nn.sigmoid(hidden)
        grad = cot_v[w].astype(F32) * (sigma * (1.0 + hidden * (1.0 - sigma)))
        hg_buf[3 * c + w] = grad.astype(BF16)
        act_v[w] = (hidden * sigma).astype(BF16)
        own = hg_buf.at[3 * c + w]
        if w == 2:
            z_send(own, 6, 4, w)
            z_send(own, 4, 3, w)
            z_send(own, 5, n_z - 3, w)
        z_send(own, 2, 2, w)
        z_send(own, 3, n_z - 2, w)
        z_send(own, 0, 1, w)
        z_send(own, 1, n_z - 1, w)
        y_send_on(own, n_z - 1, w)

    side = 1 - 2 * (z % 2)

    def pass_on(w):
        if w < 2:
            plus = arrived(2, 2, w)
            z_send(plus, 4, 1, w)
            minus = arrived(3, n_z - 2, w)
            z_send(minus, 5, n_z - 1, w)
            z_send(place(2 * side + n_z, w), 6, 2 * side + n_z, w)
        y_send_on(arrived(0, 1, w), 0, w)
        y_send_on(arrived(1, n_z - 1, w), 1, w)
        if w == 2:
            plus = arrived(2, 2, w)
            minus = arrived(3, n_z - 2, w)
        y_send_on(plus, 2, w)
        y_send_on(minus, 3, w)

    def last_on(w):
        y_send_on(arrived(4, 3, w), 4, w)
        y_send_on(arrived(5, n_z - 3, w), 5, w)
        y_send_on(arrived(6, 4, w), 6, w)

    in_c.wait()
    sum_h(0)
    sum_h(1)
    activate(0)
    sum_h(2)
    activate(1)
    pass_on(0)
    activate(2)
    act_cols = pl.ds(pl.multiple_of(b * 128, 128), 128)
    act_dst = act_out.at[:, a, :, act_cols]
    local = pltpu.make_async_copy(act_v, act_dst, in_sem.at[3])
    local.start()
    pass_on(1)
    last_on(0)
    pass_on(2)
    last_on(1)
    last_on(2)
    acts = []
    for k in range(1, 4):
        cp = remote(act_v, act_dst, act_s.at[k - 1], act_r.at[k - 1], feat_peers[k - 1])
        cp.start()
        acts.append(cp)
    got = hg_buf.at[pl.ds(0, 3 * n_z)]
    remote(got, got, p4y_s.at[0, 0], p4y_r.at[0], y_partner).wait_recv()

    def backward(s, _):
        prod_b[s] = lax.dot_general(
            tiles_v[s], hg_buf[rows_s[0, s]], (((0,), (0,)), ((), ())), preferred_element_type=F32) + prod_b[links_s[2, s]]
        return 0

    lax.fori_loop(0, slots, backward, 0, unroll=32)

    for j in range(3 * n_row):
        b_both[b, pl.ds(2 * j, 2)] = prod_b[links_s[3, j]].astype(BF16).reshape(2, 64, 128)

    bc = remote(b_both.at[b], b_both.at[b], bc_s.at[0], bc_r.at[0], {"feat": f + 1 - 2 * b})
    bc.start()

    piece_rows = u_send.shape[2]
    in_xt.wait()
    xg.wait_recv()
    got = b_both.at[1 - b]
    remote(got, got, bc_s.at[0], bc_r.at[0], y_partner).wait_recv()
    both = jnp.concatenate([b_both[0].reshape(n_row * node_dev, 128), b_both[1].reshape(n_row * node_dev, 128)], axis=1)
    for low in range(2):
        part = jnp.dot(xt_both[low], both, preferred_element_type=F32).astype(BF16)
        for core in range(2):
            u_send[low, n_row * core:n_row * (core + 1)] = part[:, 128 * core:128 * (core + 1)].reshape(
                n_row, piece_rows, 128)
    u = 2 * r + h
    k1 = []
    for k in range(1, 2 * n_g):
        q2 = (n_g * y_low + u + k) % (2 * n_g)
        low2, u2 = q2 // n_g, q2 % n_g
        dev = {"feat": 2 * low2 + b, "row": u2 // 2, "col": 2 * z + u2 % 2}
        cp = remote(u_send.at[low2, u2], u_recv.at[k - 1], k1_s.at[k - 1], k1_r.at[0], dev)
        cp.start()
        k1.append(cp)

    p5 = []
    for k in range(1, n_g):
        g2, dev = g_peer(k)
        cp = remote(b_both.at[b, pl.ds(3 * g2, 3)], b_recv.at[k - 1], p5_s.at[k - 1], p5_r.at[0], dev)
        cp.start()
        p5.append(cp)

    total = u_send[y_low, u].astype(F32)
    remote(u_recv, u_recv, k1_s.at[0], k1_r.at[0], y_partner).wait_recv()
    for k in range(2 * n_g - 1):
        total = total + u_recv[k].astype(F32)
    v_buf[z] = total.astype(BF16)
    k2 = []
    for j, off in enumerate(offs[:-1]):
        cp = remote(v_buf.at[z], v_buf.at[z], k2_s.at[j], k2_r.at[0], z_peer(off))
        cp.start()
        k2.append(cp)
    for cp in copies + p2 + sent + acts + p5 + k1 + [xg, bc]:
        cp.wait_send()

    total = b_both[b, pl.ds(3 * g, 3)].astype(F32)
    remote(b_recv, b_recv, p5_s.at[0], p5_r.at[0], y_partner).wait_recv()
    for k in range(n_g - 1):
        total = total + b_recv[k].astype(F32)
    b_full[2 * b + a] = total.astype(BF16)
    mine = b_full.at[2 * b + a]
    p6 = []
    for k in range(1, 4):
        cp = remote(mine, mine, p6_s.at[k - 1], p6_r.at[k - 1], feat_peers[k - 1])
        cp.start()
        p6.append(cp)

    got = v_buf.at[pl.ds(0, n_z - 1)]
    remote(got, got, k2_s.at[0], k2_r.at[0], y_partner).wait_recv()
    total = v_buf[0].astype(F32)
    for j in range(1, n_z):
        total = total + v_buf[j].astype(F32)
    wg_piece[...] = total * (1.0 / math.sqrt(total_nodes))

    def wg_place(piece):
        return wg_out.at[
            pl.ds(pl.multiple_of((piece % n_row) * piece_rows, piece_rows), piece_rows),
            pl.ds(pl.multiple_of((piece // n_row) * 128, 128), 128),
        ]

    local_wg = pltpu.make_async_copy(wg_piece, wg_place(u), in_sem.at[4])
    local_wg.start()
    k3 = []
    for k in range(1, n_g):
        _, dev = u_peer(k)
        cp = remote(wg_piece, wg_place(u), k3_s.at[k - 1], k3_r.at[0], dev)
        cp.start()
        k3.append(cp)
    for k in range(1, 4):
        f2 = (f + 4 - k) % 4
        got = b_full.at[2 * (f2 % 2) + (f2 // 2 + h) % 2]
        remote(got, got, p6_s.at[k - 1], p6_r.at[k - 1], y_partner).wait_recv()
    grad_t = jnp.zeros((w_ref.shape[0], node_dev), F32)
    for core in range(2):
        grad_t = grad_t + lax.dot_general(
            w_ref[:, 128 * core:128 * (core + 1)], b_full[2 * core:2 * core + 2].reshape(node_dev, 128),
            (((1,), (1,)), ((), ())), preferred_element_type=F32)
    fg_out[...] = grad_t.astype(BF16)

    for k in range(1, 4):
        f2 = (f + 4 - k) % 4
        got = act_out.at[:, (f2 // 2 + h) % 2, :, pl.ds(pl.multiple_of((f2 % 2) * 128, 128), 128)]
        remote(act_v, got, act_s.at[k - 1], act_r.at[k - 1], y_partner).wait_recv()
    local.wait()
    local_wg.wait()
    for cp in p6 + k2 + k3:
        cp.wait_send()
    got = wg_out.at[pl.ds(0, wg_out.shape[0] // n_g * (n_g - 1))]
    remote(got, got, k3_s.at[0], k3_r.at[0], y_partner).wait_recv()


def shards(n_row, n_z, features, weight, tile_values, tile_rows, tile_cols, tile_count, cotangent):
    slots = tile_values.shape[2]
    node_dev, out = cotangent.shape
    width = features.shape[1]
    n_g = 2 * n_row
    n_col = 2 * n_z
    piece_rows = 2 * width // n_g
    dma = pltpu.SemaphoreType.DMA
    pin = lambda x: pltpu.with_memory_space_constraint(x, pltpu.HBM)
    smem = pl.BlockSpec(memory_space=pltpu.SMEM)
    vmem = pl.BlockSpec(memory_space=pltpu.VMEM)
    hbm = pl.BlockSpec(memory_space=pltpu.HBM)
    sem_counts = [12, (3, 3), 3, (n_g - 1, 3), 1, (n_z, 3), (n_z, 3), (n_z - 1, 3), 3,
                  3, 3, (n_z - 1, 3), (n_z - 1, 3), (n_z, 3), 1,
                  1, 1, 1, 1, n_g - 1, 1, 3, 3, 2 * n_g - 1, 1, n_z - 1, 1, n_g - 1, 1]
    act, fg, wg = pl.pallas_call(
        functools.partial(kernel, n_row, n_z, slots, node_dev * n_row * n_col),
        out_shape=[
            jax.ShapeDtypeStruct((3, 2, 64, out), BF16),
            jax.ShapeDtypeStruct((width, node_dev), BF16),
            jax.ShapeDtypeStruct((width, out), F32),
        ],
        in_specs=[hbm, hbm, smem, hbm, hbm, hbm, hbm],
        out_specs=[vmem] * 3,
        scratch_shapes=[
            pltpu.SMEM((1, slots), jnp.int32),
            pltpu.SMEM((1, slots), jnp.int32),
            pltpu.VMEM((2, 1, slots), jnp.int32),
            pltpu.VMEM((8, 128), jnp.int32),
            pltpu.SMEM((8, 128), jnp.int32),
            pltpu.VMEM((width, node_dev), BF16),
            pltpu.VMEM((width, out), BF16),
            pltpu.VMEM((slots, 64, 128), BF16),
            pltpu.VMEM((3, 64, 128), BF16),
            pltpu.VMEM((4, 3, 64, 128), BF16),
            pltpu.VMEM((3, 3, 64, 128), BF16),
            pltpu.VMEM((3 * n_g, 64, 128), BF16),
            pltpu.VMEM((slots + 1, 64, 128), F32),
            pltpu.VMEM((n_col, 3, 64, 128), BF16),
            pltpu.VMEM((n_z, 3, 64, 128), BF16),
            pltpu.VMEM((n_z - 1, 3, 64, 128), BF16),
            pltpu.VMEM((n_z - 1, 3, 64, 128), BF16),
            pltpu.VMEM((3 * n_col, 64, 128), BF16),
            pltpu.VMEM((3, 64, 128), BF16),
            pltpu.VMEM((slots + 1, 128, 128), F32),
            pltpu.VMEM((2, 3 * n_g, 64, 128), BF16),
            pltpu.VMEM((n_g - 1, 3, 64, 128), BF16),
            pltpu.VMEM((4, 3, 64, 128), BF16),
            pltpu.VMEM((2, width, n_row * node_dev), BF16),
            pltpu.VMEM((2, n_g, piece_rows, 128), BF16),
            pltpu.VMEM((2 * n_g - 1, piece_rows, 128), BF16),
            pltpu.VMEM((n_z, piece_rows, 128), BF16),
            pltpu.VMEM((piece_rows, 128), F32),
            pltpu.SemaphoreType.REGULAR((3,)),
        ] + [dma(n if isinstance(n, tuple) else (n,)) for n in sem_counts],
        compiler_params=pltpu.CompilerParams(
            collective_id=0, has_side_effects=True, vmem_limit_bytes=40 * 1024 * 1024),
    )(
        pin(tile_rows.reshape(1, slots)), pin(tile_cols.reshape(1, slots)), tile_count,
        pin(features.T), pin(weight), pin(tile_values.reshape(slots, 2, 64, 128)), pin(cotangent.reshape(3, 2, 64, out)),
    )
    return act.reshape(node_dev, out), fg.T.reshape(1, node_dev, width), wg


def solution(mesh):
    return jax.shard_map(
        functools.partial(shards, mesh.shape["row"], mesh.shape["col"] // 2),
        mesh=mesh,
        in_specs=(
            P("col", "feat"),
            P("feat", None),
            P("row", "col", None, None, None),
            P("row", "col", None),
            P("row", "col", None),
            P("row", "col"),
            P(("row", "col"), None),
        ),
        out_specs=(P(("row", "col"), None), P("col", "row", "feat"), P("feat", None)),
        check_vma=False,
    )
```

```python
import functools
import math

import jax
import jax.numpy as jnp
from jax import lax
from jax.experimental import pallas as pl
from jax.experimental.pallas import tpu as pltpu
from jax.sharding import PartitionSpec as P

MESH = pl.DeviceIdType.MESH
F32 = jnp.float32
BF16 = jnp.bfloat16


def far_first(n):
    return sorted(range(1, n), key=lambda k: (-min(k, n - k), k))


def kernel(
    n_row, n_z, slots, total_nodes,
    rows_hbm, cols_hbm, count_s, feat_hbm, w_hbm, tiles_hbm, cot_hbm,
    act_out, fg_out, wg_out,
    rows_s, cols_s, keys_v, links_v, links_s,
    x_v, w_ref, tiles_v, cot_v,
    y_send, y_recv, y_buf, prod_f,
    s_buf, yh_recv, t_buf, z_recv, hg_buf, act_v,
    prod_b, b_both, b_recv, b_full,
    xt_both, u_send, u_recv, v_buf, wg_piece,
    here_sem, in_sem, p1_s, p1_r, p2_s, p2_r, p3a_s, p3a_r, p3b_s, p3b_r,
    act_s, act_r, p4z_s, p4z_r, p4y_s, p4y_r, xg_s, xg_r, bc_s, bc_r, p5_s, p5_r, p6_s, p6_r,
    k1_s, k1_r, k2_s, k2_r, k3_s, k3_r,
):
    f = lax.axis_index("feat")
    r = lax.axis_index("row")
    c = lax.axis_index("col")
    y_low, b = f // 2, f % 2
    z, h = c // 2, c % 2
    a = (y_low + h) % 2
    n_g = 2 * n_row

    def feat_of(role, core):
        return ((role + h) % 2) * 2 + core

    def remote(src, dst, send, recv, device):
        return pltpu.make_async_remote_copy(
            src_ref=src, dst_ref=dst, send_sem=send, recv_sem=recv, device_id=device, device_id_type=MESH
        )

    feat_peers = [{"feat": (f + k) % 4} for k in range(1, 4)]

    def g_peer(k):
        g2 = (2 * r + a + k) % n_g
        return g2, {"feat": feat_of(g2 % 2, b), "row": g2 // 2}

    def u_peer(k):
        u2 = (2 * r + h + k) % n_g
        return u2, {"row": u2 // 2, "col": 2 * z + u2 % 2}

    def z_peer(k):
        return {"col": 2 * ((z + k) % n_z) + h}

    y_partner = {"feat": (f + 2) % 4, "col": c + 1 - 2 * h}

    node_dev = x_v.shape[1]
    in_x = pltpu.make_async_copy(
        feat_hbm.at[:, pl.ds(pl.multiple_of(r * node_dev, node_dev), node_dev)], x_v, in_sem.at[0])
    in_w = pltpu.make_async_copy(w_hbm, w_ref, in_sem.at[5])
    in_keys = [
        pltpu.make_async_copy(rows_hbm, keys_v.at[0], in_sem.at[6]),
        pltpu.make_async_copy(cols_hbm, keys_v.at[1], in_sem.at[7]),
        pltpu.make_async_copy(rows_hbm, rows_s, in_sem.at[8]),
        pltpu.make_async_copy(cols_hbm, cols_s, in_sem.at[9]),
    ]
    in_t = pltpu.make_async_copy(tiles_hbm.at[:, a], tiles_v, in_sem.at[1])
    in_c = pltpu.make_async_copy(
        cot_hbm.at[:, a, :, pl.ds(pl.multiple_of(b * 128, 128), 128)], cot_v, in_sem.at[2])
    in_x.start()
    in_w.start()

    barrier = pltpu.get_barrier_semaphore()
    peers = list(feat_peers)
    x_sides = (1, n_row - 1) if n_row > 1 else ()
    for k in x_sides:
        peers.append({"row": (r + k) % n_row})
        peers.append({"feat": (f + 2) % 4, "row": (r + k) % n_row})
    peers += [z_peer(k) for k in (1, n_z - 1)]
    peers.append(y_partner)
    for peer in reversed(peers):
        pl.semaphore_signal(barrier, inc=1, device_id=peer, device_id_type=MESH)
    for cp in in_keys:
        cp.start()
    in_t.start()
    in_c.start()
    in_xt = pltpu.make_async_copy(feat_hbm, xt_both.at[y_low], in_sem.at[11])
    in_xt.start()

    in_x.wait()
    in_w.wait()
    y_part = lax.dot_general(
        x_v[...], w_ref[...], (((0,), (0,)), ((), ())), preferred_element_type=F32).astype(BF16)
    for q in range(2):
        for core in range(2):
            y_send[2 * q + core] = y_part[192 * q:192 * (q + 1), 128 * core:128 * (core + 1)].reshape(3, 64, 128)
    pl.semaphore_wait(barrier, len(peers))
    for k in (1, n_z - 1):
        pl.semaphore_signal(here_sem.at[0], inc=1, device_id=z_peer(k), device_id_type=MESH)
    for k in x_sides:
        pl.semaphore_signal(here_sem.at[2], inc=1, device_id={"row": (r + k) % n_row}, device_id_type=MESH)

    copies = []
    p1 = [[], [], []]
    for w in range(3):
        for k in range(1, 4):
            f2 = (f + k) % 4
            piece = ((f2 // 2 + h) % 2) * 2 + f2 % 2
            cp = remote(y_send.at[piece, w], y_recv.at[k - 1, w], p1_s.at[k - 1, w], p1_r.at[k - 1, w], feat_peers[k - 1])
            cp.start()
            copies.append(cp)
            p1[w].append(cp)
    for cp in in_keys:
        cp.wait()
    ids = lax.broadcasted_iota(jnp.int32, (slots, 128), 0)
    lanes = lax.broadcasted_iota(jnp.int32, (slots, 128), 1)
    live = ids < count_s[0, 0]
    for i in range(2):
        across = jnp.broadcast_to(keys_v[i], (slots, slots))
        across = jnp.concatenate([across, jnp.zeros((slots, 128 - slots), jnp.int32)], axis=1)
        down = jnp.sum(jnp.where(ids == lanes, across, 0), axis=1, keepdims=True)
        down = jnp.broadcast_to(down, (slots, 128))
        before = jnp.where(live & (ids < lanes) & (down == across), ids, -1)
        there = jnp.where(live & (down == lanes), ids, -1)
        for w, found in ((0, before), (1, there)):
            top = jnp.max(found, axis=0, keepdims=True)
            links_v[pl.ds(2 * i + w, 1), :] = jnp.where(top < 0, slots, top)
    links = pltpu.make_async_copy(links_v, links_s, in_sem.at[10])
    links.start()
    pl.semaphore_wait(here_sem.at[0], 2)
    if x_sides:
        pl.semaphore_wait(here_sem.at[2], 2)
    for k in (2, n_z - 2):
        pl.semaphore_signal(here_sem.at[1], inc=1, device_id=z_peer(k), device_id_type=MESH)

    g = 2 * r + a
    p2 = []
    g_order = sorted(range(1, n_g), key=lambda k: -min(k, n_g - k))
    for w in range(3):
        total = y_send[2 * a + b, w].astype(F32)
        for k in range(3):
            p1[w][k].wait_recv()
            total = total + y_recv[k, w].astype(F32)
        y_buf[3 * g + w] = total.astype(BF16)
        mine = y_buf.at[3 * g + w]
        for k in g_order:
            _, dev = g_peer(k)
            cp = remote(mine, mine, p2_s.at[k - 1, w], p2_r.at[0], dev)
            cp.start()
            p2.append(cp)
    prod_f[slots] = jnp.zeros((64, 128), F32)
    prod_b[slots] = jnp.zeros((128, 128), F32)
    in_t.wait()
    links.wait()
    got = y_buf.at[pl.ds(0, 3 * (n_g - 1))]
    remote(got, got, p2_s.at[0, 0], p2_r.at[0], y_partner).wait_recv()

    pl.semaphore_wait(here_sem.at[1], 2)

    xg = remote(feat_hbm, xt_both.at[y_low], xg_s.at[0], xg_r.at[0], {"feat": (f + 2) % 4})
    xg.start()

    def forward(s, _):
        block = y_buf[pl.ds(2 * cols_s[0, s], 2)].reshape(128, 128)
        prod_f[s] = jnp.dot(tiles_v[s], block, preferred_element_type=F32) + prod_f[links_s[0, s]]
        return 0

    lax.fori_loop(0, slots, forward, 0, unroll=32)

    def fill(c2, w):
        s_buf[c2, w] = prod_f[links_s[1, 3 * c2 + w]].astype(BF16)

    sent = []

    def send(src, dst, send_sem, recv_sem, device):
        cp = remote(src, dst, send_sem, recv_sem, device)
        cp.start()
        sent.append(cp)
        return cp

    offs = far_first(n_z) + [0]
    p3a = [[], [], []]
    for w in range(3):
        for j, off in enumerate(offs):
            c2 = 2 * ((z + off) % n_z) + 1 - h
            fill(c2, w)
            p3a[w].append(send(s_buf.at[c2, w], yh_recv.at[j, w], p3a_s.at[j, w], p3a_r.at[j, w], y_partner))
    for w in range(3):
        for off in offs:
            fill(2 * ((z + off) % n_z) + h, w)
    p3b = [[], [], []]
    own_part = [None] * 3

    def sum_h(w):
        for j, off in enumerate(offs):
            c2 = 2 * ((z + off) % n_z) + h
            p3a[w][j].wait_recv()
            both = s_buf[c2, w].astype(F32) + yh_recv[j, w].astype(F32)
            if off:
                t_buf[j, w] = both.astype(BF16)
                p3b[w].append(send(t_buf.at[j, w], z_recv.at[j, w], p3b_s.at[j, w], p3b_r.at[w], z_peer(off)))
            else:
                own_part[w] = both

    def place(dist, w):
        return hg_buf.at[3 * (2 * ((z + 2 * n_z - dist) % n_z) + h) + w]

    def z_send(what, j, off, w):
        send(what, what, p4z_s.at[j, w], p4z_r.at[j, w], z_peer(off))

    def y_send_on(what, j, w):
        send(what, what, p4y_s.at[j, w], p4y_r.at[0], y_partner)

    def arrived(j, dist, w):
        got = place(dist, w)
        remote(got, got, p4z_s.at[j, w], p4z_r.at[j, w], y_partner).wait_recv()
        return got

    def activate(w):
        hidden = own_part[w]
        got = z_recv.at[pl.ds(0, n_z - 1), w]
        remote(got, got, p3b_s.at[0, w], p3b_r.at[w], y_partner).wait_recv()
        for j in range(n_z - 1):
            hidden = hidden + z_recv[j, w].astype(F32)
        sigma = jax.nn.sigmoid(hidden)
        grad = cot_v[w].astype(F32) * (sigma * (1.0 + hidden * (1.0 - sigma)))
        hg_buf[3 * c + w] = grad.astype(BF16)
        act_v[w] = (hidden * sigma).astype(BF16)
        own = hg_buf.at[3 * c + w]
        if w == 2:
            z_send(own, 6, 4, w)
            z_send(own, 4, 3, w)
            z_send(own, 5, n_z - 3, w)
        z_send(own, 2, 2, w)
        z_send(own, 3, n_z - 2, w)
        z_send(own, 0, 1, w)
        z_send(own, 1, n_z - 1, w)
        y_send_on(own, n_z - 1, w)

    side = 1 - 2 * (z % 2)

    def pass_on(w):
        if w < 2:
            plus = arrived(2, 2, w)
            z_send(plus, 4, 1, w)
            minus = arrived(3, n_z - 2, w)
            z_send(minus, 5, n_z - 1, w)
            z_send(place(2 * side + n_z, w), 6, 2 * side + n_z, w)
        y_send_on(arrived(0, 1, w), 0, w)
        y_send_on(arrived(1, n_z - 1, w), 1, w)
        if w == 2:
            plus = arrived(2, 2, w)
            minus = arrived(3, n_z - 2, w)
        y_send_on(plus, 2, w)
        y_send_on(minus, 3, w)

    def last_on(w):
        y_send_on(arrived(4, 3, w), 4, w)
        y_send_on(arrived(5, n_z - 3, w), 5, w)
        y_send_on(arrived(6, 4, w), 6, w)

    in_c.wait()
    sum_h(0)
    sum_h(1)
    activate(0)
    sum_h(2)
    activate(1)
    pass_on(0)
    activate(2)
    act_cols = pl.ds(pl.multiple_of(b * 128, 128), 128)
    act_dst = act_out.at[:, a, :, act_cols]
    local = pltpu.make_async_copy(act_v, act_dst, in_sem.at[3])
    local.start()
    pass_on(1)
    last_on(0)
    pass_on(2)
    last_on(1)
    last_on(2)
    acts = []
    for k in range(1, 4):
        cp = remote(act_v, act_dst, act_s.at[k - 1], act_r.at[k - 1], feat_peers[k - 1])
        cp.start()
        acts.append(cp)
    got = hg_buf.at[pl.ds(0, 3 * n_z)]
    remote(got, got, p4y_s.at[0, 0], p4y_r.at[0], y_partner).wait_recv()

    def backward(s, _):
        prod_b[s] = lax.dot_general(
            tiles_v[s], hg_buf[rows_s[0, s]], (((0,), (0,)), ((), ())), preferred_element_type=F32) + prod_b[links_s[2, s]]
        return 0

    lax.fori_loop(0, slots, backward, 0, unroll=32)

    bc = []
    for i in range(2):
        for j in range(3 * n_row * i // 2, 3 * n_row * (i + 1) // 2):
            b_both[b, pl.ds(2 * j, 2)] = prod_b[links_s[3, j]].astype(BF16).reshape(2, 64, 128)
        half = b_both.at[b, pl.ds(3 * n_row * i, 3 * n_row)]
        cp = remote(half, half, bc_s.at[i], bc_r.at[0], {"feat": f + 1 - 2 * b})
        cp.start()
        bc.append(cp)

    piece_rows = u_send.shape[2]
    in_xt.wait()
    xg.wait_recv()
    got = b_both.at[1 - b]
    remote(got, got, bc_s.at[0], bc_r.at[0], y_partner).wait_recv()
    both = jnp.concatenate([b_both[0].reshape(n_row * node_dev, 128), b_both[1].reshape(n_row * node_dev, 128)], axis=1)
    for low in range(2):
        part = jnp.dot(xt_both[low], both, preferred_element_type=F32).astype(BF16)
        for core in range(2):
            u_send[low, n_row * core:n_row * (core + 1)] = part[:, 128 * core:128 * (core + 1)].reshape(
                n_row, piece_rows, 128)
    u = 2 * r + h
    k1 = []
    for k in range(1, 2 * n_g):
        q2 = (n_g * y_low + u + k) % (2 * n_g)
        low2, u2 = q2 // n_g, q2 % n_g
        dev = {"feat": 2 * low2 + b, "row": u2 // 2, "col": 2 * z + u2 % 2}
        cp = remote(u_send.at[low2, u2], u_recv.at[k - 1], k1_s.at[k - 1], k1_r.at[0], dev)
        cp.start()
        k1.append(cp)

    p5 = []
    for k in range(1, n_g):
        g2, dev = g_peer(k)
        cp = remote(b_both.at[b, pl.ds(3 * g2, 3)], b_recv.at[k - 1], p5_s.at[k - 1], p5_r.at[0], dev)
        cp.start()
        p5.append(cp)

    total = u_send[y_low, u].astype(F32)
    remote(u_recv, u_recv, k1_s.at[0], k1_r.at[0], y_partner).wait_recv()
    for k in range(2 * n_g - 1):
        total = total + u_recv[k].astype(F32)
    v_buf[z] = total.astype(BF16)
    k2 = []
    for j, off in enumerate(offs[:-1]):
        cp = remote(v_buf.at[z], v_buf.at[z], k2_s.at[j], k2_r.at[0], z_peer(off))
        cp.start()
        k2.append(cp)
    for cp in copies + p2 + sent + acts + p5 + k1 + bc + [xg]:
        cp.wait_send()

    total = b_both[b, pl.ds(3 * g, 3)].astype(F32)
    remote(b_recv, b_recv, p5_s.at[0], p5_r.at[0], y_partner).wait_recv()
    for k in range(n_g - 1):
        total = total + b_recv[k].astype(F32)
    b_full[2 * b + a] = total.astype(BF16)
    mine = b_full.at[2 * b + a]
    p6 = []
    for k in range(1, 4):
        cp = remote(mine, mine, p6_s.at[k - 1], p6_r.at[k - 1], feat_peers[k - 1])
        cp.start()
        p6.append(cp)

    got = v_buf.at[pl.ds(0, n_z - 1)]
    remote(got, got, k2_s.at[0], k2_r.at[0], y_partner).wait_recv()
    total = v_buf[0].astype(F32)
    for j in range(1, n_z):
        total = total + v_buf[j].astype(F32)
    wg_piece[...] = total * (1.0 / math.sqrt(total_nodes))

    def wg_place(piece):
        return wg_out.at[
            pl.ds(pl.multiple_of((piece % n_row) * piece_rows, piece_rows), piece_rows),
            pl.ds(pl.multiple_of((piece // n_row) * 128, 128), 128),
        ]

    local_wg = pltpu.make_async_copy(wg_piece, wg_place(u), in_sem.at[4])
    local_wg.start()
    k3 = []
    for k in range(1, n_g):
        _, dev = u_peer(k)
        cp = remote(wg_piece, wg_place(u), k3_s.at[k - 1], k3_r.at[k - 1], dev)
        cp.start()
        k3.append(cp)
    for k in range(1, 4):
        f2 = (f + 4 - k) % 4
        got = b_full.at[2 * (f2 % 2) + (f2 // 2 + h) % 2]
        remote(got, got, p6_s.at[k - 1], p6_r.at[k - 1], y_partner).wait_recv()
    grad_t = jnp.zeros((w_ref.shape[0], node_dev), F32)
    for core in range(2):
        grad_t = grad_t + lax.dot_general(
            w_ref[:, 128 * core:128 * (core + 1)], b_full[2 * core:2 * core + 2].reshape(node_dev, 128),
            (((1,), (1,)), ((), ())), preferred_element_type=F32)
    fg_out[...] = grad_t.astype(BF16)

    for k in range(1, n_g):
        got = wg_place((u + n_g - k) % n_g)
        remote(wg_piece, got, k3_s.at[k - 1], k3_r.at[k - 1], y_partner).wait_recv()
    for k in range(1, 4):
        f2 = (f + 4 - k) % 4
        got = act_out.at[:, (f2 // 2 + h) % 2, :, pl.ds(pl.multiple_of((f2 % 2) * 128, 128), 128)]
        remote(act_v, got, act_s.at[k - 1], act_r.at[k - 1], y_partner).wait_recv()
    local.wait()
    local_wg.wait()
    for cp in p6 + k2 + k3:
        cp.wait_send()


def shards(n_row, n_z, features, weight, tile_values, tile_rows, tile_cols, tile_count, cotangent):
    slots = tile_values.shape[2]
    node_dev, out = cotangent.shape
    width = features.shape[1]
    n_g = 2 * n_row
    n_col = 2 * n_z
    piece_rows = 2 * width // n_g
    dma = pltpu.SemaphoreType.DMA
    pin = lambda x: pltpu.with_memory_space_constraint(x, pltpu.HBM)
    smem = pl.BlockSpec(memory_space=pltpu.SMEM)
    vmem = pl.BlockSpec(memory_space=pltpu.VMEM)
    hbm = pl.BlockSpec(memory_space=pltpu.HBM)
    sem_counts = [12, (3, 3), (3, 3), (n_g - 1, 3), 1, (n_z, 3), (n_z, 3), (n_z - 1, 3), 3,
                  3, 3, (n_z - 1, 3), (n_z - 1, 3), (n_z, 3), 1,
                  1, 1, 2, 1, n_g - 1, 1, 3, 3, 2 * n_g - 1, 1, n_z - 1, 1, n_g - 1, n_g - 1]
    act, fg, wg = pl.pallas_call(
        functools.partial(kernel, n_row, n_z, slots, node_dev * n_row * n_col),
        out_shape=[
            jax.ShapeDtypeStruct((3, 2, 64, out), BF16),
            jax.ShapeDtypeStruct((width, node_dev), BF16),
            jax.ShapeDtypeStruct((width, out), F32),
        ],
        in_specs=[hbm, hbm, smem, hbm, hbm, hbm, hbm],
        out_specs=[vmem] * 3,
        scratch_shapes=[
            pltpu.SMEM((1, slots), jnp.int32),
            pltpu.SMEM((1, slots), jnp.int32),
            pltpu.VMEM((2, 1, slots), jnp.int32),
            pltpu.VMEM((8, 128), jnp.int32),
            pltpu.SMEM((8, 128), jnp.int32),
            pltpu.VMEM((width, node_dev), BF16),
            pltpu.VMEM((width, out), BF16),
            pltpu.VMEM((slots, 64, 128), BF16),
            pltpu.VMEM((3, 64, 128), BF16),
            pltpu.VMEM((4, 3, 64, 128), BF16),
            pltpu.VMEM((3, 3, 64, 128), BF16),
            pltpu.VMEM((3 * n_g, 64, 128), BF16),
            pltpu.VMEM((slots + 1, 64, 128), F32),
            pltpu.VMEM((n_col, 3, 64, 128), BF16),
            pltpu.VMEM((n_z, 3, 64, 128), BF16),
            pltpu.VMEM((n_z - 1, 3, 64, 128), BF16),
            pltpu.VMEM((n_z - 1, 3, 64, 128), BF16),
            pltpu.VMEM((3 * n_col, 64, 128), BF16),
            pltpu.VMEM((3, 64, 128), BF16),
            pltpu.VMEM((slots + 1, 128, 128), F32),
            pltpu.VMEM((2, 3 * n_g, 64, 128), BF16),
            pltpu.VMEM((n_g - 1, 3, 64, 128), BF16),
            pltpu.VMEM((4, 3, 64, 128), BF16),
            pltpu.VMEM((2, width, n_row * node_dev), BF16),
            pltpu.VMEM((2, n_g, piece_rows, 128), BF16),
            pltpu.VMEM((2 * n_g - 1, piece_rows, 128), BF16),
            pltpu.VMEM((n_z, piece_rows, 128), BF16),
            pltpu.VMEM((piece_rows, 128), F32),
            pltpu.SemaphoreType.REGULAR((3,)),
        ] + [dma(n if isinstance(n, tuple) else (n,)) for n in sem_counts],
        compiler_params=pltpu.CompilerParams(
            collective_id=0, has_side_effects=True, vmem_limit_bytes=40 * 1024 * 1024),
    )(
        pin(tile_rows.reshape(1, slots)), pin(tile_cols.reshape(1, slots)), tile_count,
        pin(features.T), pin(weight), pin(tile_values.reshape(slots, 2, 64, 128)), pin(cotangent.reshape(3, 2, 64, out)),
    )
    return act.reshape(node_dev, out), fg.T.reshape(1, node_dev, width), wg


def solution(mesh):
    return jax.shard_map(
        functools.partial(shards, mesh.shape["row"], mesh.shape["col"] // 2),
        mesh=mesh,
        in_specs=(
            P("col", "feat"),
            P("feat", None),
            P("row", "col", None, None, None),
            P("row", "col", None),
            P("row", "col", None),
            P("row", "col"),
            P(("row", "col"), None),
        ),
        out_specs=(P(("row", "col"), None), P("col", "row", "feat"), P("feat", None)),
        check_vma=False,
    )
```
